128 devices in a mesh: gx: 16 (over x, y), gy: 8 (over z, core).
Axes of the slice: x: 4, y: 4, z: 4, core: 2. Of those that a mesh axis runs over, the one named last changes fastest.
Arguments:
- features: bfloat16 [32, 4194304], P(None, ('gx', 'gy')), may hold values from -6 to 6
- weights: bfloat16 [4194304, 128], P(('gx', 'gy')), as said below
- owners: int32 [32768], P(('gx', 'gy')), may hold values from 0 to 127, as said below
- tile_ids: int32 [32768], P(('gx', 'gy')), may hold values from 0 to 127, as said below
- counts: int32 [128], P(('gx', 'gy')), may hold values from 128 to 256, as said below
- conv_first: bfloat16 [27, 32, 32], replicated, may hold values from -0.21875 to 0.21875
- bias_first: float32 [32], replicated, may hold values from -3 to 3
- conv_second: bfloat16 [27, 32, 32], replicated, may hold values from -0.21875 to 0.21875
- bias_second: float32 [32], replicated, may hold values from -3 to 3
- head: bfloat16 [3, 32], replicated, may hold values from -1 to 1
Outputs:
- grid_out: bfloat16 [32, 16, 128, 1024], P(None, None, 'gx', 'gy')
- velocity: float32 [3, 4194304], P(None, ('gx', 'gy'))
The draws below stay inside these ranges and needn't reach their ends.
Inputs may be any that keep to these rules, and one draw needn't show every extreme that they name: `owners`: the first 128 slots of each device name the device itself. Later slots that are live name a device whose brick is one step away along gx, along gy or both (no wrap, never the device itself); later slots that are not live name the device itself. Among its later live slots one device names any one owner at most 16 times; some device names every one of its neighbours exactly 16 times, and some device is named exactly 16 times by each of its neighbours other than device 0. `tile_ids`: on each device the first 128 slots name every tile of its brick once; later slots name any tile. `counts`: number of live blocks of each device, which stand first among its slots. Each row holds a particle's quadratic B-spline weights on its block's tile, cell index (z 4 + x) 8 + y; its 27 nonzero weights lie inside the tile and sum to one.
All inputs are finite; a program needn't handle non-finite values.
Results may differ from the reference program's by a relative error of at most 0.0051.
Values may be sent and summed in bfloat16 or wider, within the bound.
No kernel may reach another device: no remote copies, remote signals or barrier semaphores. Data moves between devices by JAX's collectives and lax.ppermute only.
A program may use at most 384 MiB of HBM per device.

```python
import jax
import jax.numpy as jnp
from jax import lax

C = 32
TILE = 128
PB = 128
SLAB = 16
BX = 8
BY = 128
NEIGHBOUR_LIMIT = 16
TILES_DEV = 128
BLOCKS = 32768
PARTICLES = 4194304
NX = 128
NY = 1024
N_GX = 16
N_GY = 8


def block_plan(key):
    devices = N_GX * N_GY
    device = jnp.arange(devices, dtype=jnp.int32)
    dev_x = device // N_GY
    dev_y = device % N_GY
    key_amount, key_row, key_col, key_order, key_recv_x, key_recv_y = jax.random.split(key, 6)
    amount = jax.random.randint(key_amount, (devices, 9), 0, NEIGHBOUR_LIMIT + 1)
    offset = jnp.arange(9, dtype=jnp.int32)
    step_x = offset // 3 - 1
    step_y = offset % 3 - 1
    target_x = dev_x[:, None] + step_x[None, :]
    target_y = dev_y[:, None] + step_y[None, :]
    inside = (target_x >= 0) & (target_x < N_GX) & (target_y >= 0) & (target_y < N_GY)
    target_id = target_x * N_GY + target_y
    full_dev = (1 + jax.random.randint(key_row, (), 0, N_GX - 2)) * N_GY + 1 + jax.random.randint(key_col, (), 0, N_GY - 2)
    recv_dev = (1 + jax.random.randint(key_recv_x, (), 0, N_GX - 2)) * N_GY + 1 + jax.random.randint(key_recv_y, (), 0, N_GY - 2)
    amount = jnp.where(device[:, None] == full_dev, NEIGHBOUR_LIMIT, amount)
    amount = jnp.where(target_id == recv_dev, NEIGHBOUR_LIMIT, amount)
    amount = jnp.where(device[:, None] == 0, 0, amount)
    amount = jnp.where(offset[None, :] == 4, 0, amount)
    amount = jnp.where(inside, amount, 0)
    slots = jnp.arange(9 * NEIGHBOUR_LIMIT, dtype=jnp.int32)
    kind = slots // NEIGHBOUR_LIMIT
    rank = slots % NEIGHBOUR_LIMIT
    valid = rank[None, :] < amount[:, kind]
    target = target_id[:, kind]
    target = jnp.where(valid, target, device[:, None])
    orders = jax.vmap(lambda k: jax.random.permutation(k, 9 * NEIGHBOUR_LIMIT))(jax.random.split(key_order, devices))
    score = orders + jnp.where(valid, 0, 9 * NEIGHBOUR_LIMIT)
    order = jnp.argsort(score, axis=1)
    routed = jnp.take_along_axis(target, order, axis=1)[:, :8 * NEIGHBOUR_LIMIT]
    own = jnp.broadcast_to(device[:, None], (devices, TILES_DEV))
    owners = jnp.concatenate([own, routed], axis=1).reshape(-1).astype(jnp.int32)
    return (owners, (TILES_DEV + jnp.sum(amount, axis=1)).astype(jnp.int32))


def draw_owners(key, part):
    owners, totals = block_plan(key)
    return owners


def draw_counts(key, part):
    owners, totals = block_plan(key)
    return totals


def draw_tile_ids(key, part):
    key = jax.random.fold_in(key, 7)
    devices = N_GX * N_GY
    key_perm, key_rest = jax.random.split(key, 2)
    own = jax.vmap(lambda k: jax.random.permutation(k, TILES_DEV))(jax.random.split(key_perm, devices))
    rest = jax.random.randint(key_rest, (devices, 8 * NEIGHBOUR_LIMIT), 0, TILES_DEV)
    return jnp.concatenate([own, rest], axis=1).reshape(-1).astype(jnp.int32)


def spline_rows(base, frac, size):
    cell = jnp.arange(size, dtype=jnp.float32)
    slot_position = base.astype(jnp.float32) - 0.5 + frac
    dist = jnp.abs(cell[None, :] - slot_position[:, None])
    near = 0.75 - dist * dist
    far = 0.5 * (1.5 - dist) ** 2
    return jnp.where(dist < 0.5, near, jnp.where(dist < 1.5, far, 0.0))


def draw_weights(key, part):
    key = jax.random.fold_in(key, 11)
    count = BLOCKS * PB
    keys = jax.random.split(key, 6)
    base_z = jax.random.randint(keys[0], (count,), 1, 3)
    base_x = jax.random.randint(keys[1], (count,), 1, 3)
    base_y = jax.random.randint(keys[2], (count,), 1, 7)
    frac_z = jax.random.uniform(keys[3], (count,), jnp.float32)
    frac_x = jax.random.uniform(keys[4], (count,), jnp.float32)
    frac_y = jax.random.uniform(keys[5], (count,), jnp.float32)
    along_z = spline_rows(base_z, frac_z, 4)
    along_x = spline_rows(base_x, frac_x, 4)
    along_y = spline_rows(base_y, frac_y, 8)
    table = along_z[:, :, None, None] * along_x[:, None, :, None] * along_y[:, None, None, :]
    return table.reshape(count, 128).astype(jnp.bfloat16)


def level_of(key, extent, pieces, smallest, high):
    def one(position, blocks):
        draws = jax.random.uniform(jax.random.fold_in(jax.random.fold_in(key, 6), position), (blocks,), jnp.float32, smallest / len(pieces), high / len(pieces))
        return jnp.repeat(jnp.exp(draws), extent[position] // blocks).reshape((-1,) + (1,) * (len(extent) - position - 1))

    loudness = one(*pieces[0])
    for cut in pieces[1:]:
        loudness = loudness * one(*cut)
    return loudness


def normal_values(key, extent, scale, bound, cuts=(), kind=jnp.bfloat16):
    entries = jax.random.normal(key, extent, jnp.float32) * scale
    if len(cuts) > 0:
        entries = level_of(key, extent, cuts, -0.22, 0.18) * entries
    return jnp.clip(entries, min=-bound, max=bound).astype(kind)


def setup_inputs(seed: int = 0) -> dict:
    key_of = jax.random.split(jax.random.key(seed), 11)
    features = normal_values(key_of[0], (C, PARTICLES), 1.0, 6.0, ((1, 128),))
    weights = draw_weights(jax.random.fold_in(key_of[10], 71), 0)
    owners = draw_owners(jax.random.fold_in(key_of[10], 71), 0)
    tile_ids = draw_tile_ids(jax.random.fold_in(key_of[10], 71), 0)
    counts = draw_counts(jax.random.fold_in(key_of[10], 71), 0)
    conv_first = normal_values(key_of[5], (27, C, C), (27 * C) ** -0.5, 0.21875)
    bias_first = normal_values(key_of[6], (C,), 0.5, 3.0, (), jnp.float32)
    conv_second = normal_values(key_of[7], (27, C, C), (27 * C) ** -0.5, 0.21875)
    bias_second = normal_values(key_of[8], (C,), 0.5, 3.0, (), jnp.float32)
    head = normal_values(key_of[9], (3, C), C ** -0.5, 1.0)
    return dict(features=features, weights=weights, owners=owners, tile_ids=tile_ids, counts=counts, conv_first=conv_first, bias_first=bias_first, conv_second=conv_second, bias_second=bias_second, head=head)


def convolve(field, kernel):
    taps = kernel.astype(jnp.float32).reshape(3, 3, 3, C, C).transpose(3, 4, 0, 1, 2)
    out = lax.conv_general_dilated(field[None], taps, (1, 1, 1), "SAME",
                                   dimension_numbers=("NCDHW", "OIDHW", "NCDHW"),
                                   precision=lax.Precision.HIGHEST)
    return out[0]


def reference(features, weights, owners, tile_ids, counts, conv_first, bias_first, conv_second, bias_second, head):
    devices = N_GX * N_GY
    blk = BLOCKS // devices
    feats = features.astype(jnp.float32).reshape(C, BLOCKS, PB)
    wts = weights.astype(jnp.float32).reshape(BLOCKS, PB, TILE)
    tiles = jnp.einsum("cbp,bpk->bck", feats, wts, precision=lax.Precision.HIGHEST)
    local = jnp.arange(BLOCKS, dtype=jnp.int32) % blk
    live = local < jnp.repeat(counts, blk)
    tiles = jnp.where(live[:, None, None], tiles, 0.0).astype(jnp.bfloat16)
    owner_x = owners // N_GY
    owner_y = owners % N_GY
    per_y = BY // 8
    per_x = BX // 4
    tile_z = tile_ids // (per_x * per_y)
    rest = tile_ids % (per_x * per_y)
    tile_x = rest // per_y
    tile_y = rest % per_y
    global_tile = ((tile_z * (NX // 4) + owner_x * per_x + tile_x) * (NY // 8) + owner_y * per_y + tile_y).astype(jnp.int32)
    total_tiles = (SLAB // 4) * (NX // 4) * (NY // 8)
    summed = jax.ops.segment_sum(tiles.astype(jnp.float32).reshape(BLOCKS, C * TILE), global_tile, total_tiles)
    grid0 = summed.reshape(SLAB // 4, NX // 4, NY // 8, C, 4, 4, 8).transpose(3, 0, 4, 1, 5, 2, 6)
    grid0 = grid0.reshape(C, SLAB, NX, NY).astype(jnp.bfloat16)
    pre = convolve(grid0.astype(jnp.float32), conv_first) + bias_first[:, None, None, None]
    hidden = jax.nn.gelu(pre).astype(jnp.bfloat16)
    second = convolve(hidden.astype(jnp.float32), conv_second) + bias_second[:, None, None, None]
    grid_out = (grid0.astype(jnp.float32) + second).astype(jnp.bfloat16)
    grid_vel = jnp.einsum("oc,czxy->ozxy", head.astype(jnp.float32), grid_out.astype(jnp.float32),
                          precision=lax.Precision.HIGHEST)
    tiled = grid_vel.reshape(3, SLAB // 4, 4, NX // 4, 4, NY // 8, 8).transpose(1, 3, 5, 0, 2, 4, 6)
    tiled = tiled.reshape(total_tiles, 3, TILE)
    picked = jnp.take(tiled, global_tile, axis=0)
    velocity = jnp.einsum("bok,bpk->obp", picked, wts, precision=lax.Precision.HIGHEST)
    velocity = jnp.where(live[None, :, None], velocity, 0.0).reshape(3, BLOCKS * PB)
    return grid_out, velocity
```

```python
import jax
import jax.numpy as jnp
import numpy as np
from jax import lax
from jax.experimental import pallas as pl
from jax.experimental.pallas import tpu as pltpu
from jax.sharding import PartitionSpec as P

C = 32
SLAB = 16
BY = 128
SLOTS = 16
PAY = SLOTS * 32 + 16
ROWS = 144
STEP = 16
STEPS = 8
MIB = 1 << 20
F32 = jnp.float32
BF16 = jnp.bfloat16
VMEM = pltpu.VMEM
SMEM = pltpu.SMEM


def lanes_of(shape):
    return lax.broadcasted_iota(jnp.int32, shape, len(shape) - 1)


def params(limit, grid=False):
    if grid:
        return pltpu.CompilerParams(
            dimension_semantics=("arbitrary",), vmem_limit_bytes=limit * MIB
        )
    return pltpu.CompilerParams(vmem_limit_bytes=limit * MIB)


def cost(flops, nbytes):
    return pl.CostEstimate(flops=flops, bytes_accessed=nbytes, transcendentals=0)


def splat_four(f_ref, w_ref, first):
    parts = []
    for j in range(4):
        at = (first + j) * 128
        parts.append(
            jnp.dot(f_ref[:, at : at + 128], w_ref[at : at + 128, :], preferred_element_type=F32)
        )
    a = jnp.concatenate(parts, 0).astype(BF16).astype(F32)
    a = a.T.reshape(4, 2, 2, 8, 128)
    lane = lanes_of((4, 2, 8, 128))
    v0, v1 = a[:, 0], a[:, 1]
    n0 = jnp.where(lane < 64, v0, pltpu.roll(v1, 64, 3))
    n1 = jnp.where(lane < 64, pltpu.roll(v0, 64, 3), v1)
    lane = lanes_of((4, 8, 128))
    tiles = []
    for n in (n0, n1):
        v0, v1 = n[:, 0], n[:, 1]
        tiles.append(jnp.where(lane % 64 < 32, v0, pltpu.roll(v1, 32, 2)))
        tiles.append(jnp.where(lane % 64 < 32, pltpu.roll(v0, 96, 2), v1))
    return tiles


def far_splat_kernel(owners, ids, counts, f_ref, w_ref, lo, mid, hi, slots, tiles, idrows, filled):
    step = pl.program_id(0)
    ix = lax.axis_index("gx")
    iy = lax.axis_index("gy")

    @pl.when(step == 0)
    def _():
        tiles[...] = jnp.zeros_like(tiles)
        idrows[...] = jnp.zeros_like(idrows)
        for k in range(9):
            filled[k] = 0

    lane = lanes_of((1, 128))
    count = counts[0]
    for group in range(STEP // 4):
        got = splat_four(f_ref, w_ref, group * 4)
        for j in range(4):
            block = step * STEP + group * 4 + j
            owner = owners[128 + block]
            live = 128 + block < count
            target = ((owner >> 3) - ix + 1) * 3 + (owner & 7) - iy + 1
            target = jnp.where(live, target, 4)
            rank = filled[target]
            filled[target] = jnp.where(live, rank + 1, 0)
            slot = target * SLOTS + rank
            slots[block] = slot
            tiles[slot] = got[j].reshape(32, 128).astype(BF16)
            row = idrows[pl.ds(target, 1), :]
            idrows[pl.ds(target, 1), :] = jnp.where(
                lane == rank, ids[128 + block].astype(F32), row
            )

    @pl.when(step == STEPS - 1)
    def _():
        for dx, out in enumerate((lo, mid, hi)):
            for dy in range(3):
                k = dx * 3 + dy
                out[dy, 0 : SLOTS * 32, :] = tiles[k * SLOTS : (k + 1) * SLOTS].reshape(
                    SLOTS * 32, 128
                )
                out[dy, SLOTS * 32 : PAY, :] = jnp.broadcast_to(
                    idrows[k : k + 1, :], (16, 128)
                ).astype(BF16)


def far_splat(features, weights, owners, ids, counts):
    pay = jax.ShapeDtypeStruct((3, PAY, 128), BF16)
    whole = pl.BlockSpec((3, PAY, 128), lambda i: (0, 0, 0))
    smem = pl.BlockSpec(memory_space=SMEM)
    return pl.pallas_call(
        far_splat_kernel,
        grid=(STEPS,),
        in_specs=[
            smem,
            smem,
            smem,
            pl.BlockSpec((C, STEP * 128), lambda i: (0, STEPS + i)),
            pl.BlockSpec((STEP * 128, 128), lambda i: (STEPS + i, 0)),
        ],
        out_specs=[whole, whole, whole, smem],
        out_shape=[pay, pay, pay, jax.ShapeDtypeStruct((128,), jnp.int32)],
        scratch_shapes=[
            VMEM((9 * SLOTS, 32, 128), BF16),
            VMEM((16, 128), F32),
            SMEM((9,), jnp.int32),
        ],
        compiler_params=params(16, True),
        cost_estimate=cost(2 * 128 * 32 * 128 * 128, 6 * MIB),
        name="far_splat",
    )(owners, ids, counts, features, weights)


def tile_place(tile):
    return (tile >> 5) * 4, (tile >> 4) & 1, pl.multiple_of((tile & 15) * 8, 8)


def own_splat_kernel(ids, f_ref, w_ref, out, grid):
    step = pl.program_id(0)
    for group in range(STEP // 4):
        got = splat_four(f_ref, w_ref, group * 4)
        for j in range(4):
            z, tx, y = tile_place(ids[step * STEP + group * 4 + j])
            grid[tx, pl.ds(z, 4), pl.ds(y, 8), :] = got[j]

    @pl.when(step == STEPS - 1)
    def _():
        out[...] = grid[...].astype(BF16)


def own_splat(features, weights, ids):
    return pl.pallas_call(
        own_splat_kernel,
        grid=(STEPS,),
        in_specs=[
            pl.BlockSpec(memory_space=SMEM),
            pl.BlockSpec((C, STEP * 128), lambda i: (0, i)),
            pl.BlockSpec((STEP * 128, 128), lambda i: (i, 0)),
        ],
        out_specs=pl.BlockSpec((2, SLAB, BY, 128), lambda i: (0, 0, 0, 0)),
        out_shape=jax.ShapeDtypeStruct((2, SLAB, BY, 128), BF16),
        scratch_shapes=[VMEM((2, SLAB, BY, 128), F32)],
        compiler_params=params(16, True),
        cost_estimate=cost(2 * 128 * 32 * 128 * 128, 6 * MIB),
        name="own_splat",
    )(ids, features, weights)


def sum_kernel(own, from_ylo, from_yhi, from_xlo, from_xhi, g, ylo, yhi, ids, grid, idv, sem):
    groups = [(from_ylo, 0), (from_ylo, 1), (from_ylo, 2)]
    groups += [(from_yhi, 0), (from_yhi, 1), (from_yhi, 2)]
    groups += [(from_xlo, 1), (from_xhi, 1)]
    rows = [ref[k, SLOTS * 32 : PAY, :].astype(F32)[0:1] for ref, k in groups]
    idv[...] = jnp.concatenate(rows, 0).astype(jnp.int32)
    copy = pltpu.make_async_copy(idv, ids, sem)
    copy.start()
    grid[...] = own[...].astype(F32)
    copy.wait()
    for n, (ref, k) in enumerate(groups):

        def add(j, carry, n=n, ref=ref, k=k):
            z, tx, y = tile_place(ids[n, j])
            tile = ref[k, pl.ds(pl.multiple_of(j * 32, 32), 32), :].astype(F32).reshape(4, 8, 128)
            grid[tx, pl.ds(z, 4), pl.ds(y, 8), :] += tile
            return carry

        lax.fori_loop(0, SLOTS, add, 0, unroll=4)
    g[...] = grid[...].astype(BF16)
    for tx in range(2):
        for r in range(2):
            ylo[tx * 2 + r] = grid[tx, :, r, :].astype(BF16)
            yhi[tx * 2 + r] = grid[tx, :, BY - 2 + r, :].astype(BF16)


def sum_tiles(own, from_ylo, from_yhi, from_xlo, from_xhi):
    vm = pl.BlockSpec(memory_space=VMEM)
    edge = jax.ShapeDtypeStruct((4, SLAB, 128), BF16)
    return pl.pallas_call(
        sum_kernel,
        in_specs=[vm] * 5,
        out_specs=[vm, vm, vm, pl.BlockSpec(memory_space=SMEM)],
        out_shape=[
            jax.ShapeDtypeStruct((2, SLAB, BY, 128), BF16),
            edge,
            edge,
            jax.ShapeDtypeStruct((8, 128), jnp.int32),
        ],
        scratch_shapes=[
            VMEM((2, SLAB, BY, 128), F32),
            VMEM((8, 128), jnp.int32),
            pltpu.SemaphoreType.DMA,
        ],
        compiler_params=params(16),
        cost_estimate=cost(1000, 4 * MIB),
        name="sum_tiles",
    )(own, from_ylo, from_yhi, from_xlo, from_xhi)


def widen_kernel(g, rlo, rhi, x, slo, shi, edge):
    edge[...] = jnp.zeros_like(edge)
    for tx in range(2):
        for r in range(2):
            edge[tx, 0, :, 6 + r, :] = rlo[tx * 2 + r].astype(F32)
            edge[tx, 1, :, r, :] = rhi[tx * 2 + r].astype(F32)
    lane = lanes_of((ROWS, 128))

    def plane(tx, z):
        return jnp.concatenate([edge[tx, 0, z], g[tx, z].astype(F32), edge[tx, 1, z]], 0)

    def pair(z, carry):
        a, b = plane(0, z), plane(0, z + 8)
        x[0, z] = a.astype(BF16)
        x[0, z + 8] = b.astype(BF16)
        slo[z] = jnp.where(lane < 64, a, pltpu.roll(b, 64, 1)).astype(BF16)
        a, b = plane(1, z), plane(1, z + 8)
        x[1, z] = a.astype(BF16)
        x[1, z + 8] = b.astype(BF16)
        shi[z] = jnp.where(lane < 64, pltpu.roll(a, 64, 1), b).astype(BF16)
        return carry

    lax.fori_loop(0, 8, pair, 0)


def widen_y(g, rlo, rhi):
    vm = pl.BlockSpec(memory_space=VMEM)
    side = jax.ShapeDtypeStruct((SLAB // 2, ROWS, 128), BF16)
    return pl.pallas_call(
        widen_kernel,
        in_specs=[vm] * 3,
        out_specs=[vm] * 3,
        out_shape=[jax.ShapeDtypeStruct((2, SLAB, ROWS, 128), BF16), side, side],
        scratch_shapes=[VMEM((2, 2, SLAB, 8, 128), F32)],
        compiler_params=params(8),
        cost_estimate=cost(1000, 3 * MIB),
        name="widen_y",
    )(g, rlo, rhi)


def rows_inside(shape, iy):
    row = lax.broadcasted_iota(jnp.int32, shape, 1)
    return ((row != 7) | (iy > 0)) & ((row != 136) | (iy < 7))


def shifted(v):
    return (pltpu.roll(v, 1, 1), v, pltpu.roll(v, ROWS - 1, 1))


def inner_kernel(x, g, t1, b1, t2, b2, part, xs, hs):
    iy = lax.axis_index("gy")
    for dy in range(3):
        xs[dy, 0] = jnp.zeros((ROWS, 256), BF16)
        xs[dy, SLAB + 1] = jnp.zeros((ROWS, 256), BF16)
        hs[dy, 0] = jnp.zeros((BY, 256), BF16)
        hs[dy, SLAB + 1] = jnp.zeros((BY, 256), BF16)

    def shift(z, carry):
        for tx in range(2):
            v = x[tx, pl.ds(z, 1)].astype(F32)
            for dy, s in enumerate(shifted(v)):
                xs[dy, pl.ds(z + 1, 1), :, tx * 128 : tx * 128 + 128] = s.astype(BF16)
        return carry

    lax.fori_loop(0, SLAB, shift, 0)

    def first(n, carry):
        taps = [
            xs[dy, pl.ds(n * 4 + dz, 4)].reshape(4 * ROWS, 256)
            for dz in range(3)
            for dy in range(3)
        ]
        acc = jnp.dot(jnp.concatenate(taps, 1), t1[...], preferred_element_type=F32) + b1[...]
        h = jax.nn.gelu(acc).reshape(4, ROWS, 256)
        h = jnp.where(rows_inside(h.shape, iy), h, 0.0)
        for dy, s in enumerate(shifted(h)):
            hs[dy, pl.ds(n * 4 + 1, 4)] = s[:, 8 : 8 + BY].astype(BF16)
        return carry

    lax.fori_loop(0, 4, first, 0)

    def second(n, carry):
        taps = [
            hs[dy, pl.ds(n * 4 + dz, 4)].reshape(4 * BY, 256) for dz in range(3) for dy in range(3)
        ]
        taps += [g[tx, pl.ds(n * 4, 4)].reshape(4 * BY, 128) for tx in range(2)]
        acc = jnp.dot(jnp.concatenate(taps, 1), t2[...], preferred_element_type=F32) + b2[...]
        part[pl.ds(n * 4, 4)] = acc.reshape(4, BY, 256)
        return carry

    lax.fori_loop(0, 4, second, 0)


def inner_convs(x, g, t1, b1, t2, b2):
    vm = pl.BlockSpec(memory_space=VMEM)
    return pl.pallas_call(
        inner_kernel,
        in_specs=[vm] * 6,
        out_specs=vm,
        out_shape=jax.ShapeDtypeStruct((SLAB, BY, 256), F32),
        scratch_shapes=[
            VMEM((3, SLAB + 2, ROWS, 256), BF16),
            VMEM((3, SLAB + 2, BY, 256), BF16),
        ],
        compiler_params=params(32),
        cost_estimate=cost(2 * 20 * 256 * 256 * 2304, 6 * MIB),
        name="inner_convs",
    )(x, g, t1, b1, t2, b2)


def tile_row(tile):
    return ((tile >> 5) * 4 + ((tile >> 2) & 3)) * 8 + ((tile >> 4) & 1) * 4 + (tile & 3)


def edge_kernel(
    x, rlo, rhi, part, t1, b1, t2, headx, ids, out, table, ans_ylo, ans_yhi, ans_x, es, hs, vel
):
    ix = lax.axis_index("gx")
    iy = lax.axis_index("gy")
    for dy in range(3):
        es[dy, 0] = jnp.zeros((ROWS, 256), BF16)
        es[dy, SLAB + 1] = jnp.zeros((ROWS, 256), BF16)
        hs[dy, 0] = jnp.zeros((BY, 128), BF16)
        hs[dy, SLAB + 1] = jnp.zeros((BY, 128), BF16)
    lane = lanes_of((1, ROWS, 128))

    def put(z, low, high):
        for k, v in enumerate((low, high)):
            for dy, s in enumerate(shifted(v)):
                es[dy, pl.ds(z + 1, 1), :, k * 128 : k * 128 + 128] = s.astype(BF16)

    def shift(z, carry):
        a = rlo[pl.ds(z, 1)].astype(F32)
        b = rhi[pl.ds(z, 1)].astype(F32)
        for half in range(2):
            zz = z + 8 * half
            own0 = x[0, pl.ds(zz, 1)].astype(F32)
            own1 = x[1, pl.ds(zz, 1)].astype(F32)
            left = pltpu.roll(a, 64, 2) if half == 0 else a
            right = b if half == 0 else pltpu.roll(b, 64, 2)
            put(zz, jnp.where(lane < 64, own0, left), jnp.where(lane < 64, right, own1))
        return carry

    lax.fori_loop(0, 8, shift, 0)

    def first(n, carry):
        taps = [
            es[dy, pl.ds(n * 4 + dz, 4)].reshape(4 * ROWS, 256)
            for dz in range(3)
            for dy in range(3)
        ]
        acc = jnp.dot(jnp.concatenate(taps, 1), t1[...], preferred_element_type=F32) + b1[...]
        h = jax.nn.gelu(acc).reshape(4, ROWS, 128)
        ln = lanes_of(h.shape)
        keep = ((ln >= 32) | (ix > 0)) & ((ln < 96) | (ix < 15))
        h = jnp.where(rows_inside(h.shape, iy) & keep, h, 0.0)
        for dy, s in enumerate(shifted(h)):
            hs[dy, pl.ds(n * 4 + 1, 4)] = s[:, 8 : 8 + BY].astype(BF16)
        return carry

    lax.fori_loop(0, 4, first, 0)

    def second(n, carry):
        taps = [
            hs[dy, pl.ds(n * 4 + dz, 4)].reshape(4 * BY, 128) for dz in range(3) for dy in range(3)
        ]
        acc = jnp.dot(jnp.concatenate(taps, 1), t2[...], preferred_element_type=F32)
        for k in range(4):
            z = n * 4 + k
            total = (acc[k * BY : (k + 1) * BY] + part[z]).T.astype(BF16)
            out[:, pl.ds(z, 1)] = total.reshape(32, 1, 8, 128)
            v = jnp.dot(headx[...], total, preferred_element_type=F32)
            for a in range(3):
                vel[a, pl.ds(z, 1)] = v[8 * a : 8 * a + 8].reshape(1, 8, 128)
        return carry

    lax.fori_loop(0, 4, second, 0)

    table[...] = jnp.zeros_like(table)
    sub = lax.broadcasted_iota(jnp.int32, (4, 8, 128), 1)
    ln = lanes_of((4, 8, 128))
    for a in range(3):
        v = vel[a].reshape(4, 2, 2, 8, 128)
        v0, v1 = v[:, 0], v[:, 1]
        l2 = lanes_of(v0.shape)
        m0 = jnp.where(l2 < 64, v0, pltpu.roll(v1, 64, 3))
        m1 = jnp.where(l2 < 64, pltpu.roll(v0, 64, 3), v1)
        for k, m in enumerate((m0, m1)):
            v0, v1 = m[:, 0], m[:, 1]
            n0 = jnp.where(ln % 64 < 32, v0, pltpu.roll(v1, 32, 2))
            n1 = jnp.where(ln % 64 < 32, pltpu.roll(v0, 96, 2), v1)
            for kk, w in enumerate((n0, n1)):
                for bit, step in ((2, 16), (1, 8)):
                    up = pltpu.roll(pltpu.roll(w, 8 - bit, 1), step, 2)
                    down = pltpu.roll(pltpu.roll(w, bit, 1), 128 - step, 2)
                    s1 = (sub & bit) != 0
                    l1 = (ln & step) != 0
                    w = jnp.where(s1 == l1, w, jnp.where(l1, up, down))
                for tz in range(4):
                    row = (tz * 4 + k * 2 + kk) * 8
                    table[row : row + 8, a, :] = w[tz]

    srow = lax.broadcasted_iota(jnp.int32, (8, 128), 0)
    places = [(ans_ylo, 0), (ans_ylo, 1), (ans_ylo, 2), (ans_yhi, 0), (ans_yhi, 1), (ans_yhi, 2)]
    places += [(ans_x, 0), (ans_x, 1)]
    for n, (ref, k) in enumerate(places):

        def answer(j, carry, n=n, ref=ref, k=k):
            halves = []
            for h in range(2):
                r0 = table[tile_row(ids[n, j * 4 + 2 * h])]
                r1 = table[tile_row(ids[n, j * 4 + 2 * h + 1])]
                halves.append(jnp.where(srow < 4, r0, pltpu.roll(r1, 4, 0)))
            ref[k, pl.ds(pl.multiple_of(j * 16, 16), 16), :] = jnp.concatenate(halves, 0).astype(
                BF16
            )
            return carry

        lax.fori_loop(0, SLOTS // 4, answer, 0, unroll=2)


def edge_convs(x, rlo, rhi, part, t1, b1, t2, headx, ids):
    vm = pl.BlockSpec(memory_space=VMEM)
    ans = jax.ShapeDtypeStruct((3, 64, 128), BF16)
    return pl.pallas_call(
        edge_kernel,
        in_specs=[vm] * 8 + [pl.BlockSpec(memory_space=SMEM)],
        out_specs=[vm] * 5,
        out_shape=[
            jax.ShapeDtypeStruct((C, SLAB, 8, BY), BF16),
            jax.ShapeDtypeStruct((128, 8, 128), F32),
            ans,
            ans,
            jax.ShapeDtypeStruct((2, 64, 128), BF16),
        ],
        scratch_shapes=[
            VMEM((3, SLAB + 2, ROWS, 256), BF16),
            VMEM((3, SLAB + 2, BY, 128), BF16),
            VMEM((3, SLAB, 8, 128), F32),
        ],
        compiler_params=params(32),
        cost_estimate=cost(2 * 9 * 256 * 256 * 2304, 6 * MIB),
        name="edge_convs",
    )(x, rlo, rhi, part, t1, b1, t2, headx, ids)


def read_four(rows, w_ref, first):
    lhs = jnp.concatenate(rows, 0).astype(BF16)
    w = w_ref[first * 128 : (first + 4) * 128, :]
    r = lax.dot_general(lhs, w, (((1,), (1,)), ((), ())), preferred_element_type=F32)
    return [r[8 * j : 8 * j + 3, 128 * j : 128 * j + 128] for j in range(4)]


def own_read_kernel(ids, table, w_ref, out):
    step = pl.program_id(0)
    for group in range(STEP // 4):
        rows = [table[tile_row(ids[step * STEP + group * 4 + j])] for j in range(4)]
        for j, v in enumerate(read_four(rows, w_ref, group * 4)):
            at = (group * 4 + j) * 128
            out[:, at : at + 128] = v


def own_read(ids, table, weights, particles):
    return pl.pallas_call(
        own_read_kernel,
        grid=(STEPS,),
        in_specs=[
            pl.BlockSpec(memory_space=SMEM),
            pl.BlockSpec((128, 8, 128), lambda i: (0, 0, 0)),
            pl.BlockSpec((STEP * 128, 128), lambda i: (i, 0)),
        ],
        out_specs=pl.BlockSpec((3, STEP * 128), lambda i: (0, i)),
        out_shape=jax.ShapeDtypeStruct((3, particles), F32),
        compiler_params=params(16, True),
        cost_estimate=cost(2 * 128 * 32 * 128 * 128, 5 * MIB),
        name="own_read",
    )(ids, table, weights)


def far_read_kernel(slots, counts, blo, bhi, ylo, yhi, w_ref, vel, out, table):
    step = pl.program_id(0)

    @pl.when(step == 0)
    def _():
        places = [(blo, 0), (blo, 1), (blo, 2), (ylo, 1), None, (yhi, 1)]
        places += [(bhi, 0), (bhi, 1), (bhi, 2)]
        for k, place in enumerate(places):
            if place is None:
                table[k * SLOTS : (k + 1) * SLOTS] = jnp.zeros((SLOTS, 8, 128), F32)
                continue
            v = place[0][place[1]].astype(F32).reshape(8, 8, 128)
            turned = pltpu.roll(v, 4, 1)
            for j in range(8):
                table[k * SLOTS + 2 * j] = v[j]
                table[k * SLOTS + 2 * j + 1] = turned[j]

    count = counts[0]
    for group in range(STEP // 4):
        first = step * STEP + group * 4
        rows = [table[slots[first + j]] for j in range(4)]
        for j, v in enumerate(read_four(rows, w_ref, group * 4)):
            at = (group * 4 + j) * 128
            out[:, at : at + 128] = jnp.where(128 + first + j < count, v, 0.0)


def far_read(slots, counts, blo, bhi, ylo, yhi, weights, vel):
    smem = pl.BlockSpec(memory_space=SMEM)
    ans = pl.BlockSpec((3, 64, 128), lambda i: (0, 0, 0))
    return pl.pallas_call(
        far_read_kernel,
        grid=(STEPS,),
        in_specs=[
            smem,
            smem,
            ans,
            ans,
            ans,
            ans,
            pl.BlockSpec((STEP * 128, 128), lambda i: (STEPS + i, 0)),
            pl.BlockSpec(memory_space=pl.ANY),
        ],
        out_specs=pl.BlockSpec((3, STEP * 128), lambda i: (0, STEPS + i)),
        out_shape=jax.ShapeDtypeStruct(vel.shape, F32),
        scratch_shapes=[VMEM((9 * SLOTS, 8, 128), F32)],
        input_output_aliases={7: 0},
        compiler_params=params(16, True),
        cost_estimate=cost(2 * 128 * 32 * 128 * 128, 5 * MIB),
        name="far_read",
    )(slots, counts, blo, bhi, ylo, yhi, weights, vel)


def band(pin, pout):
    out = np.zeros((len(pin), len(pout), 3), np.float32)
    for i, p in enumerate(pin):
        for j, q in enumerate(pout):
            if p is not None and q is not None and abs(p - q) <= 1:
                out[i, j, p - q + 1] = 1
    return jnp.asarray(out, BF16)


def banded(conv, pin, pout, out_last):
    taps = conv.reshape(3, 3, 3, C, C)
    spec = "zdyoc,pqd->zypcoq" if out_last else "zdyoc,pqd->zypcqo"
    t = jnp.einsum(spec, taps, band(pin, pout), preferred_element_type=F32).astype(BF16)
    return t.reshape(9 * len(pin) * C, len(pout) * C)


def on_device(
    features,
    weights,
    owners,
    tile_ids,
    counts,
    conv_first,
    bias_first,
    conv_second,
    bias_second,
    head,
):
    particles = features.shape[1]

    def step(x, axis, by):
        size = lax.axis_size(axis)
        return lax.ppermute(
            x, axis, [(i, i + by) for i in range(size) if 0 <= i + by < size]
        )

    none = None
    t1a = banded(conv_first, [0, 1, 2, 3, 4, 5, 6, 7], [none, 1, 2, 3, 4, 5, 6, none], False)
    t1b = banded(conv_first, [0, 1, -2, -1, 8, 9, 6, 7], [-1, 0, 7, 8], False)
    t2a = banded(conv_second, [none, 1, 2, 3, 4, 5, 6, none], list(range(8)), True)
    t2b = banded(conv_second, [-1, 0, 7, 8], list(range(8)), True)
    same = np.zeros((8, C, C, 8), np.float32)
    for q in range(8):
        same[q, np.arange(C), np.arange(C), q] = 1
    t2a = jnp.concatenate([t2a, jnp.asarray(same.reshape(256, 256), BF16)], 0)
    b1a = jnp.tile(bias_first, 8)[None, :]
    b1b = jnp.tile(bias_first, 4)[None, :]
    b2 = jnp.repeat(bias_second, 8)[None, :]
    headx = jnp.einsum("ao,xw->axow", head, jnp.eye(8, dtype=BF16)).reshape(24, 256)
    headx = jnp.concatenate([headx, jnp.zeros((8, 256), BF16)], 0)

    lo, mid, hi, slots = far_splat(features, weights, owners, tile_ids, counts)
    from_xlo = step(hi, "gx", 1)
    from_xhi = step(lo, "gx", -1)
    own = own_splat(features, weights, tile_ids)
    to_hi = jnp.stack([from_xlo[2], mid[2], from_xhi[2]])
    to_lo = jnp.stack([from_xlo[0], mid[0], from_xhi[0]])
    from_ylo = step(to_hi, "gy", 1)
    from_yhi = step(to_lo, "gy", -1)
    g, ylo, yhi, ids = sum_tiles(own, from_ylo, from_yhi, from_xlo, from_xhi)

    rlo = step(yhi, "gy", 1)
    rhi = step(ylo, "gy", -1)
    x, slo, shi = widen_y(g, rlo, rhi)
    xlo = step(shi, "gx", 1)
    xhi = step(slo, "gx", -1)
    part = inner_convs(x, g, t1a, b1a, t2a, b2)
    grid_out, table, ans_ylo, ans_yhi, ans_x = edge_convs(
        x, xlo, xhi, part, t1b, b1b, t2b, headx, ids
    )

    back_yhi = step(ans_ylo, "gy", -1)
    back_ylo = step(ans_yhi, "gy", 1)
    vel = own_read(tile_ids, table, weights, particles)
    to_lo = jnp.stack([back_ylo[0], ans_x[0], back_yhi[0]])
    to_hi = jnp.stack([back_ylo[2], ans_x[1], back_yhi[2]])
    back_xhi = step(to_lo, "gx", -1)
    back_xlo = step(to_hi, "gx", 1)
    velocity = far_read(slots, counts, back_xlo, back_xhi, back_ylo, back_yhi, weights, vel)
    return grid_out, velocity


def solution(mesh):
    in_specs = (
        P(None, ("gx", "gy")),
        P(("gx", "gy"), None),
        P(("gx", "gy")),
        P(("gx", "gy")),
        P(("gx", "gy")),
        P(),
        P(),
        P(),
        P(),
        P(),
    )
    out_specs = (P(None, None, "gx", "gy"), P(None, ("gx", "gy")))
    return jax.shard_map(
        on_device, mesh=mesh, in_specs=in_specs, out_specs=out_specs, check_vma=False
    )
```

```python
import jax
import jax.numpy as jnp
import numpy as np
from jax import lax
from jax.experimental import pallas as pl
from jax.experimental.pallas import tpu as pltpu
from jax.sharding import PartitionSpec as P

C = 32
SLAB = 16
BY = 128
SLOTS = 16
PAY = SLOTS * 32 + 16
ROWS = 144
STEP = 16
STEPS = 8
MIB = 1 << 20
F32 = jnp.float32
BF16 = jnp.bfloat16
VMEM = pltpu.VMEM
SMEM = pltpu.SMEM


def lanes_of(shape):
    return lax.broadcasted_iota(jnp.int32, shape, len(shape) - 1)


def params(limit, grid=False):
    if grid:
        return pltpu.CompilerParams(
            dimension_semantics=("arbitrary",), vmem_limit_bytes=limit * MIB
        )
    return pltpu.CompilerParams(vmem_limit_bytes=limit * MIB)


def cost(flops, nbytes):
    return pl.CostEstimate(flops=flops, bytes_accessed=nbytes, transcendentals=0)


def splat_four(f, w_ref, first):
    parts = []
    for j in (0, 2):
        at = (first + j) * 128
        fa = f[:, at : at + 128]
        fb = f[:, at + 128 : at + 256]
        none = jnp.zeros_like(fa)
        lhs = jnp.concatenate(
            [jnp.concatenate([fa, none], 1), jnp.concatenate([none, fb], 1)], 0
        )
        parts.append(jnp.dot(lhs, w_ref[at : at + 256, :], preferred_element_type=F32))
    a = jnp.concatenate(parts, 0).astype(BF16).T.astype(F32)
    a = a.reshape(4, 2, 2, 8, 128)
    lane = lanes_of((4, 2, 8, 128))
    v0, v1 = a[:, 0], a[:, 1]
    n0 = jnp.where(lane < 64, v0, pltpu.roll(v1, 64, 3))
    n1 = jnp.where(lane < 64, pltpu.roll(v0, 64, 3), v1)
    lane = lanes_of((4, 8, 128))
    tiles = []
    for n in (n0, n1):
        v0, v1 = n[:, 0], n[:, 1]
        tiles.append(jnp.where(lane % 64 < 32, v0, pltpu.roll(v1, 32, 2)))
        tiles.append(jnp.where(lane % 64 < 32, pltpu.roll(v0, 96, 2), v1))
    return tiles


def chunk_copies(f_hbm, w_hbm, fv, wv, sems, first):
    rows = STEP * 128
    pairs = []
    for c in range(STEPS):
        at = first * 128 + c * rows
        pairs.append(
            (
                pltpu.make_async_copy(
                    w_hbm.at[pl.ds(at, rows)], wv.at[pl.ds(c * rows, rows)], sems.at[c]
                ),
                pltpu.make_async_copy(f_hbm.at[:, pl.ds(at, rows)], fv.at[c], sems.at[STEPS + c]),
            )
        )
    return pairs


def far_splat_kernel(
    owners_h, ids_h, counts_h, f_hbm, w_hbm, lo, mid, hi, slots,
    fv, wv, tiles, idrows, filled, owners, ids, counts, sems, isems,
):
    ix = lax.axis_index("gx")
    iy = lax.axis_index("gy")
    copies = chunk_copies(f_hbm, w_hbm, fv, wv, sems, 128)
    small = [
        pltpu.make_async_copy(src, dst, isems.at[k])
        for k, (src, dst) in enumerate(((owners_h, owners), (ids_h, ids), (counts_h, counts)))
    ]
    for copy in small:
        copy.start()
    for pair in copies:
        for copy in pair:
            copy.start()
    tiles[...] = jnp.zeros_like(tiles)
    idrows[...] = jnp.zeros_like(idrows)
    for k in range(9):
        filled[k] = 0
    for copy in small:
        copy.wait()
    lane = lanes_of((1, 128))
    count = counts[0]
    for c, pair in enumerate(copies):
        for copy in pair:
            copy.wait()
        got = []
        for group in range(STEP // 4):
            got += splat_four(fv.at[c], wv.at[pl.ds(c * STEP * 128, STEP * 128)], group * 4)
        for j in range(STEP):
            block = c * STEP + j
            owner = owners[128 + block]
            live = 128 + block < count
            target = ((owner >> 3) - ix + 1) * 3 + (owner & 7) - iy + 1
            target = jnp.where(live, target, 4)
            rank = filled[target]
            filled[target] = jnp.where(live, rank + 1, 0)
            slot = target * SLOTS + rank
            slots[block] = slot
            tiles[slot] = got[j].reshape(32, 128).astype(BF16)
            row = idrows[pl.ds(target, 1), :]
            idrows[pl.ds(target, 1), :] = jnp.where(
                lane == rank, ids[128 + block].astype(F32), row
            )
    for dx, out in enumerate((lo, mid, hi)):
        for dy in range(3):
            k = dx * 3 + dy
            out[dy, 0 : SLOTS * 32, :] = tiles[k * SLOTS : (k + 1) * SLOTS].reshape(
                SLOTS * 32, 128
            )
            out[dy, SLOTS * 32 : PAY, :] = jnp.broadcast_to(
                idrows[k : k + 1, :], (16, 128)
            ).astype(BF16)


def far_splat(features, weights, owners, ids, counts):
    pay = jax.ShapeDtypeStruct((3, PAY, 128), BF16)
    vm = pl.BlockSpec(memory_space=VMEM)
    anywhere = pl.BlockSpec(memory_space=pl.ANY)
    return pl.pallas_call(
        far_splat_kernel,
        in_specs=[anywhere] * 5,
        out_specs=[vm, vm, vm, pl.BlockSpec(memory_space=SMEM)],
        out_shape=[pay, pay, pay, jax.ShapeDtypeStruct((128,), jnp.int32)],
        scratch_shapes=[
            VMEM((STEPS, C, STEP * 128), BF16),
            VMEM((STEPS * STEP * 128, 128), BF16),
            VMEM((9 * SLOTS, 32, 128), BF16),
            VMEM((16, 128), F32),
            SMEM((9,), jnp.int32),
            SMEM((256,), jnp.int32),
            SMEM((256,), jnp.int32),
            SMEM((1,), jnp.int32),
            pltpu.SemaphoreType.DMA((2 * STEPS,)),
            pltpu.SemaphoreType.DMA((3,)),
        ],
        compiler_params=params(56),
        cost_estimate=cost(2 * 128 * 32 * 128 * 128, 6 * MIB),
        name="far_splat",
    )(owners, ids, counts, features, weights)


def tile_place(tile):
    return (tile >> 5) * 4, (tile >> 4) & 1, pl.multiple_of((tile & 15) * 8, 8)


def own_splat_kernel(ids, f_hbm, w_hbm, out, fv, wv, grid, sems):
    copies = chunk_copies(f_hbm, w_hbm, fv, wv, sems, 0)
    for pair in copies:
        for copy in pair:
            copy.start()
    for c, pair in enumerate(copies):
        for copy in pair:
            copy.wait()
        got = []
        for group in range(STEP // 4):
            got += splat_four(fv.at[c], wv.at[pl.ds(c * STEP * 128, STEP * 128)], group * 4)
        for j in range(STEP):
            z, tx, y = tile_place(ids[c * STEP + j])
            grid[tx, pl.ds(z, 4), pl.ds(y, 8), :] = got[j]
    out[...] = grid[...].astype(BF16)


def own_splat(features, weights, ids):
    anywhere = pl.BlockSpec(memory_space=pl.ANY)
    return pl.pallas_call(
        own_splat_kernel,
        in_specs=[pl.BlockSpec(memory_space=SMEM), anywhere, anywhere],
        out_specs=pl.BlockSpec(memory_space=VMEM),
        out_shape=jax.ShapeDtypeStruct((2, SLAB, BY, 128), BF16),
        scratch_shapes=[
            VMEM((STEPS, C, STEP * 128), BF16),
            VMEM((STEPS * STEP * 128, 128), BF16),
            VMEM((2, SLAB, BY, 128), F32),
            pltpu.SemaphoreType.DMA((2 * STEPS,)),
        ],
        compiler_params=params(56),
        cost_estimate=cost(2 * 128 * 32 * 128 * 128, 6 * MIB),
        name="own_splat",
    )(ids, features, weights)


def sum_kernel(own, from_ylo, from_yhi, from_xlo, from_xhi, g, ylo, yhi, ids, grid, idv, sem):
    groups = [(from_ylo, 0), (from_ylo, 1), (from_ylo, 2)]
    groups += [(from_yhi, 0), (from_yhi, 1), (from_yhi, 2)]
    groups += [(from_xlo, 1), (from_xhi, 1)]
    rows = [ref[k, SLOTS * 32 : PAY, :].astype(F32)[0:1] for ref, k in groups]
    idv[...] = jnp.concatenate(rows, 0).astype(jnp.int32)
    copy = pltpu.make_async_copy(idv, ids, sem)
    copy.start()
    grid[...] = own[...].astype(F32)
    copy.wait()
    for n, (ref, k) in enumerate(groups):

        def add(j, carry, n=n, ref=ref, k=k):
            z, tx, y = tile_place(ids[n, j])
            tile = ref[k, pl.ds(pl.multiple_of(j * 32, 32), 32), :].astype(F32).reshape(4, 8, 128)
            grid[tx, pl.ds(z, 4), pl.ds(y, 8), :] += tile
            return carry

        lax.fori_loop(0, SLOTS, add, 0, unroll=4)
    g[...] = grid[...].astype(BF16)
    for tx in range(2):
        for r in range(2):
            ylo[tx * 2 + r] = grid[tx, :, r, :].astype(BF16)
            yhi[tx * 2 + r] = grid[tx, :, BY - 2 + r, :].astype(BF16)


def sum_tiles(own, from_ylo, from_yhi, from_xlo, from_xhi):
    vm = pl.BlockSpec(memory_space=VMEM)
    edge = jax.ShapeDtypeStruct((4, SLAB, 128), BF16)
    return pl.pallas_call(
        sum_kernel,
        in_specs=[vm] * 5,
        out_specs=[vm, vm, vm, pl.BlockSpec(memory_space=SMEM)],
        out_shape=[
            jax.ShapeDtypeStruct((2, SLAB, BY, 128), BF16),
            edge,
            edge,
            jax.ShapeDtypeStruct((8, 128), jnp.int32),
        ],
        scratch_shapes=[
            VMEM((2, SLAB, BY, 128), F32),
            VMEM((8, 128), jnp.int32),
            pltpu.SemaphoreType.DMA,
        ],
        compiler_params=params(16),
        cost_estimate=cost(1000, 4 * MIB),
        name="sum_tiles",
    )(own, from_ylo, from_yhi, from_xlo, from_xhi)


def widen_kernel(g, rlo, rhi, x, slo, shi, edge):
    edge[...] = jnp.zeros_like(edge)
    for tx in range(2):
        for r in range(2):
            edge[tx, 0, :, 6 + r, :] = rlo[tx * 2 + r].astype(F32)
            edge[tx, 1, :, r, :] = rhi[tx * 2 + r].astype(F32)
    lane = lanes_of((ROWS, 128))

    def plane(tx, z):
        return jnp.concatenate([edge[tx, 0, z], g[tx, z].astype(F32), edge[tx, 1, z]], 0)

    def pair(z, carry):
        a, b = plane(0, z), plane(0, z + 8)
        x[0, z] = a.astype(BF16)
        x[0, z + 8] = b.astype(BF16)
        slo[z] = jnp.where(lane < 64, a, pltpu.roll(b, 64, 1)).astype(BF16)
        a, b = plane(1, z), plane(1, z + 8)
        x[1, z] = a.astype(BF16)
        x[1, z + 8] = b.astype(BF16)
        shi[z] = jnp.where(lane < 64, pltpu.roll(a, 64, 1), b).astype(BF16)
        return carry

    lax.fori_loop(0, 8, pair, 0)


def widen_y(g, rlo, rhi):
    vm = pl.BlockSpec(memory_space=VMEM)
    side = jax.ShapeDtypeStruct((SLAB // 2, ROWS, 128), BF16)
    return pl.pallas_call(
        widen_kernel,
        in_specs=[vm] * 3,
        out_specs=[vm] * 3,
        out_shape=[jax.ShapeDtypeStruct((2, SLAB, ROWS, 128), BF16), side, side],
        scratch_shapes=[VMEM((2, 2, SLAB, 8, 128), F32)],
        compiler_params=params(8),
        cost_estimate=cost(1000, 3 * MIB),
        name="widen_y",
    )(g, rlo, rhi)


def rows_inside(shape, iy):
    row = lax.broadcasted_iota(jnp.int32, shape, 1)
    return ((row != 7) | (iy > 0)) & ((row != 136) | (iy < 7))


def shifted(v):
    return (pltpu.roll(v, 1, 1), v, pltpu.roll(v, ROWS - 1, 1))


def inner_kernel(x, g, t1, b1, t2, b2, part, xs, hs):
    iy = lax.axis_index("gy")
    for dy in range(3):
        xs[dy, 0] = jnp.zeros((ROWS, 256), BF16)
        xs[dy, SLAB + 1] = jnp.zeros((ROWS, 256), BF16)
        hs[dy, 0] = jnp.zeros((BY, 256), BF16)
        hs[dy, SLAB + 1] = jnp.zeros((BY, 256), BF16)

    def shift(z, carry):
        for tx in range(2):
            v = x[tx, pl.ds(z, 1)].astype(F32)
            for dy, s in enumerate(shifted(v)):
                xs[dy, pl.ds(z + 1, 1), :, tx * 128 : tx * 128 + 128] = s.astype(BF16)
        return carry

    lax.fori_loop(0, SLAB, shift, 0)

    def first(n, carry):
        taps = [
            xs[dy, pl.ds(n * 4 + dz, 4)].reshape(4 * ROWS, 256)
            for dz in range(3)
            for dy in range(3)
        ]
        acc = jnp.dot(jnp.concatenate(taps, 1), t1[...], preferred_element_type=F32) + b1[...]
        h = jax.nn.gelu(acc).reshape(4, ROWS, 256)
        h = jnp.where(rows_inside(h.shape, iy), h, 0.0)
        for dy, s in enumerate(shifted(h)):
            hs[dy, pl.ds(n * 4 + 1, 4)] = s[:, 8 : 8 + BY].astype(BF16)
        return carry

    lax.fori_loop(0, 4, first, 0)

    def second(n, carry):
        taps = [
            hs[dy, pl.ds(n * 4 + dz, 4)].reshape(4 * BY, 256) for dz in range(3) for dy in range(3)
        ]
        taps += [g[tx, pl.ds(n * 4, 4)].reshape(4 * BY, 128) for tx in range(2)]
        acc = jnp.dot(jnp.concatenate(taps, 1), t2[...], preferred_element_type=F32) + b2[...]
        part[pl.ds(n * 4, 4)] = acc.reshape(4, BY, 256)
        return carry

    lax.fori_loop(0, 4, second, 0)


def inner_convs(x, g, t1, b1, t2, b2):
    vm = pl.BlockSpec(memory_space=VMEM)
    return pl.pallas_call(
        inner_kernel,
        in_specs=[vm] * 6,
        out_specs=vm,
        out_shape=jax.ShapeDtypeStruct((SLAB, BY, 256), F32),
        scratch_shapes=[
            VMEM((3, SLAB + 2, ROWS, 256), BF16),
            VMEM((3, SLAB + 2, BY, 256), BF16),
        ],
        compiler_params=params(32),
        cost_estimate=cost(2 * 20 * 256 * 256 * 2304, 6 * MIB),
        name="inner_convs",
    )(x, g, t1, b1, t2, b2)


def tile_row(tile):
    return ((tile >> 5) * 4 + ((tile >> 2) & 3)) * 8 + ((tile >> 4) & 1) * 4 + (tile & 3)


def edge_kernel(
    x, rlo, rhi, part, t1, b1, t2, headx, ids, out, table, ans_ylo, ans_yhi, ans_x, es, hs, vel
):
    ix = lax.axis_index("gx")
    iy = lax.axis_index("gy")
    for dy in range(3):
        es[dy, 0] = jnp.zeros((ROWS, 256), BF16)
        es[dy, SLAB + 1] = jnp.zeros((ROWS, 256), BF16)
        hs[dy, 0] = jnp.zeros((BY, 128), BF16)
        hs[dy, SLAB + 1] = jnp.zeros((BY, 128), BF16)
    lane = lanes_of((1, ROWS, 128))

    def put(z, low, high):
        for k, v in enumerate((low, high)):
            for dy, s in enumerate(shifted(v)):
                es[dy, pl.ds(z + 1, 1), :, k * 128 : k * 128 + 128] = s.astype(BF16)

    def shift(z, carry):
        a = rlo[pl.ds(z, 1)].astype(F32)
        b = rhi[pl.ds(z, 1)].astype(F32)
        for half in range(2):
            zz = z + 8 * half
            own0 = x[0, pl.ds(zz, 1)].astype(F32)
            own1 = x[1, pl.ds(zz, 1)].astype(F32)
            left = pltpu.roll(a, 64, 2) if half == 0 else a
            right = b if half == 0 else pltpu.roll(b, 64, 2)
            put(zz, jnp.where(lane < 64, own0, left), jnp.where(lane < 64, right, own1))
        return carry

    lax.fori_loop(0, 8, shift, 0)

    def first(n, carry):
        taps = [
            es[dy, pl.ds(n * 4 + dz, 4)].reshape(4 * ROWS, 256)
            for dz in range(3)
            for dy in range(3)
        ]
        acc = jnp.dot(jnp.concatenate(taps, 1), t1[...], preferred_element_type=F32) + b1[...]
        h = jax.nn.gelu(acc).reshape(4, ROWS, 128)
        ln = lanes_of(h.shape)
        keep = ((ln >= 32) | (ix > 0)) & ((ln < 96) | (ix < 15))
        h = jnp.where(rows_inside(h.shape, iy) & keep, h, 0.0)
        for dy, s in enumerate(shifted(h)):
            hs[dy, pl.ds(n * 4 + 1, 4)] = s[:, 8 : 8 + BY].astype(BF16)
        return carry

    lax.fori_loop(0, 4, first, 0)

    def second(n, carry):
        taps = [
            hs[dy, pl.ds(n * 4 + dz, 4)].reshape(4 * BY, 128) for dz in range(3) for dy in range(3)
        ]
        acc = jnp.dot(jnp.concatenate(taps, 1), t2[...], preferred_element_type=F32)
        for k in range(4):
            z = n * 4 + k
            total = (acc[k * BY : (k + 1) * BY] + part[z]).T.astype(BF16)
            out[:, pl.ds(z, 1)] = total.reshape(32, 1, 8, 128)
            v = jnp.dot(headx[...], total, preferred_element_type=F32)
            for a in range(3):
                vel[a, pl.ds(z, 1)] = v[8 * a : 8 * a + 8].reshape(1, 8, 128)
        return carry

    lax.fori_loop(0, 4, second, 0)

    table[...] = jnp.zeros_like(table)
    sub = lax.broadcasted_iota(jnp.int32, (4, 8, 128), 1)
    ln = lanes_of((4, 8, 128))
    for a in range(3):
        v = vel[a].reshape(4, 2, 2, 8, 128)
        v0, v1 = v[:, 0], v[:, 1]
        l2 = lanes_of(v0.shape)
        m0 = jnp.where(l2 < 64, v0, pltpu.roll(v1, 64, 3))
        m1 = jnp.where(l2 < 64, pltpu.roll(v0, 64, 3), v1)
        for k, m in enumerate((m0, m1)):
            v0, v1 = m[:, 0], m[:, 1]
            n0 = jnp.where(ln % 64 < 32, v0, pltpu.roll(v1, 32, 2))
            n1 = jnp.where(ln % 64 < 32, pltpu.roll(v0, 96, 2), v1)
            for kk, w in enumerate((n0, n1)):
                for bit, step in ((2, 16), (1, 8)):
                    up = pltpu.roll(pltpu.roll(w, 8 - bit, 1), step, 2)
                    down = pltpu.roll(pltpu.roll(w, bit, 1), 128 - step, 2)
                    s1 = (sub & bit) != 0
                    l1 = (ln & step) != 0
                    w = jnp.where(s1 == l1, w, jnp.where(l1, up, down))
                for tz in range(4):
                    row = (tz * 4 + k * 2 + kk) * 8
                    table[row : row + 8, a, :] = w[tz]

    places = [(ans_ylo, 0), (ans_ylo, 1), (ans_ylo, 2), (ans_yhi, 0), (ans_yhi, 1), (ans_yhi, 2)]
    places += [(ans_x, 0), (ans_x, 1)]
    for n, (ref, k) in enumerate(places):

        def answer(j, carry, n=n, ref=ref, k=k):
            halves = []
            for h in range(2):
                r0 = table[tile_row(ids[n, j * 4 + 2 * h])]
                r1 = table[tile_row(ids[n, j * 4 + 2 * h + 1])]
                halves.append(two_blocks(r0, r1))
            ref[k, pl.ds(pl.multiple_of(j * 16, 16), 16), :] = jnp.concatenate(halves, 0).astype(
                BF16
            )
            return carry

        lax.fori_loop(0, SLOTS // 4, answer, 0, unroll=2)


def edge_convs(x, rlo, rhi, part, t1, b1, t2, headx, ids):
    vm = pl.BlockSpec(memory_space=VMEM)
    ans = jax.ShapeDtypeStruct((3, 64, 128), BF16)
    return pl.pallas_call(
        edge_kernel,
        in_specs=[vm] * 8 + [pl.BlockSpec(memory_space=SMEM)],
        out_specs=[vm] * 5,
        out_shape=[
            jax.ShapeDtypeStruct((C, SLAB, 8, BY), BF16),
            jax.ShapeDtypeStruct((128, 8, 128), F32),
            ans,
            ans,
            jax.ShapeDtypeStruct((2, 64, 128), BF16),
        ],
        scratch_shapes=[
            VMEM((3, SLAB + 2, ROWS, 256), BF16),
            VMEM((3, SLAB + 2, BY, 128), BF16),
            VMEM((3, SLAB, 8, 128), F32),
        ],
        compiler_params=params(32),
        cost_estimate=cost(2 * 9 * 256 * 256 * 2304, 6 * MIB),
        name="edge_convs",
    )(x, rlo, rhi, part, t1, b1, t2, headx, ids)


BATCH = 32


def read_batch(rows, w_ref, first, out, at, count):
    cells = rows.astype(BF16).T
    owner = lanes_of((128, 128)) >> 2
    right = jnp.concatenate(
        [jnp.where(owner == b, cells, jnp.zeros_like(cells)) for b in range(BATCH)], 0
    )
    left = jnp.concatenate(
        [w_ref[(first + b) * 128 : (first + b + 1) * 128, :] for b in range(BATCH)], 1
    )
    r = jnp.dot(left, right, preferred_element_type=F32).T
    for b in range(BATCH):
        v = r[4 * b : 4 * b + 3]
        if count is not None:
            v = jnp.where(128 + first + b < count, v, 0.0)
        out[:, at + b * 128 : at + (b + 1) * 128] = v


def two_blocks(r0, r1):
    row = lax.broadcasted_iota(jnp.int32, (8, 128), 0)
    return jnp.where(row < 4, r0, pltpu.roll(r1, 4, 0))


def weight_copies(w_hbm, wv, sems, first):
    n = 128 // BATCH
    rows = BATCH * 128
    return [
        pltpu.make_async_copy(
            w_hbm.at[pl.ds(first * 128 + k * rows, rows)], wv.at[pl.ds(k * rows, rows)], sems.at[k]
        )
        for k in range(n)
    ]


def own_read_kernel(ids, table, w_hbm, out, far_w, wv, sems, fsems):
    copies = weight_copies(w_hbm, wv, sems, 0)
    later = weight_copies(w_hbm, far_w, fsems, 128)
    for copy in copies + later:
        copy.start()
    for k, copy in enumerate(copies):
        rows = [
            two_blocks(
                table[tile_row(ids[k * BATCH + 2 * j])], table[tile_row(ids[k * BATCH + 2 * j + 1])]
            )
            for j in range(BATCH // 2)
        ]
        copy.wait()
        read_batch(jnp.concatenate(rows, 0), wv, k * BATCH, out, k * BATCH * 128, None)
    for copy in later:
        copy.wait()


def own_read(ids, table, weights, particles):
    vm = pl.BlockSpec(memory_space=VMEM)
    return pl.pallas_call(
        own_read_kernel,
        in_specs=[pl.BlockSpec(memory_space=SMEM), vm, pl.BlockSpec(memory_space=pl.ANY)],
        out_specs=[vm, vm],
        out_shape=[
            jax.ShapeDtypeStruct((3, particles // 2), F32),
            jax.ShapeDtypeStruct((particles // 2, 128), BF16),
        ],
        scratch_shapes=[
            VMEM((particles // 2, 128), BF16),
            pltpu.SemaphoreType.DMA((128 // BATCH,)),
            pltpu.SemaphoreType.DMA((128 // BATCH,)),
        ],
        compiler_params=params(48),
        cost_estimate=cost(2 * 128 * 32 * 128 * 128, 9 * MIB),
        name="own_read",
    )(ids, table, weights)


def far_read_kernel(slots, counts, blo, bhi, ylo, yhi, w, near, out, table):
    places = [(blo, 0), (blo, 1), (blo, 2), (ylo, 1), None, (yhi, 1)]
    places += [(bhi, 0), (bhi, 1), (bhi, 2)]
    for k, place in enumerate(places):
        if place is None:
            table[k * SLOTS : (k + 1) * SLOTS] = jnp.zeros((SLOTS, 8, 128), F32)
            continue
        v = place[0][place[1]].astype(F32).reshape(8, 8, 128)
        turned = pltpu.roll(v, 4, 1)
        for j in range(8):
            table[k * SLOTS + 2 * j] = v[j]
            table[k * SLOTS + 2 * j + 1] = turned[j]
    half = near.shape[1]
    out[:, 0:half] = near[...]
    for k in range(128 // BATCH):
        rows = [
            two_blocks(table[slots[k * BATCH + 2 * j]], table[slots[k * BATCH + 2 * j + 1]])
            for j in range(BATCH // 2)
        ]
        read_batch(
            jnp.concatenate(rows, 0), w, k * BATCH, out, half + k * BATCH * 128, counts[0]
        )


def far_read(slots, counts, blo, bhi, ylo, yhi, w, near):
    vm = pl.BlockSpec(memory_space=VMEM)
    smem = pl.BlockSpec(memory_space=SMEM)
    return pl.pallas_call(
        far_read_kernel,
        in_specs=[smem, smem] + [vm] * 6,
        out_specs=vm,
        out_shape=jax.ShapeDtypeStruct((3, 2 * near.shape[1]), F32),
        scratch_shapes=[VMEM((9 * SLOTS, 8, 128), F32)],
        compiler_params=params(24),
        cost_estimate=cost(2 * 128 * 32 * 128 * 128, 5 * MIB),
        name="far_read",
    )(slots, counts, blo, bhi, ylo, yhi, w, near)


def band(pin, pout, out_last):
    out = np.zeros((4, C, len(pin), len(pout), C), np.float32)
    for i, p in enumerate(pin):
        for j, q in enumerate(pout):
            if p is not None and q is not None and abs(p - q) <= 1:
                out[p - q + 1, np.arange(C), i, j, np.arange(C)] = 1
    if out_last:
        out = out.swapaxes(3, 4)
    return jnp.asarray(out.reshape(4 * C, -1), BF16)


def prepare_kernel(
    c1, c2, bias1, bias2, head, e1a, e1b, e2a, e2b, t1a, t1b, t2a, t2b, hx, b1a, b1b, b2
):
    one = (
        lax.broadcasted_iota(jnp.int32, (C, C), 0) == lax.broadcasted_iota(jnp.int32, (C, C), 1)
    ).astype(BF16)
    nothing = jnp.zeros((C, C), BF16)
    for conv, made in ((c1, ((e1a, t1a, 256), (e1b, t1b, 128))), (c2, ((e2a, t2a, 256), (e2b, t2b, 256)))):
        pieces = []
        for k in range(9):
            pieces += [conv[k // 3 * 9 + d * 3 + k % 3] for d in range(3)] + [nothing]
        turned = lax.dot_general(
            one, jnp.concatenate(pieces, 0), (((1,), (1,)), ((), ())), preferred_element_type=F32
        ).astype(BF16)
        lhs = jnp.concatenate([turned[:, 128 * k : 128 * k + 128] for k in range(9)], 0)
        for e, t, width in made:
            planes = e.shape[1] // width
            for p in range(planes):
                r = jnp.dot(lhs, e[:, p * width : (p + 1) * width], preferred_element_type=F32)
                r = r.astype(BF16)
                for k in range(9):
                    at = (k * planes + p) * C
                    t[at : at + C, :] = r[C * k : C * k + C]
    row = lax.broadcasted_iota(jnp.int32, (256, 256), 0)
    col = lanes_of((256, 256))
    t2a[2304:2560, :] = ((row & 31) == (col >> 3)).astype(F32).astype(BF16) * (
        (row >> 5) == (col & 7)
    ).astype(F32).astype(BF16)
    spread = (
        lax.broadcasted_iota(jnp.int32, (C, 256), 0) == (lanes_of((C, 256)) >> 3)
    ).astype(F32)
    wide = jnp.dot(head[...], spread.astype(BF16), preferred_element_type=F32)
    keep = (lanes_of((8, 256)) & 7) == lax.broadcasted_iota(jnp.int32, (8, 256), 0)
    parts = [jnp.where(keep, jnp.broadcast_to(wide[a : a + 1], (8, 256)), 0.0) for a in range(3)]
    hx[...] = jnp.concatenate(parts + [jnp.zeros((8, 256), F32)], 0).astype(BF16)
    b1 = jnp.concatenate([bias1[...]] * 8, 1)
    b1a[...] = b1
    b1b[...] = b1[:, 0:128]
    b2[...] = jnp.dot(
        bias2[...], spread, preferred_element_type=F32, precision=lax.Precision.HIGHEST
    )


def prepare(conv_first, conv_second, bias_first, bias_second, head):
    none = None
    inner = [none, 1, 2, 3, 4, 5, 6, none]
    every = list(range(8))
    e1a = band(every, inner, False)
    e1b = band([0, 1, -2, -1, 8, 9, 6, 7], [-1, 0, 7, 8], False)
    e2a = band(inner, every, True)
    e2b = band([-1, 0, 7, 8], every, True)
    vm = pl.BlockSpec(memory_space=VMEM)
    return pl.pallas_call(
        prepare_kernel,
        in_specs=[vm] * 9,
        out_specs=[vm] * 8,
        out_shape=[
            jax.ShapeDtypeStruct((2304, 256), BF16),
            jax.ShapeDtypeStruct((2304, 128), BF16),
            jax.ShapeDtypeStruct((2560, 256), BF16),
            jax.ShapeDtypeStruct((1152, 256), BF16),
            jax.ShapeDtypeStruct((32, 256), BF16),
            jax.ShapeDtypeStruct((1, 256), F32),
            jax.ShapeDtypeStruct((1, 128), F32),
            jax.ShapeDtypeStruct((1, 256), F32),
        ],
        compiler_params=params(16),
        cost_estimate=cost(2 * 300 * 128 * 6144, 5 * MIB),
        name="prepare",
    )(conv_first, conv_second, bias_first[None], bias_second[None], head, e1a, e1b, e2a, e2b)


def on_device(
    features,
    weights,
    owners,
    tile_ids,
    counts,
    conv_first,
    bias_first,
    conv_second,
    bias_second,
    head,
):
    particles = features.shape[1]

    def step(x, axis, by):
        size = lax.axis_size(axis)
        return lax.ppermute(
            x, axis, [(i, i + by) for i in range(size) if 0 <= i + by < size]
        )

    lo, mid, hi, slots = far_splat(features, weights, owners, tile_ids, counts)
    from_xlo = step(hi, "gx", 1)
    from_xhi = step(lo, "gx", -1)
    t1a, t1b, t2a, t2b, headx, b1a, b1b, b2 = prepare(
        conv_first, conv_second, bias_first, bias_second, head
    )
    own = own_splat(features, weights, tile_ids)
    to_hi = jnp.stack([from_xlo[2], mid[2], from_xhi[2]])
    to_lo = jnp.stack([from_xlo[0], mid[0], from_xhi[0]])
    from_ylo = step(to_hi, "gy", 1)
    from_yhi = step(to_lo, "gy", -1)
    g, ylo, yhi, ids = sum_tiles(own, from_ylo, from_yhi, from_xlo, from_xhi)

    rlo = step(yhi, "gy", 1)
    rhi = step(ylo, "gy", -1)
    x, slo, shi = widen_y(g, rlo, rhi)
    xlo = step(shi, "gx", 1)
    xhi = step(slo, "gx", -1)
    part = inner_convs(x, g, t1a, b1a, t2a, b2)
    grid_out, table, ans_ylo, ans_yhi, ans_x = edge_convs(
        x, xlo, xhi, part, t1b, b1b, t2b, headx, ids
    )

    back_yhi = step(ans_ylo, "gy", -1)
    back_ylo = step(ans_yhi, "gy", 1)
    near, far_w = own_read(tile_ids, table, weights, particles)
    to_lo = jnp.stack([back_ylo[0], ans_x[0], back_yhi[0]])
    to_hi = jnp.stack([back_ylo[2], ans_x[1], back_yhi[2]])
    back_xhi = step(to_lo, "gx", -1)
    back_xlo = step(to_hi, "gx", 1)
    velocity = far_read(slots, counts, back_xlo, back_xhi, back_ylo, back_yhi, far_w, near)
    return grid_out, velocity


def solution(mesh):
    in_specs = (
        P(None, ("gx", "gy")),
        P(("gx", "gy"), None),
        P(("gx", "gy")),
        P(("gx", "gy")),
        P(("gx", "gy")),
        P(),
        P(),
        P(),
        P(),
        P(),
    )
    out_specs = (P(None, None, "gx", "gy"), P(None, ("gx", "gy")))
    return jax.shard_map(
        on_device, mesh=mesh, in_specs=in_specs, out_specs=out_specs, check_vma=False
    )
```

```python
import jax
import jax.numpy as jnp
import numpy as np
from jax import lax
from jax.experimental import pallas as pl
from jax.experimental.pallas import tpu as pltpu
from jax.sharding import PartitionSpec as P

C = 32
SLAB = 16
BY = 128
SLOTS = 16
PAY = SLOTS * 32 + 16
ROWS = 144
STEP = 16
STEPS = 8
MIB = 1 << 20
F32 = jnp.float32
BF16 = jnp.bfloat16
VMEM = pltpu.VMEM
SMEM = pltpu.SMEM


def lanes_of(shape):
    return lax.broadcasted_iota(jnp.int32, shape, len(shape) - 1)


def params(limit, grid=False):
    if grid:
        return pltpu.CompilerParams(
            dimension_semantics=("arbitrary",), vmem_limit_bytes=limit * MIB
        )
    return pltpu.CompilerParams(vmem_limit_bytes=limit * MIB)


def cost(flops, nbytes):
    return pl.CostEstimate(flops=flops, bytes_accessed=nbytes, transcendentals=0)


def splat_four(f, w_ref, first):
    parts = []
    for j in (0, 2):
        at = (first + j) * 128
        fa = f[:, at : at + 128]
        fb = f[:, at + 128 : at + 256]
        none = jnp.zeros_like(fa)
        lhs = jnp.concatenate(
            [jnp.concatenate([fa, none], 1), jnp.concatenate([none, fb], 1)], 0
        )
        parts.append(jnp.dot(lhs, w_ref[at : at + 256, :], preferred_element_type=F32))
    a = jnp.concatenate(parts, 0).astype(BF16).T.astype(F32)
    a = a.reshape(4, 2, 2, 8, 128)
    lane = lanes_of((4, 2, 8, 128))
    v0, v1 = a[:, 0], a[:, 1]
    n0 = jnp.where(lane < 64, v0, pltpu.roll(v1, 64, 3))
    n1 = jnp.where(lane < 64, pltpu.roll(v0, 64, 3), v1)
    lane = lanes_of((4, 8, 128))
    tiles = []
    for n in (n0, n1):
        v0, v1 = n[:, 0], n[:, 1]
        tiles.append(jnp.where(lane % 64 < 32, v0, pltpu.roll(v1, 32, 2)))
        tiles.append(jnp.where(lane % 64 < 32, pltpu.roll(v0, 96, 2), v1))
    return tiles


def chunk_copies(f_hbm, w_hbm, fv, wv, sems, first):
    rows = STEP * 128
    pairs = []
    for c in range(STEPS):
        at = first * 128 + c * rows
        pairs.append(
            (
                pltpu.make_async_copy(
                    w_hbm.at[pl.ds(at, rows)], wv.at[pl.ds(c * rows, rows)], sems.at[c]
                ),
                pltpu.make_async_copy(f_hbm.at[:, pl.ds(at, rows)], fv.at[c], sems.at[STEPS + c]),
            )
        )
    return pairs


def far_splat_kernel(
    owners_h, ids_h, counts_h, f_hbm, w_hbm, lo, mid, hi, slots,
    fv, wv, tiles, idrows, filled, owners, ids, counts, sems, isems,
):
    ix = lax.axis_index("gx")
    iy = lax.axis_index("gy")
    copies = chunk_copies(f_hbm, w_hbm, fv, wv, sems, 128)
    small = [
        pltpu.make_async_copy(src, dst, isems.at[k])
        for k, (src, dst) in enumerate(((owners_h, owners), (ids_h, ids), (counts_h, counts)))
    ]
    for copy in small:
        copy.start()
    for pair in copies:
        for copy in pair:
            copy.start()
    tiles[...] = jnp.zeros_like(tiles)
    idrows[...] = jnp.zeros_like(idrows)
    for k in range(9):
        filled[k] = 0
    for copy in small:
        copy.wait()
    lane = lanes_of((1, 128))
    count = counts[0]
    for c, pair in enumerate(copies):
        for copy in pair:
            copy.wait()
        got = []
        for group in range(STEP // 4):
            got += splat_four(fv.at[c], wv.at[pl.ds(c * STEP * 128, STEP * 128)], group * 4)
        for j in range(STEP):
            block = c * STEP + j
            owner = owners[128 + block]
            live = 128 + block < count
            target = ((owner >> 3) - ix + 1) * 3 + (owner & 7) - iy + 1
            target = jnp.where(live, target, 4)
            rank = filled[target]
            filled[target] = jnp.where(live, rank + 1, 0)
            slot = target * SLOTS + rank
            slots[block] = slot
            tiles[slot] = got[j].reshape(32, 128).astype(BF16)
            row = idrows[pl.ds(target, 1), :]
            idrows[pl.ds(target, 1), :] = jnp.where(
                lane == rank, ids[128 + block].astype(F32), row
            )
    for dx, out in enumerate((lo, mid, hi)):
        for dy in range(3):
            k = dx * 3 + dy
            out[dy, 0 : SLOTS * 32, :] = tiles[k * SLOTS : (k + 1) * SLOTS].reshape(
                SLOTS * 32, 128
            )
            out[dy, SLOTS * 32 : PAY, :] = jnp.broadcast_to(
                idrows[k : k + 1, :], (16, 128)
            ).astype(BF16)


def far_splat(features, weights, owners, ids, counts):
    pay = jax.ShapeDtypeStruct((3, PAY, 128), BF16)
    vm = pl.BlockSpec(memory_space=VMEM)
    anywhere = pl.BlockSpec(memory_space=pl.ANY)
    return pl.pallas_call(
        far_splat_kernel,
        in_specs=[anywhere] * 5,
        out_specs=[vm, vm, vm, pl.BlockSpec(memory_space=SMEM)],
        out_shape=[pay, pay, pay, jax.ShapeDtypeStruct((128,), jnp.int32)],
        scratch_shapes=[
            VMEM((STEPS, C, STEP * 128), BF16),
            VMEM((STEPS * STEP * 128, 128), BF16),
            VMEM((9 * SLOTS, 32, 128), BF16),
            VMEM((16, 128), F32),
            SMEM((9,), jnp.int32),
            SMEM((256,), jnp.int32),
            SMEM((256,), jnp.int32),
            SMEM((1,), jnp.int32),
            pltpu.SemaphoreType.DMA((2 * STEPS,)),
            pltpu.SemaphoreType.DMA((3,)),
        ],
        compiler_params=params(56),
        cost_estimate=cost(2 * 128 * 32 * 128 * 128, 6 * MIB),
        name="far_splat",
    )(owners, ids, counts, features, weights)


def tile_place(tile):
    return (tile >> 5) * 4, (tile >> 4) & 1, pl.multiple_of((tile & 15) * 8, 8)


def own_splat_kernel(ids, f_hbm, w_hbm, out, fv, wv, grid, sems):
    copies = chunk_copies(f_hbm, w_hbm, fv, wv, sems, 0)
    for pair in copies:
        for copy in pair:
            copy.start()
    for c, pair in enumerate(copies):
        for copy in pair:
            copy.wait()
        got = []
        for group in range(STEP // 4):
            got += splat_four(fv.at[c], wv.at[pl.ds(c * STEP * 128, STEP * 128)], group * 4)
        for j in range(STEP):
            z, tx, y = tile_place(ids[c * STEP + j])
            grid[tx, pl.ds(z, 4), pl.ds(y, 8), :] = got[j]
    out[...] = grid[...].astype(BF16)


def own_splat(features, weights, ids):
    anywhere = pl.BlockSpec(memory_space=pl.ANY)
    return pl.pallas_call(
        own_splat_kernel,
        in_specs=[pl.BlockSpec(memory_space=SMEM), anywhere, anywhere],
        out_specs=pl.BlockSpec(memory_space=VMEM),
        out_shape=jax.ShapeDtypeStruct((2, SLAB, BY, 128), BF16),
        scratch_shapes=[
            VMEM((STEPS, C, STEP * 128), BF16),
            VMEM((STEPS * STEP * 128, 128), BF16),
            VMEM((2, SLAB, BY, 128), F32),
            pltpu.SemaphoreType.DMA((2 * STEPS,)),
        ],
        compiler_params=params(56),
        cost_estimate=cost(2 * 128 * 32 * 128 * 128, 6 * MIB),
        name="own_splat",
    )(ids, features, weights)


def sum_kernel(own, from_ylo, from_yhi, from_xlo, from_xhi, g, ylo, yhi, ids, grid, idv, sem):
    groups = [(from_ylo, 0), (from_ylo, 1), (from_ylo, 2)]
    groups += [(from_yhi, 0), (from_yhi, 1), (from_yhi, 2)]
    groups += [(from_xlo, 1), (from_xhi, 1)]
    rows = [ref[k, SLOTS * 32 : PAY, :].astype(F32)[0:1] for ref, k in groups]
    idv[...] = jnp.concatenate(rows, 0).astype(jnp.int32)
    copy = pltpu.make_async_copy(idv, ids, sem)
    copy.start()
    grid[...] = own[...].astype(F32)
    copy.wait()
    for n, (ref, k) in enumerate(groups):

        def add(j, carry, n=n, ref=ref, k=k):
            z, tx, y = tile_place(ids[n, j])
            tile = ref[k, pl.ds(pl.multiple_of(j * 32, 32), 32), :].astype(F32).reshape(4, 8, 128)
            grid[tx, pl.ds(z, 4), pl.ds(y, 8), :] += tile
            return carry

        lax.fori_loop(0, SLOTS, add, 0, unroll=4)
    g[...] = grid[...].astype(BF16)
    for tx in range(2):
        for r in range(2):
            ylo[tx * 2 + r] = grid[tx, :, r, :].astype(BF16)
            yhi[tx * 2 + r] = grid[tx, :, BY - 2 + r, :].astype(BF16)


def sum_tiles(own, from_ylo, from_yhi, from_xlo, from_xhi):
    vm = pl.BlockSpec(memory_space=VMEM)
    edge = jax.ShapeDtypeStruct((4, SLAB, 128), BF16)
    return pl.pallas_call(
        sum_kernel,
        in_specs=[vm] * 5,
        out_specs=[vm, vm, vm, pl.BlockSpec(memory_space=SMEM)],
        out_shape=[
            jax.ShapeDtypeStruct((2, SLAB, BY, 128), BF16),
            edge,
            edge,
            jax.ShapeDtypeStruct((8, 128), jnp.int32),
        ],
        scratch_shapes=[
            VMEM((2, SLAB, BY, 128), F32),
            VMEM((8, 128), jnp.int32),
            pltpu.SemaphoreType.DMA,
        ],
        compiler_params=params(16),
        cost_estimate=cost(1000, 4 * MIB),
        name="sum_tiles",
    )(own, from_ylo, from_yhi, from_xlo, from_xhi)


def widen_kernel(g, rlo, rhi, x, slo, shi, edge):
    edge[...] = jnp.zeros_like(edge)
    for tx in range(2):
        for r in range(2):
            edge[tx, 0, :, 6 + r, :] = rlo[tx * 2 + r].astype(F32)
            edge[tx, 1, :, r, :] = rhi[tx * 2 + r].astype(F32)
    lane = lanes_of((ROWS, 128))

    def plane(tx, z):
        return jnp.concatenate([edge[tx, 0, z], g[tx, z].astype(F32), edge[tx, 1, z]], 0)

    def pair(z, carry):
        a, b = plane(0, z), plane(0, z + 8)
        x[0, z] = a.astype(BF16)
        x[0, z + 8] = b.astype(BF16)
        slo[z] = jnp.where(lane < 64, a, pltpu.roll(b, 64, 1)).astype(BF16)
        a, b = plane(1, z), plane(1, z + 8)
        x[1, z] = a.astype(BF16)
        x[1, z + 8] = b.astype(BF16)
        shi[z] = jnp.where(lane < 64, pltpu.roll(a, 64, 1), b).astype(BF16)
        return carry

    lax.fori_loop(0, 8, pair, 0)


def widen_y(g, rlo, rhi):
    vm = pl.BlockSpec(memory_space=VMEM)
    side = jax.ShapeDtypeStruct((SLAB // 2, ROWS, 128), BF16)
    return pl.pallas_call(
        widen_kernel,
        in_specs=[vm] * 3,
        out_specs=[vm] * 3,
        out_shape=[jax.ShapeDtypeStruct((2, SLAB, ROWS, 128), BF16), side, side],
        scratch_shapes=[VMEM((2, 2, SLAB, 8, 128), F32)],
        compiler_params=params(8),
        cost_estimate=cost(1000, 3 * MIB),
        name="widen_y",
    )(g, rlo, rhi)


def rows_inside(shape, iy):
    row = lax.broadcasted_iota(jnp.int32, shape, 1)
    return ((row != 7) | (iy > 0)) & ((row != 136) | (iy < 7))


def shifted(v):
    return (pltpu.roll(v, 1, 1), v, pltpu.roll(v, ROWS - 1, 1))


PAIRS = SLAB // 2


def window(ref, n, k):
    m = n * 4 + k // 2
    out = []
    for dy in range(3):
        v = ref[dy, m : m + 4, k % 2]
        out.append(v.reshape(4 * v.shape[1], v.shape[2]))
    return out


def inner_kernel(x, g, t1, t1o, b1, t2, b2, part, pre, xs, hs):
    iy = lax.axis_index("gy")
    for dy in range(3):
        xs[dy, 0, 0] = jnp.zeros((ROWS, 256), BF16)
        xs[dy, PAIRS, 1] = jnp.zeros((ROWS, 256), BF16)
        hs[dy, 0, 0] = jnp.zeros((BY, 256), BF16)
        hs[dy, PAIRS, 1] = jnp.zeros((BY, 256), BF16)

    def shift(n, carry):
        for k in range(2):
            for tx in range(2):
                v = x[tx, pl.ds(2 * n + k, 1)].astype(F32)
                for dy, s in enumerate(shifted(v)):
                    xs[dy, pl.ds(n + k, 1), 1 - k, :, tx * 128 : tx * 128 + 128] = s.astype(BF16)
        return carry

    lax.fori_loop(0, PAIRS, shift, 0)
    for n in range(2):
        for zo in range(2):
            taps = window(xs, n, zo) + window(xs, n, zo + 1) + window(xs, n, zo + 2)
            acc = jnp.dot(jnp.concatenate(taps, 1), t1[...], preferred_element_type=F32) + b1[...]
            h = jax.nn.gelu(acc).reshape(4, ROWS, 256)
            h = jnp.where(rows_inside(h.shape, iy), h, 0.0)
            for dy, s in enumerate(shifted(h)):
                m = n * 4 + zo
                hs[dy, m : m + 4, 1 - zo] = s[:, 8 : 8 + BY].astype(BF16)
    for n in range(2):
        taps = sum([window(xs, n, zi) for zi in range(4)], [])
        acc = jnp.dot(jnp.concatenate(taps, 1), t1o[...], preferred_element_type=F32) + b1[...]
        pre[n] = acc
    for n in range(2):
        for zo in range(2):
            taps = window(hs, n, zo) + window(hs, n, zo + 1) + window(hs, n, zo + 2)
            taps += [g[tx, n * 4 : n * 4 + 4, zo].reshape(4 * BY, 128) for tx in range(2)]
            acc = jnp.dot(jnp.concatenate(taps, 1), t2[...], preferred_element_type=F32) + b2[...]
            part[n * 4 : n * 4 + 4, zo] = acc.reshape(4, BY, 256)


def inner_convs(x, g, t1, t1o, b1, t2, b2):
    vm = pl.BlockSpec(memory_space=VMEM)
    return pl.pallas_call(
        inner_kernel,
        in_specs=[vm] * 7,
        out_specs=[vm, vm],
        out_shape=[
            jax.ShapeDtypeStruct((PAIRS, 2, BY, 256), F32),
            jax.ShapeDtypeStruct((2, 4 * ROWS, 256), F32),
        ],
        scratch_shapes=[
            VMEM((3, PAIRS + 1, 2, ROWS, 256), BF16),
            VMEM((3, PAIRS + 1, 2, BY, 256), BF16),
        ],
        compiler_params=params(32),
        cost_estimate=cost(2 * 20 * 256 * 256 * 2304, 6 * MIB),
        name="inner_convs",
    )(x, g.reshape(2, PAIRS, 2, BY, 128), t1, t1o, b1, t2, b2)


def tile_row(tile):
    return ((tile >> 5) * 4 + ((tile >> 2) & 3)) * 8 + ((tile >> 4) & 1) * 4 + (tile & 3)


def edge_kernel(
    rlo, rhi, part, pre, t1, t2, headx, ids, total, table, ans_ylo, ans_yhi, ans_x, es, hs, vel
):
    ix = lax.axis_index("gx")
    iy = lax.axis_index("gy")
    for dy in range(3):
        es[dy, 0, 0] = jnp.zeros((ROWS, 128), BF16)
        es[dy, PAIRS, 1] = jnp.zeros((ROWS, 128), BF16)
        hs[dy, 0, 0] = jnp.zeros((BY, 128), BF16)
        hs[dy, PAIRS, 1] = jnp.zeros((BY, 128), BF16)
    lane = lanes_of((1, ROWS, 128))
    for z in range(8):
        a = rlo[z : z + 1].astype(F32)
        b = rhi[z : z + 1].astype(F32)
        near = jnp.where(lane < 64, a, pltpu.roll(b, 64, 2))
        far = jnp.where(lane < 64, pltpu.roll(a, 64, 2), b)
        for zz, v in ((z, near), (z + 8, far)):
            m = (zz + 1) // 2
            for dy, s in enumerate(shifted(v)):
                es[dy, m : m + 1, (zz + 1) % 2] = s.astype(BF16)
    for n in range(2):
        taps = sum([window(es, n, zi) for zi in range(4)], [])
        acc = jnp.dot(jnp.concatenate(taps, 1), t1[...], preferred_element_type=F32) + pre[n]
        h = jax.nn.gelu(acc).reshape(4, ROWS, 256)
        ln = lanes_of(h.shape) & 127
        keep = ((ln >= 32) | (ix > 0)) & ((ln < 96) | (ix < 15))
        h = jnp.where(rows_inside(h.shape, iy) & keep, h, 0.0)
        for dy, s in enumerate(shifted(h)):
            s = s[:, 8 : 8 + BY].astype(BF16)
            hs[dy, n * 4 : n * 4 + 4, 1] = s[:, :, 0:128]
            hs[dy, n * 4 + 1 : n * 4 + 5, 0] = s[:, :, 128:256]
    for n in range(2):
        for zo in range(2):
            taps = window(hs, n, zo) + window(hs, n, zo + 1) + window(hs, n, zo + 2)
            acc = jnp.dot(jnp.concatenate(taps, 1), t2[...], preferred_element_type=F32)
            acc = acc.reshape(4, BY, 256) + part[n * 4 : n * 4 + 4, zo]
            acc = acc.astype(BF16)
            total[n * 4 : n * 4 + 4, zo] = acc
            v = jnp.concatenate([acc[p] for p in range(4)], 1)
            v = jnp.dot(v, headx[...], preferred_element_type=F32).T
            for p in range(4):
                for a in range(3):
                    at = p * 32 + a * 8
                    vel[a, 2 * (n * 4 + p) + zo] = v[at : at + 8]

    table[...] = jnp.zeros_like(table)
    sub = lax.broadcasted_iota(jnp.int32, (4, 8, 128), 1)
    ln = lanes_of((4, 8, 128))
    for a in range(3):
        v = vel[a].reshape(4, 2, 2, 8, 128)
        v0, v1 = v[:, 0], v[:, 1]
        l2 = lanes_of(v0.shape)
        m0 = jnp.where(l2 < 64, v0, pltpu.roll(v1, 64, 3))
        m1 = jnp.where(l2 < 64, pltpu.roll(v0, 64, 3), v1)
        for k, m in enumerate((m0, m1)):
            v0, v1 = m[:, 0], m[:, 1]
            n0 = jnp.where(ln % 64 < 32, v0, pltpu.roll(v1, 32, 2))
            n1 = jnp.where(ln % 64 < 32, pltpu.roll(v0, 96, 2), v1)
            for kk, w in enumerate((n0, n1)):
                for bit, step in ((2, 16), (1, 8)):
                    up = pltpu.roll(pltpu.roll(w, 8 - bit, 1), step, 2)
                    down = pltpu.roll(pltpu.roll(w, bit, 1), 128 - step, 2)
                    s1 = (sub & bit) != 0
                    l1 = (ln & step) != 0
                    w = jnp.where(s1 == l1, w, jnp.where(l1, up, down))
                for tz in range(4):
                    row = (tz * 4 + k * 2 + kk) * 8
                    table[row : row + 8, a, :] = w[tz]

    places = [(ans_ylo, 0), (ans_ylo, 1), (ans_ylo, 2), (ans_yhi, 0), (ans_yhi, 1), (ans_yhi, 2)]
    places += [(ans_x, 0), (ans_x, 1)]
    for n, (ref, k) in enumerate(places):

        def answer(j, carry, n=n, ref=ref, k=k):
            halves = []
            for h in range(2):
                r0 = table[tile_row(ids[n, j * 4 + 2 * h])]
                r1 = table[tile_row(ids[n, j * 4 + 2 * h + 1])]
                halves.append(two_blocks(r0, r1))
            ref[k, pl.ds(pl.multiple_of(j * 16, 16), 16), :] = jnp.concatenate(halves, 0).astype(
                BF16
            )
            return carry

        lax.fori_loop(0, SLOTS // 4, answer, 0, unroll=4)


def edge_convs(rlo, rhi, part, pre, t1, t2, headx, ids):
    vm = pl.BlockSpec(memory_space=VMEM)
    ans = jax.ShapeDtypeStruct((3, 64, 128), BF16)
    return pl.pallas_call(
        edge_kernel,
        in_specs=[vm] * 7 + [pl.BlockSpec(memory_space=SMEM)],
        out_specs=[vm] * 5,
        out_shape=[
            jax.ShapeDtypeStruct((SLAB // 2, 2, BY, 256), BF16),
            jax.ShapeDtypeStruct((128, 8, 128), F32),
            ans,
            ans,
            jax.ShapeDtypeStruct((2, 64, 128), BF16),
        ],
        scratch_shapes=[
            VMEM((3, PAIRS + 1, 2, ROWS, 128), BF16),
            VMEM((3, PAIRS + 1, 2, BY, 128), BF16),
            VMEM((3, SLAB, 8, 128), F32),
        ],
        compiler_params=params(32),
        cost_estimate=cost(2 * 9 * 256 * 256 * 2304, 6 * MIB),
        name="edge_convs",
    )(rlo, rhi, part, pre, t1, t2, headx, ids)


def turn_kernel(total, out):
    for k in range(4):
        out[:, k] = total[k // 2, k % 2].T.reshape(32, 8, 128)


def turn(total):
    return pl.pallas_call(
        turn_kernel,
        grid=(4,),
        in_specs=[pl.BlockSpec((2, 2, BY, 256), lambda i: (i, 0, 0, 0))],
        out_specs=pl.BlockSpec((C, 4, 8, BY), lambda i: (0, i, 0, 0)),
        out_shape=jax.ShapeDtypeStruct((C, SLAB, 8, BY), BF16),
        compiler_params=params(8, True),
        cost_estimate=cost(1000, 8 * MIB),
        name="turn",
    )(total)


BATCH = 32


def read_batch(rows, w_ref, first, out, at, count):
    cells = rows.astype(BF16).T
    owner = lanes_of((128, 128)) >> 2
    right = jnp.concatenate(
        [jnp.where(owner == b, cells, jnp.zeros_like(cells)) for b in range(BATCH)], 0
    )
    left = jnp.concatenate(
        [w_ref[(first + b) * 128 : (first + b + 1) * 128, :] for b in range(BATCH)], 1
    )
    r = jnp.dot(left, right, preferred_element_type=F32).T
    for b in range(BATCH):
        v = r[4 * b : 4 * b + 3]
        if count is not None:
            v = jnp.where(128 + first + b < count, v, 0.0)
        out[:, at + b * 128 : at + (b + 1) * 128] = v


def two_blocks(r0, r1):
    row = lax.broadcasted_iota(jnp.int32, (8, 128), 0)
    return jnp.where(row < 4, r0, pltpu.roll(r1, 4, 0))


def weight_copies(w_hbm, wv, sems, first):
    n = 128 // BATCH
    rows = BATCH * 128
    return [
        pltpu.make_async_copy(
            w_hbm.at[pl.ds(first * 128 + k * rows, rows)], wv.at[pl.ds(k * rows, rows)], sems.at[k]
        )
        for k in range(n)
    ]


def own_read_kernel(ids, table, w_hbm, out, far_w, wv, sems, fsems):
    copies = weight_copies(w_hbm, wv, sems, 0)
    later = weight_copies(w_hbm, far_w, fsems, 128)
    for copy in copies + later:
        copy.start()
    for k, copy in enumerate(copies):
        rows = [
            two_blocks(
                table[tile_row(ids[k * BATCH + 2 * j])], table[tile_row(ids[k * BATCH + 2 * j + 1])]
            )
            for j in range(BATCH // 2)
        ]
        copy.wait()
        read_batch(jnp.concatenate(rows, 0), wv, k * BATCH, out, k * BATCH * 128, None)
    for copy in later:
        copy.wait()


def own_read(ids, table, weights, particles):
    vm = pl.BlockSpec(memory_space=VMEM)
    return pl.pallas_call(
        own_read_kernel,
        in_specs=[pl.BlockSpec(memory_space=SMEM), vm, pl.BlockSpec(memory_space=pl.ANY)],
        out_specs=[vm, vm],
        out_shape=[
            jax.ShapeDtypeStruct((3, particles // 2), F32),
            jax.ShapeDtypeStruct((particles // 2, 128), BF16),
        ],
        scratch_shapes=[
            VMEM((particles // 2, 128), BF16),
            pltpu.SemaphoreType.DMA((128 // BATCH,)),
            pltpu.SemaphoreType.DMA((128 // BATCH,)),
        ],
        compiler_params=params(48),
        cost_estimate=cost(2 * 128 * 32 * 128 * 128, 9 * MIB),
        name="own_read",
    )(ids, table, weights)


def far_read_kernel(slots, counts, blo, bhi, ylo, yhi, w, near, out, table):
    places = [(blo, 0), (blo, 1), (blo, 2), (ylo, 1), None, (yhi, 1)]
    places += [(bhi, 0), (bhi, 1), (bhi, 2)]
    for k, place in enumerate(places):
        if place is None:
            table[k * SLOTS : (k + 1) * SLOTS] = jnp.zeros((SLOTS, 8, 128), F32)
            continue
        v = place[0][place[1]].astype(F32).reshape(8, 8, 128)
        turned = pltpu.roll(v, 4, 1)
        for j in range(8):
            table[k * SLOTS + 2 * j] = v[j]
            table[k * SLOTS + 2 * j + 1] = turned[j]
    half = near.shape[1]
    out[:, 0:half] = near[...]
    for k in range(128 // BATCH):
        rows = [
            two_blocks(table[slots[k * BATCH + 2 * j]], table[slots[k * BATCH + 2 * j + 1]])
            for j in range(BATCH // 2)
        ]
        read_batch(
            jnp.concatenate(rows, 0), w, k * BATCH, out, half + k * BATCH * 128, counts[0]
        )


def far_read(slots, counts, blo, bhi, ylo, yhi, w, near):
    vm = pl.BlockSpec(memory_space=VMEM)
    smem = pl.BlockSpec(memory_space=SMEM)
    return pl.pallas_call(
        far_read_kernel,
        in_specs=[smem, smem] + [vm] * 6,
        out_specs=vm,
        out_shape=jax.ShapeDtypeStruct((3, 2 * near.shape[1]), F32),
        scratch_shapes=[VMEM((9 * SLOTS, 8, 128), F32)],
        compiler_params=params(24),
        cost_estimate=cost(2 * 128 * 32 * 128 * 128, 5 * MIB),
        name="far_read",
    )(slots, counts, blo, bhi, ylo, yhi, w, near)


def band(pin, pout, out_last):
    out = np.zeros((4, C, len(pin), len(pout), C), np.float32)
    for i, p in enumerate(pin):
        for j, q in enumerate(pout):
            if p is not None and q is not None and abs(p - q) <= 1:
                out[p - q + 1, np.arange(C), i, j, np.arange(C)] = 1
    if out_last:
        out = out.swapaxes(3, 4)
    return jnp.asarray(out.reshape(4 * C, -1), BF16)


def prepare_kernel(
    c1, c2, bias1, bias2, head, e1a, e1o, e1r, e2a, e2b, t1a, t1o, t1r, t2a, t2b, hx, b1, b2
):
    one = (
        lax.broadcasted_iota(jnp.int32, (C, C), 0) == lax.broadcasted_iota(jnp.int32, (C, C), 1)
    ).astype(BF16)
    nothing = jnp.zeros((C, C), BF16)
    for t in (t1o, t1r):
        third = t.shape[0] // 4
        t[0:third, 128:256] = jnp.zeros((third, 128), BF16)
        t[3 * third : 4 * third, 0:128] = jnp.zeros((third, 128), BF16)
    plans = (
        (c1, ((e1a, t1a, 256), (e1o, t1o, 128), (e1r, t1r, 128))),
        (c2, ((e2a, t2a, 256), (e2b, t2b, 256))),
    )
    for conv, made in plans:
        pieces = []
        for k in range(9):
            pieces += [conv[k // 3 * 9 + d * 3 + k % 3] for d in range(3)] + [nothing]
        turned = lax.dot_general(
            one, jnp.concatenate(pieces, 0), (((1,), (1,)), ((), ())), preferred_element_type=F32
        ).astype(BF16)
        lhs = jnp.concatenate([turned[:, 128 * k : 128 * k + 128] for k in range(9)], 0)
        for e, t, width in made:
            planes = e.shape[1] // width
            for p in range(planes):
                r = jnp.dot(lhs, e[:, p * width : (p + 1) * width], preferred_element_type=F32)
                r = r.astype(BF16)
                for k in range(9):
                    block = r[C * k : C * k + C]
                    at = (k * planes + p) * C
                    if width == 256:
                        t[at : at + C, :] = block
                        continue
                    for zo in range(2):
                        down = at + zo * 3 * planes * C
                        t[down : down + C, zo * 128 : zo * 128 + 128] = block
    row = lax.broadcasted_iota(jnp.int32, (256, 256), 0)
    col = lanes_of((256, 256))
    t2a[2304:2560, :] = ((row & 31) == (col >> 3)).astype(F32).astype(BF16) * (
        (row >> 5) == (col & 7)
    ).astype(F32).astype(BF16)
    spread = (
        lax.broadcasted_iota(jnp.int32, (C, 256), 0) == (lanes_of((C, 256)) >> 3)
    ).astype(F32)
    wide = jnp.dot(head[...], spread.astype(BF16), preferred_element_type=F32)
    keep = (lanes_of((8, 256)) & 7) == lax.broadcasted_iota(jnp.int32, (8, 256), 0)
    parts = [jnp.where(keep, jnp.broadcast_to(wide[a : a + 1], (8, 256)), 0.0) for a in range(3)]
    one_z = jnp.concatenate(parts + [jnp.zeros((8, 256), F32)], 0)
    turned = jnp.concatenate([one_z] * 4, 0).T
    group = lanes_of((256, 128)) >> 5
    for p in range(4):
        hx[p * 256 : p * 256 + 256, :] = jnp.where(group == p, turned, 0.0).astype(BF16)
    b1[...] = jnp.concatenate([bias1[...]] * 8, 1)
    b2[...] = jnp.dot(
        bias2[...], spread, preferred_element_type=F32, precision=lax.Precision.HIGHEST
    )


def prepare(conv_first, conv_second, bias_first, bias_second, head):
    none = None
    inner = [none, 1, 2, 3, 4, 5, 6, none]
    every = list(range(8))
    e1a = band(every, inner, False)
    e1o = band(every, [-1, 0, 7, 8], False)
    e1r = band([-2, -1, 8, 9], [-1, 0, 7, 8], False)
    e2a = band(inner, every, True)
    e2b = band([-1, 0, 7, 8], every, True)
    vm = pl.BlockSpec(memory_space=VMEM)
    return pl.pallas_call(
        prepare_kernel,
        in_specs=[vm] * 10,
        out_specs=[vm] * 8,
        out_shape=[
            jax.ShapeDtypeStruct((2304, 256), BF16),
            jax.ShapeDtypeStruct((3072, 256), BF16),
            jax.ShapeDtypeStruct((1536, 256), BF16),
            jax.ShapeDtypeStruct((2560, 256), BF16),
            jax.ShapeDtypeStruct((1152, 256), BF16),
            jax.ShapeDtypeStruct((1024, 128), BF16),
            jax.ShapeDtypeStruct((1, 256), F32),
            jax.ShapeDtypeStruct((1, 256), F32),
        ],
        compiler_params=params(16),
        cost_estimate=cost(2 * 300 * 128 * 6144, 5 * MIB),
        name="prepare",
    )(conv_first, conv_second, bias_first[None], bias_second[None], head, e1a, e1o, e1r, e2a, e2b)


def on_device(
    features,
    weights,
    owners,
    tile_ids,
    counts,
    conv_first,
    bias_first,
    conv_second,
    bias_second,
    head,
):
    particles = features.shape[1]

    def step(x, axis, by):
        size = lax.axis_size(axis)
        return lax.ppermute(
            x, axis, [(i, i + by) for i in range(size) if 0 <= i + by < size]
        )

    lo, mid, hi, slots = far_splat(features, weights, owners, tile_ids, counts)
    from_xlo = step(hi, "gx", 1)
    from_xhi = step(lo, "gx", -1)
    t1a, t1o, t1r, t2a, t2b, headx, b1, b2 = prepare(
        conv_first, conv_second, bias_first, bias_second, head
    )
    own = own_splat(features, weights, tile_ids)
    own, from_xlo, from_xhi, mid = lax.optimization_barrier((own, from_xlo, from_xhi, mid))
    to_hi = jnp.stack([from_xlo[2], mid[2], from_xhi[2]])
    to_lo = jnp.stack([from_xlo[0], mid[0], from_xhi[0]])
    from_ylo = step(to_hi, "gy", 1)
    from_yhi = step(to_lo, "gy", -1)
    g, ylo, yhi, ids = sum_tiles(own, from_ylo, from_yhi, from_xlo, from_xhi)

    rlo = step(yhi, "gy", 1)
    rhi = step(ylo, "gy", -1)
    x, slo, shi = widen_y(g, rlo, rhi)
    xlo = step(shi, "gx", 1)
    xhi = step(slo, "gx", -1)
    part, pre = inner_convs(x, g, t1a, t1o, b1, t2a, b2)
    total, table, ans_ylo, ans_yhi, ans_x = edge_convs(
        xlo, xhi, part, pre, t1r, t2b, headx, ids
    )

    back_yhi = step(ans_ylo, "gy", -1)
    back_ylo = step(ans_yhi, "gy", 1)
    grid_out = turn(total)
    grid_out, back_ylo, back_yhi = lax.optimization_barrier((grid_out, back_ylo, back_yhi))
    near, far_w = own_read(tile_ids, table, weights, particles)
    to_lo = jnp.stack([back_ylo[0], ans_x[0], back_yhi[0]])
    to_hi = jnp.stack([back_ylo[2], ans_x[1], back_yhi[2]])
    back_xhi = step(to_lo, "gx", -1)
    back_xlo = step(to_hi, "gx", 1)
    velocity = far_read(slots, counts, back_xlo, back_xhi, back_ylo, back_yhi, far_w, near)
    return grid_out, velocity


def solution(mesh):
    in_specs = (
        P(None, ("gx", "gy")),
        P(("gx", "gy"), None),
        P(("gx", "gy")),
        P(("gx", "gy")),
        P(("gx", "gy")),
        P(),
        P(),
        P(),
        P(),
        P(),
    )
    out_specs = (P(None, None, "gx", "gy"), P(None, ("gx", "gy")))
    return jax.shard_map(
        on_device, mesh=mesh, in_specs=in_specs, out_specs=out_specs, check_vma=False
    )
```

```python
import jax
import jax.numpy as jnp
import numpy as np
from jax import lax
from jax.experimental import pallas as pl
from jax.experimental.pallas import tpu as pltpu
from jax.sharding import PartitionSpec as P

C = 32
SLAB = 16
BY = 128
SLOTS = 16
PAY = SLOTS * 32 + 16
ROWS = 144
STEP = 16
STEPS = 8
MIB = 1 << 20
F32 = jnp.float32
BF16 = jnp.bfloat16
VMEM = pltpu.VMEM
SMEM = pltpu.SMEM


def lanes_of(shape):
    return lax.broadcasted_iota(jnp.int32, shape, len(shape) - 1)


def params(limit, grid=False):
    if grid:
        return pltpu.CompilerParams(
            dimension_semantics=("arbitrary",), vmem_limit_bytes=limit * MIB
        )
    return pltpu.CompilerParams(vmem_limit_bytes=limit * MIB)


def cost(flops, nbytes):
    return pl.CostEstimate(flops=flops, bytes_accessed=nbytes, transcendentals=0)


def splat_four(f, w_ref, first):
    parts = []
    for j in (0, 2):
        at = (first + j) * 128
        fa = f[:, at : at + 128]
        fb = f[:, at + 128 : at + 256]
        none = jnp.zeros_like(fa)
        lhs = jnp.concatenate(
            [jnp.concatenate([fa, none], 1), jnp.concatenate([none, fb], 1)], 0
        )
        parts.append(jnp.dot(lhs, w_ref[at : at + 256, :], preferred_element_type=F32))
    a = jnp.concatenate(parts, 0).astype(BF16).T.astype(F32)
    a = a.reshape(4, 2, 2, 8, 128)
    lane = lanes_of((4, 2, 8, 128))
    v0, v1 = a[:, 0], a[:, 1]
    n0 = jnp.where(lane < 64, v0, pltpu.roll(v1, 64, 3))
    n1 = jnp.where(lane < 64, pltpu.roll(v0, 64, 3), v1)
    lane = lanes_of((4, 8, 128))
    tiles = []
    for n in (n0, n1):
        v0, v1 = n[:, 0], n[:, 1]
        tiles.append(jnp.where(lane % 64 < 32, v0, pltpu.roll(v1, 32, 2)))
        tiles.append(jnp.where(lane % 64 < 32, pltpu.roll(v0, 96, 2), v1))
    return tiles


def chunk_copies(f_hbm, w_hbm, fv, wv, sems, first):
    rows = STEP * 128
    pairs = []
    for c in range(STEPS):
        at = first * 128 + c * rows
        pairs.append(
            (
                pltpu.make_async_copy(
                    w_hbm.at[pl.ds(at, rows)], wv.at[pl.ds(c * rows, rows)], sems.at[c]
                ),
                pltpu.make_async_copy(f_hbm.at[:, pl.ds(at, rows)], fv.at[c], sems.at[STEPS + c]),
            )
        )
    return pairs


def far_splat_kernel(
    owners_h, ids_h, counts_h, f_hbm, w_hbm, lo, mid, hi, slots,
    fv, wv, tiles, idrows, filled, owners, ids, counts, sems, isems,
):
    ix = lax.axis_index("gx")
    iy = lax.axis_index("gy")
    copies = chunk_copies(f_hbm, w_hbm, fv, wv, sems, 128)
    small = [
        pltpu.make_async_copy(src, dst, isems.at[k])
        for k, (src, dst) in enumerate(((owners_h, owners), (ids_h, ids), (counts_h, counts)))
    ]
    for copy in small:
        copy.start()
    for pair in copies:
        for copy in pair:
            copy.start()
    tiles[...] = jnp.zeros_like(tiles)
    idrows[...] = jnp.zeros_like(idrows)
    for k in range(9):
        filled[k] = 0
    for copy in small:
        copy.wait()
    lane = lanes_of((1, 128))
    count = counts[0]
    for c, pair in enumerate(copies):
        for copy in pair:
            copy.wait()
        got = []
        for group in range(STEP // 4):
            got += splat_four(fv.at[c], wv.at[pl.ds(c * STEP * 128, STEP * 128)], group * 4)
        for j in range(STEP):
            block = c * STEP + j
            owner = owners[128 + block]
            live = 128 + block < count
            target = ((owner >> 3) - ix + 1) * 3 + (owner & 7) - iy + 1
            target = jnp.where(live, target, 4)
            rank = filled[target]
            filled[target] = jnp.where(live, rank + 1, 0)
            slot = target * SLOTS + rank
            slots[block] = slot
            tiles[slot] = got[j].reshape(32, 128).astype(BF16)
            row = idrows[pl.ds(target, 1), :]
            idrows[pl.ds(target, 1), :] = jnp.where(
                lane == rank, ids[128 + block].astype(F32), row
            )
    for dx, out in enumerate((lo, mid, hi)):
        for dy in range(3):
            k = dx * 3 + dy
            out[dy, 0 : SLOTS * 32, :] = tiles[k * SLOTS : (k + 1) * SLOTS].reshape(
                SLOTS * 32, 128
            )
            out[dy, SLOTS * 32 : PAY, :] = jnp.broadcast_to(
                idrows[k : k + 1, :], (16, 128)
            ).astype(BF16)


def far_splat(features, weights, owners, ids, counts):
    pay = jax.ShapeDtypeStruct((3, PAY, 128), BF16)
    vm = pl.BlockSpec(memory_space=VMEM)
    anywhere = pl.BlockSpec(memory_space=pl.ANY)
    return pl.pallas_call(
        far_splat_kernel,
        in_specs=[anywhere] * 5,
        out_specs=[vm, vm, vm, pl.BlockSpec(memory_space=SMEM)],
        out_shape=[pay, pay, pay, jax.ShapeDtypeStruct((128,), jnp.int32)],
        scratch_shapes=[
            VMEM((STEPS, C, STEP * 128), BF16),
            VMEM((STEPS * STEP * 128, 128), BF16),
            VMEM((9 * SLOTS, 32, 128), BF16),
            VMEM((16, 128), F32),
            SMEM((9,), jnp.int32),
            SMEM((256,), jnp.int32),
            SMEM((256,), jnp.int32),
            SMEM((1,), jnp.int32),
            pltpu.SemaphoreType.DMA((2 * STEPS,)),
            pltpu.SemaphoreType.DMA((3,)),
        ],
        compiler_params=params(56),
        cost_estimate=cost(2 * 128 * 32 * 128 * 128, 6 * MIB),
        name="far_splat",
    )(owners, ids, counts, features, weights)


def tile_place(tile):
    return (tile >> 5) * 4, (tile >> 4) & 1, pl.multiple_of((tile & 15) * 8, 8)


def own_splat_kernel(ids, f_hbm, w_hbm, out, fv, wv, grid, sems):
    copies = chunk_copies(f_hbm, w_hbm, fv, wv, sems, 0)
    for pair in copies:
        for copy in pair:
            copy.start()
    for c, pair in enumerate(copies):
        for copy in pair:
            copy.wait()
        got = []
        for group in range(STEP // 4):
            got += splat_four(fv.at[c], wv.at[pl.ds(c * STEP * 128, STEP * 128)], group * 4)
        for j in range(STEP):
            z, tx, y = tile_place(ids[c * STEP + j])
            grid[tx, pl.ds(z, 4), pl.ds(y, 8), :] = got[j]
    out[...] = grid[...].astype(BF16)


def own_splat(features, weights, ids):
    anywhere = pl.BlockSpec(memory_space=pl.ANY)
    return pl.pallas_call(
        own_splat_kernel,
        in_specs=[pl.BlockSpec(memory_space=SMEM), anywhere, anywhere],
        out_specs=pl.BlockSpec(memory_space=VMEM),
        out_shape=jax.ShapeDtypeStruct((2, SLAB, BY, 128), BF16),
        scratch_shapes=[
            VMEM((STEPS, C, STEP * 128), BF16),
            VMEM((STEPS * STEP * 128, 128), BF16),
            VMEM((2, SLAB, BY, 128), F32),
            pltpu.SemaphoreType.DMA((2 * STEPS,)),
        ],
        compiler_params=params(56),
        cost_estimate=cost(2 * 128 * 32 * 128 * 128, 6 * MIB),
        name="own_splat",
    )(ids, features, weights)


BUNDLE = 3 * PAY + 64


def ids_of(groups):
    rows = [ref[at + SLOTS * 32 : at + PAY, :].astype(F32)[0:1] for ref, at in groups]
    return jnp.concatenate(rows, 0).astype(jnp.int32)


def tile_of(ref, at, j):
    rows = ref[pl.ds(pl.multiple_of(at + j * 32, 16), 32), :]
    return rows.astype(F32).reshape(4, 8, 128)


def add_tiles(grid, ids, n, ref, at):
    def add(j, carry):
        z, tx, y = tile_place(ids[n, j])
        grid[tx, pl.ds(z, 4), pl.ds(y, 8), :] += tile_of(ref, at, j)
        return carry

    lax.fori_loop(0, SLOTS, add, 0, unroll=4)


def column_kernel(
    own, xlo, xhi, mid, g, ids, to_lo, to_hi, fwd_lo, fwd_hi, keep_lo, keep_hi, acc, idv, sem
):
    zero, one, two = 0, PAY, 2 * PAY
    groups = [(xlo, one), (xhi, one)]
    groups += [(xlo, two), (mid, two), (xhi, two), (xlo, zero), (mid, zero), (xhi, zero)]
    idv[...] = ids_of(groups)
    copy = pltpu.make_async_copy(idv, ids, sem)
    copy.start()
    g[...] = own[...].astype(F32)
    acc[...] = jnp.zeros_like(acc)
    for n, (ref, at) in enumerate(groups[2:]):
        out, k = (to_hi, n) if n < 3 else (to_lo, n - 3)
        out[k * PAY : (k + 1) * PAY, :] = ref[at : at + PAY, :]
    copy.wait()
    for n, (ref, at) in enumerate(groups):
        if n < 2:
            add_tiles(g, ids, n, ref, at)
            continue

        def add(j, carry, n=n, ref=ref, at=at):
            tile = ids[n, j]
            ty = tile & 15
            place = jnp.where(ty == 0, 0, jnp.where(ty == 15, 1, 2)) + (0 if n < 5 else 3)
            acc[place, (tile >> 4) & 1, pl.ds((tile >> 5) * 4, 4)] += tile_of(ref, at, j)
            return carry

        lax.fori_loop(0, SLOTS, add, 0, unroll=4)
    for tx in range(2):
        for r in range(2):
            k = tx * 2 + r
            rows = slice(3 * PAY + k * 16, 3 * PAY + k * 16 + 16)
            to_lo[rows, :] = g[tx, :, r, :].astype(BF16)
            to_hi[rows, :] = g[tx, :, BY - 2 + r, :].astype(BF16)
            keep_hi[k] = acc[0, tx, :, r, :]
            fwd_hi[k] = acc[1, tx, :, 6 + r, :].astype(BF16)
            fwd_lo[k] = acc[3, tx, :, r, :].astype(BF16)
            keep_lo[k] = acc[4, tx, :, 6 + r, :]


def column(own, xlo, xhi, mid):
    vm = pl.BlockSpec(memory_space=VMEM)
    bundle = jax.ShapeDtypeStruct((BUNDLE, 128), BF16)
    flat = [v.reshape(3 * PAY, 128) for v in (xlo, xhi, mid)]
    return pl.pallas_call(
        column_kernel,
        in_specs=[vm] * 4,
        out_specs=[vm, pl.BlockSpec(memory_space=SMEM)] + [vm] * 6,
        out_shape=[
            jax.ShapeDtypeStruct((2, SLAB, BY, 128), F32),
            jax.ShapeDtypeStruct((8, 128), jnp.int32),
            bundle,
            bundle,
            jax.ShapeDtypeStruct((4, SLAB, 128), BF16),
            jax.ShapeDtypeStruct((4, SLAB, 128), BF16),
            jax.ShapeDtypeStruct((4, SLAB, 128), F32),
            jax.ShapeDtypeStruct((4, SLAB, 128), F32),
        ],
        scratch_shapes=[
            VMEM((6, 2, SLAB, 8, 128), F32),
            VMEM((8, 128), jnp.int32),
            pltpu.SemaphoreType.DMA,
        ],
        compiler_params=params(16),
        cost_estimate=cost(1000, 4 * MIB),
        name="column",
    )(own, *flat)


def sum_kernel(
    part, ylo, yhi, far_lo, far_hi, keep_lo, keep_hi, g, x, slo, shi, ids, grid, edge, idv, sem
):
    groups = [(ref, k * PAY) for ref in (ylo, yhi) for k in range(3)]
    idv[0:6, :] = ids_of(groups)
    idv[6:8, :] = jnp.zeros((2, 128), jnp.int32)
    copy = pltpu.make_async_copy(idv, ids, sem)
    copy.start()
    grid[...] = part[...]
    edge[...] = jnp.zeros_like(edge)
    for tx in range(2):
        for r in range(2):
            k = tx * 2 + r
            rows = slice(3 * PAY + k * 16, 3 * PAY + k * 16 + 16)
            low = ylo[rows, :].astype(F32) + far_lo[k].astype(F32) + keep_lo[k]
            high = yhi[rows, :].astype(F32) + far_hi[k].astype(F32) + keep_hi[k]
            edge[tx, 0, :, 6 + r, :] = low
            edge[tx, 1, :, r, :] = high
    copy.wait()
    for n, (ref, at) in enumerate(groups):
        add_tiles(grid, ids, n, ref, at)
    lane = lanes_of((ROWS, 128))

    def plane(tx, z):
        return jnp.concatenate([edge[tx, 0, z], grid[tx, z], edge[tx, 1, z]], 0)

    def pair(z, carry):
        for tx, ref in enumerate((slo, shi)):
            a, b = plane(tx, z), plane(tx, z + 8)
            x[tx, z] = a.astype(BF16)
            x[tx, z + 8] = b.astype(BF16)
            g[tx, z] = a[8 : 8 + BY].astype(BF16)
            g[tx, z + 8] = b[8 : 8 + BY].astype(BF16)
            if tx == 0:
                ref[z] = jnp.where(lane < 64, a, pltpu.roll(b, 64, 1)).astype(BF16)
            else:
                ref[z] = jnp.where(lane < 64, pltpu.roll(a, 64, 1), b).astype(BF16)
        return carry

    lax.fori_loop(0, 8, pair, 0, unroll=2)


def sum_tiles(part, ylo, yhi, far_lo, far_hi, keep_lo, keep_hi):
    vm = pl.BlockSpec(memory_space=VMEM)
    side = jax.ShapeDtypeStruct((SLAB // 2, ROWS, 128), BF16)
    return pl.pallas_call(
        sum_kernel,
        in_specs=[vm] * 7,
        out_specs=[vm] * 4 + [pl.BlockSpec(memory_space=SMEM)],
        out_shape=[
            jax.ShapeDtypeStruct((2, SLAB, BY, 128), BF16),
            jax.ShapeDtypeStruct((2, SLAB, ROWS, 128), BF16),
            side,
            side,
            jax.ShapeDtypeStruct((8, 128), jnp.int32),
        ],
        scratch_shapes=[
            VMEM((2, SLAB, BY, 128), F32),
            VMEM((2, 2, SLAB, 8, 128), F32),
            VMEM((8, 128), jnp.int32),
            pltpu.SemaphoreType.DMA,
        ],
        compiler_params=params(16),
        cost_estimate=cost(1000, 4 * MIB),
        name="sum_tiles",
    )(part, ylo, yhi, far_lo, far_hi, keep_lo, keep_hi)


def rows_inside(shape, iy):
    row = lax.broadcasted_iota(jnp.int32, shape, 1)
    return ((row != 7) | (iy > 0)) & ((row != 136) | (iy < 7))


def shifted(v):
    return (pltpu.roll(v, 1, 1), v, pltpu.roll(v, ROWS - 1, 1))


PAIRS = SLAB // 2


def window(ref, n, k):
    m = n * 4 + k // 2
    out = []
    for dy in range(3):
        v = ref[dy, m : m + 4, k % 2]
        out.append(v.reshape(4 * v.shape[1], v.shape[2]))
    return out


def inner_kernel(x, g, t1, t1o, b1, t2, b2, part, pre, xs, hs):
    iy = lax.axis_index("gy")
    for dy in range(3):
        xs[dy, 0, 0] = jnp.zeros((ROWS, 256), BF16)
        xs[dy, PAIRS, 1] = jnp.zeros((ROWS, 256), BF16)
        hs[dy, 0, 0] = jnp.zeros((BY, 256), BF16)
        hs[dy, PAIRS, 1] = jnp.zeros((BY, 256), BF16)

    def shift(n, carry):
        for k in range(2):
            for tx in range(2):
                v = x[tx, pl.ds(2 * n + k, 1)].astype(F32)
                for dy, s in enumerate(shifted(v)):
                    xs[dy, pl.ds(n + k, 1), 1 - k, :, tx * 128 : tx * 128 + 128] = s.astype(BF16)
        return carry

    lax.fori_loop(0, PAIRS, shift, 0)
    for n in range(2):
        for zo in range(2):
            taps = window(xs, n, zo) + window(xs, n, zo + 1) + window(xs, n, zo + 2)
            acc = jnp.dot(jnp.concatenate(taps, 1), t1[...], preferred_element_type=F32) + b1[...]
            h = jax.nn.gelu(acc).reshape(4, ROWS, 256)
            h = jnp.where(rows_inside(h.shape, iy), h, 0.0)
            for dy, s in enumerate(shifted(h)):
                m = n * 4 + zo
                hs[dy, m : m + 4, 1 - zo] = s[:, 8 : 8 + BY].astype(BF16)
    for n in range(2):
        taps = sum([window(xs, n, zi) for zi in range(4)], [])
        acc = jnp.dot(jnp.concatenate(taps, 1), t1o[...], preferred_element_type=F32) + b1[...]
        pre[n] = acc
    for n in range(2):
        for zo in range(2):
            taps = window(hs, n, zo) + window(hs, n, zo + 1) + window(hs, n, zo + 2)
            taps += [g[tx, n * 4 : n * 4 + 4, zo].reshape(4 * BY, 128) for tx in range(2)]
            acc = jnp.dot(jnp.concatenate(taps, 1), t2[...], preferred_element_type=F32) + b2[...]
            part[n * 4 : n * 4 + 4, zo] = acc.reshape(4, BY, 256)


def inner_convs(x, g, t1, t1o, b1, t2, b2):
    vm = pl.BlockSpec(memory_space=VMEM)
    return pl.pallas_call(
        inner_kernel,
        in_specs=[vm] * 7,
        out_specs=[vm, vm],
        out_shape=[
            jax.ShapeDtypeStruct((PAIRS, 2, BY, 256), F32),
            jax.ShapeDtypeStruct((2, 4 * ROWS, 256), F32),
        ],
        scratch_shapes=[
            VMEM((3, PAIRS + 1, 2, ROWS, 256), BF16),
            VMEM((3, PAIRS + 1, 2, BY, 256), BF16),
        ],
        compiler_params=params(32),
        cost_estimate=cost(2 * 20 * 256 * 256 * 2304, 6 * MIB),
        name="inner_convs",
    )(x, g.reshape(2, PAIRS, 2, BY, 128), t1, t1o, b1, t2, b2)


def tile_row(tile):
    return ((tile >> 5) * 4 + ((tile >> 2) & 3)) * 8 + ((tile >> 4) & 1) * 4 + (tile & 3)


def edge_kernel(
    rlo, rhi, part, pre, t1, t2, headx, ids, idx, total, table, ans_ylo, ans_yhi, ans_x, es, hs, vel
):
    ix = lax.axis_index("gx")
    iy = lax.axis_index("gy")
    for dy in range(3):
        es[dy, 0, 0] = jnp.zeros((ROWS, 128), BF16)
        es[dy, PAIRS, 1] = jnp.zeros((ROWS, 128), BF16)
        hs[dy, 0, 0] = jnp.zeros((BY, 128), BF16)
        hs[dy, PAIRS, 1] = jnp.zeros((BY, 128), BF16)
    lane = lanes_of((1, ROWS, 128))
    for z in range(8):
        a = rlo[z : z + 1].astype(F32)
        b = rhi[z : z + 1].astype(F32)
        near = jnp.where(lane < 64, a, pltpu.roll(b, 64, 2))
        far = jnp.where(lane < 64, pltpu.roll(a, 64, 2), b)
        for zz, v in ((z, near), (z + 8, far)):
            m = (zz + 1) // 2
            for dy, s in enumerate(shifted(v)):
                es[dy, m : m + 1, (zz + 1) % 2] = s.astype(BF16)
    for n in range(2):
        taps = sum([window(es, n, zi) for zi in range(4)], [])
        acc = jnp.dot(jnp.concatenate(taps, 1), t1[...], preferred_element_type=F32) + pre[n]
        h = jax.nn.gelu(acc).reshape(4, ROWS, 256)
        ln = lanes_of(h.shape) & 127
        keep = ((ln >= 32) | (ix > 0)) & ((ln < 96) | (ix < 15))
        h = jnp.where(rows_inside(h.shape, iy) & keep, h, 0.0)
        for dy, s in enumerate(shifted(h)):
            s = s[:, 8 : 8 + BY].astype(BF16)
            hs[dy, n * 4 : n * 4 + 4, 1] = s[:, :, 0:128]
            hs[dy, n * 4 + 1 : n * 4 + 5, 0] = s[:, :, 128:256]
    for n in range(2):
        for zo in range(2):
            taps = window(hs, n, zo) + window(hs, n, zo + 1) + window(hs, n, zo + 2)
            acc = jnp.dot(jnp.concatenate(taps, 1), t2[...], preferred_element_type=F32)
            acc = acc.reshape(4, BY, 256) + part[n * 4 : n * 4 + 4, zo]
            acc = acc.astype(BF16)
            total[n * 4 : n * 4 + 4, zo] = acc
            v = jnp.concatenate([acc[p] for p in range(4)], 1)
            v = jnp.dot(v, headx[...], preferred_element_type=F32).T
            for p in range(4):
                for a in range(3):
                    at = p * 32 + a * 8
                    vel[a, 2 * (n * 4 + p) + zo] = v[at : at + 8]

    table[...] = jnp.zeros_like(table)
    sub = lax.broadcasted_iota(jnp.int32, (4, 8, 128), 1)
    ln = lanes_of((4, 8, 128))
    for a in range(3):
        v = vel[a].reshape(4, 2, 2, 8, 128)
        v0, v1 = v[:, 0], v[:, 1]
        l2 = lanes_of(v0.shape)
        m0 = jnp.where(l2 < 64, v0, pltpu.roll(v1, 64, 3))
        m1 = jnp.where(l2 < 64, pltpu.roll(v0, 64, 3), v1)
        for k, m in enumerate((m0, m1)):
            v0, v1 = m[:, 0], m[:, 1]
            n0 = jnp.where(ln % 64 < 32, v0, pltpu.roll(v1, 32, 2))
            n1 = jnp.where(ln % 64 < 32, pltpu.roll(v0, 96, 2), v1)
            for kk, w in enumerate((n0, n1)):
                for bit, step in ((2, 16), (1, 8)):
                    up = pltpu.roll(pltpu.roll(w, 8 - bit, 1), step, 2)
                    down = pltpu.roll(pltpu.roll(w, bit, 1), 128 - step, 2)
                    s1 = (sub & bit) != 0
                    l1 = (ln & step) != 0
                    w = jnp.where(s1 == l1, w, jnp.where(l1, up, down))
                for tz in range(4):
                    row = (tz * 4 + k * 2 + kk) * 8
                    table[row : row + 8, a, :] = w[tz]

    places = [(ans_ylo, 0), (ans_ylo, 1), (ans_ylo, 2), (ans_yhi, 0), (ans_yhi, 1), (ans_yhi, 2)]
    places += [(ans_x, 0), (ans_x, 1)]
    for n, (ref, k) in enumerate(places):
        source, row = (ids, n) if n < 6 else (idx, n - 6)

        def answer(j, carry, source=source, row=row, ref=ref, k=k):
            halves = []
            for h in range(2):
                r0 = table[tile_row(source[row, j * 4 + 2 * h])]
                r1 = table[tile_row(source[row, j * 4 + 2 * h + 1])]
                halves.append(two_blocks(r0, r1))
            ref[k, pl.ds(pl.multiple_of(j * 16, 16), 16), :] = jnp.concatenate(halves, 0).astype(
                BF16
            )
            return carry

        lax.fori_loop(0, SLOTS // 4, answer, 0, unroll=4)


def edge_convs(rlo, rhi, part, pre, t1, t2, headx, ids, idx):
    vm = pl.BlockSpec(memory_space=VMEM)
    ans = jax.ShapeDtypeStruct((3, 64, 128), BF16)
    return pl.pallas_call(
        edge_kernel,
        in_specs=[vm] * 7 + [pl.BlockSpec(memory_space=SMEM)] * 2,
        out_specs=[vm] * 5,
        out_shape=[
            jax.ShapeDtypeStruct((SLAB // 2, 2, BY, 256), BF16),
            jax.ShapeDtypeStruct((128, 8, 128), F32),
            ans,
            ans,
            jax.ShapeDtypeStruct((2, 64, 128), BF16),
        ],
        scratch_shapes=[
            VMEM((3, PAIRS + 1, 2, ROWS, 128), BF16),
            VMEM((3, PAIRS + 1, 2, BY, 128), BF16),
            VMEM((3, SLAB, 8, 128), F32),
        ],
        compiler_params=params(32),
        cost_estimate=cost(2 * 9 * 256 * 256 * 2304, 6 * MIB),
        name="edge_convs",
    )(rlo, rhi, part, pre, t1, t2, headx, ids, idx)


def turn_kernel(total, out):
    for k in range(4):
        out[:, k] = total[k // 2, k % 2].T.reshape(32, 8, 128)


def turn(total):
    return pl.pallas_call(
        turn_kernel,
        grid=(4,),
        in_specs=[pl.BlockSpec((2, 2, BY, 256), lambda i: (i, 0, 0, 0))],
        out_specs=pl.BlockSpec((C, 4, 8, BY), lambda i: (0, i, 0, 0)),
        out_shape=jax.ShapeDtypeStruct((C, SLAB, 8, BY), BF16),
        compiler_params=params(8, True),
        cost_estimate=cost(1000, 8 * MIB),
        name="turn",
    )(total)


BATCH = 32


def read_batch(rows, w_ref, first, out, at, count):
    cells = rows.astype(BF16).T
    owner = lanes_of((128, 128)) >> 2
    right = jnp.concatenate(
        [jnp.where(owner == b, cells, jnp.zeros_like(cells)) for b in range(BATCH)], 0
    )
    left = jnp.concatenate(
        [w_ref[(first + b) * 128 : (first + b + 1) * 128, :] for b in range(BATCH)], 1
    )
    r = jnp.dot(left, right, preferred_element_type=F32).T
    for b in range(BATCH):
        v = r[4 * b : 4 * b + 3]
        if count is not None:
            v = jnp.where(128 + first + b < count, v, 0.0)
        out[:, at + b * 128 : at + (b + 1) * 128] = v


def two_blocks(r0, r1):
    row = lax.broadcasted_iota(jnp.int32, (8, 128), 0)
    return jnp.where(row < 4, r0, pltpu.roll(r1, 4, 0))


def weight_copies(w_hbm, wv, sems, first):
    n = 128 // BATCH
    rows = BATCH * 128
    return [
        pltpu.make_async_copy(
            w_hbm.at[pl.ds(first * 128 + k * rows, rows)], wv.at[pl.ds(k * rows, rows)], sems.at[k]
        )
        for k in range(n)
    ]


def own_read_kernel(ids, table, w_hbm, out, far_w, wv, sems, fsems):
    copies = weight_copies(w_hbm, wv, sems, 0)
    later = weight_copies(w_hbm, far_w, fsems, 128)
    for copy in copies + later:
        copy.start()
    for k, copy in enumerate(copies):
        rows = [
            two_blocks(
                table[tile_row(ids[k * BATCH + 2 * j])], table[tile_row(ids[k * BATCH + 2 * j + 1])]
            )
            for j in range(BATCH // 2)
        ]
        copy.wait()
        read_batch(jnp.concatenate(rows, 0), wv, k * BATCH, out, k * BATCH * 128, None)
    for copy in later:
        copy.wait()


def own_read(ids, table, weights, particles):
    vm = pl.BlockSpec(memory_space=VMEM)
    return pl.pallas_call(
        own_read_kernel,
        in_specs=[pl.BlockSpec(memory_space=SMEM), vm, pl.BlockSpec(memory_space=pl.ANY)],
        out_specs=[vm, vm],
        out_shape=[
            jax.ShapeDtypeStruct((3, particles // 2), F32),
            jax.ShapeDtypeStruct((particles // 2, 128), BF16),
        ],
        scratch_shapes=[
            VMEM((particles // 2, 128), BF16),
            pltpu.SemaphoreType.DMA((128 // BATCH,)),
            pltpu.SemaphoreType.DMA((128 // BATCH,)),
        ],
        compiler_params=params(48),
        cost_estimate=cost(2 * 128 * 32 * 128 * 128, 9 * MIB),
        name="own_read",
    )(ids, table, weights)


def far_read_kernel(slots, counts, blo, bhi, ylo, yhi, w, near, out, table):
    places = [(blo, 0), (blo, 1), (blo, 2), (ylo, 1), None, (yhi, 1)]
    places += [(bhi, 0), (bhi, 1), (bhi, 2)]
    for k, place in enumerate(places):
        if place is None:
            table[k * SLOTS : (k + 1) * SLOTS] = jnp.zeros((SLOTS, 8, 128), F32)
            continue
        v = place[0][place[1]].astype(F32).reshape(8, 8, 128)
        turned = pltpu.roll(v, 4, 1)
        for j in range(8):
            table[k * SLOTS + 2 * j] = v[j]
            table[k * SLOTS + 2 * j + 1] = turned[j]
    half = near.shape[1]
    out[:, 0:half] = near[...]
    for k in range(128 // BATCH):
        rows = [
            two_blocks(table[slots[k * BATCH + 2 * j]], table[slots[k * BATCH + 2 * j + 1]])
            for j in range(BATCH // 2)
        ]
        read_batch(
            jnp.concatenate(rows, 0), w, k * BATCH, out, half + k * BATCH * 128, counts[0]
        )


def far_read(slots, counts, blo, bhi, ylo, yhi, w, near):
    vm = pl.BlockSpec(memory_space=VMEM)
    smem = pl.BlockSpec(memory_space=SMEM)
    return pl.pallas_call(
        far_read_kernel,
        in_specs=[smem, smem] + [vm] * 6,
        out_specs=vm,
        out_shape=jax.ShapeDtypeStruct((3, 2 * near.shape[1]), F32),
        scratch_shapes=[VMEM((9 * SLOTS, 8, 128), F32)],
        compiler_params=params(24),
        cost_estimate=cost(2 * 128 * 32 * 128 * 128, 5 * MIB),
        name="far_read",
    )(slots, counts, blo, bhi, ylo, yhi, w, near)


def band(pin, pout, out_last):
    out = np.zeros((4, C, len(pin), len(pout), C), np.float32)
    for i, p in enumerate(pin):
        for j, q in enumerate(pout):
            if p is not None and q is not None and abs(p - q) <= 1:
                out[p - q + 1, np.arange(C), i, j, np.arange(C)] = 1
    if out_last:
        out = out.swapaxes(3, 4)
    return jnp.asarray(out.reshape(4 * C, -1), BF16)


def prepare_kernel(
    c1, c2, bias1, bias2, head, e1a, e1o, e1r, e2a, e2b, t1a, t1o, t1r, t2a, t2b, hx, b1, b2
):
    one = (
        lax.broadcasted_iota(jnp.int32, (C, C), 0) == lax.broadcasted_iota(jnp.int32, (C, C), 1)
    ).astype(BF16)
    nothing = jnp.zeros((C, C), BF16)
    for t in (t1o, t1r):
        third = t.shape[0] // 4
        t[0:third, 128:256] = jnp.zeros((third, 128), BF16)
        t[3 * third : 4 * third, 0:128] = jnp.zeros((third, 128), BF16)
    plans = (
        (c1, ((e1a, t1a, 256), (e1o, t1o, 128), (e1r, t1r, 128))),
        (c2, ((e2a, t2a, 256), (e2b, t2b, 256))),
    )
    for conv, made in plans:
        pieces = []
        for k in range(9):
            pieces += [conv[k // 3 * 9 + d * 3 + k % 3] for d in range(3)] + [nothing]
        turned = lax.dot_general(
            one, jnp.concatenate(pieces, 0), (((1,), (1,)), ((), ())), preferred_element_type=F32
        ).astype(BF16)
        lhs = jnp.concatenate([turned[:, 128 * k : 128 * k + 128] for k in range(9)], 0)
        for e, t, width in made:
            planes = e.shape[1] // width
            for p in range(planes):
                r = jnp.dot(lhs, e[:, p * width : (p + 1) * width], preferred_element_type=F32)
                r = r.astype(BF16)
                for k in range(9):
                    block = r[C * k : C * k + C]
                    at = (k * planes + p) * C
                    if width == 256:
                        t[at : at + C, :] = block
                        continue
                    for zo in range(2):
                        down = at + zo * 3 * planes * C
                        t[down : down + C, zo * 128 : zo * 128 + 128] = block
    row = lax.broadcasted_iota(jnp.int32, (256, 256), 0)
    col = lanes_of((256, 256))
    t2a[2304:2560, :] = ((row & 31) == (col >> 3)).astype(F32).astype(BF16) * (
        (row >> 5) == (col & 7)
    ).astype(F32).astype(BF16)
    spread = (
        lax.broadcasted_iota(jnp.int32, (C, 256), 0) == (lanes_of((C, 256)) >> 3)
    ).astype(F32)
    wide = jnp.dot(head[...], spread.astype(BF16), preferred_element_type=F32)
    keep = (lanes_of((8, 256)) & 7) == lax.broadcasted_iota(jnp.int32, (8, 256), 0)
    parts = [jnp.where(keep, jnp.broadcast_to(wide[a : a + 1], (8, 256)), 0.0) for a in range(3)]
    one_z = jnp.concatenate(parts + [jnp.zeros((8, 256), F32)], 0)
    turned = jnp.concatenate([one_z] * 4, 0).T
    group = lanes_of((256, 128)) >> 5
    for p in range(4):
        hx[p * 256 : p * 256 + 256, :] = jnp.where(group == p, turned, 0.0).astype(BF16)
    b1[...] = jnp.concatenate([bias1[...]] * 8, 1)
    b2[...] = jnp.dot(
        bias2[...], spread, preferred_element_type=F32, precision=lax.Precision.HIGHEST
    )


def prepare(conv_first, conv_second, bias_first, bias_second, head):
    none = None
    inner = [none, 1, 2, 3, 4, 5, 6, none]
    every = list(range(8))
    e1a = band(every, inner, False)
    e1o = band(every, [-1, 0, 7, 8], False)
    e1r = band([-2, -1, 8, 9], [-1, 0, 7, 8], False)
    e2a = band(inner, every, True)
    e2b = band([-1, 0, 7, 8], every, True)
    vm = pl.BlockSpec(memory_space=VMEM)
    return pl.pallas_call(
        prepare_kernel,
        in_specs=[vm] * 10,
        out_specs=[vm] * 8,
        out_shape=[
            jax.ShapeDtypeStruct((2304, 256), BF16),
            jax.ShapeDtypeStruct((3072, 256), BF16),
            jax.ShapeDtypeStruct((1536, 256), BF16),
            jax.ShapeDtypeStruct((2560, 256), BF16),
            jax.ShapeDtypeStruct((1152, 256), BF16),
            jax.ShapeDtypeStruct((1024, 128), BF16),
            jax.ShapeDtypeStruct((1, 256), F32),
            jax.ShapeDtypeStruct((1, 256), F32),
        ],
        compiler_params=params(16),
        cost_estimate=cost(2 * 300 * 128 * 6144, 5 * MIB),
        name="prepare",
    )(conv_first, conv_second, bias_first[None], bias_second[None], head, e1a, e1o, e1r, e2a, e2b)


def on_device(
    features,
    weights,
    owners,
    tile_ids,
    counts,
    conv_first,
    bias_first,
    conv_second,
    bias_second,
    head,
):
    particles = features.shape[1]

    def step(x, axis, by):
        size = lax.axis_size(axis)
        return lax.ppermute(
            x, axis, [(i, i + by) for i in range(size) if 0 <= i + by < size]
        )

    lo, mid, hi, slots = far_splat(features, weights, owners, tile_ids, counts)
    from_xlo = step(hi, "gx", 1)
    from_xhi = step(lo, "gx", -1)
    t1a, t1o, t1r, t2a, t2b, headx, b1, b2 = prepare(
        conv_first, conv_second, bias_first, bias_second, head
    )
    own = own_splat(features, weights, tile_ids)
    made = (t1a, t1o, t1r, t2a, t2b, headx, b1, b2)
    own, made, from_xlo, from_xhi = lax.optimization_barrier((own, made, from_xlo, from_xhi))
    t1a, t1o, t1r, t2a, t2b, headx, b1, b2 = made

    g, idx, to_lo, to_hi, fwd_lo, fwd_hi, keep_lo, keep_hi = column(own, from_xlo, from_xhi, mid)
    from_ylo = step(to_hi, "gy", 1)
    from_yhi = step(to_lo, "gy", -1)
    far_lo = step(fwd_hi, "gy", 2)
    far_hi = step(fwd_lo, "gy", -2)
    g, x, slo, shi, ids = sum_tiles(g, from_ylo, from_yhi, far_lo, far_hi, keep_lo, keep_hi)

    xlo = step(shi, "gx", 1)
    xhi = step(slo, "gx", -1)
    part, pre = inner_convs(x, g, t1a, t1o, b1, t2a, b2)
    total, table, ans_ylo, ans_yhi, ans_x = edge_convs(
        xlo, xhi, part, pre, t1r, t2b, headx, ids, idx
    )

    back_yhi = step(ans_ylo, "gy", -1)
    back_ylo = step(ans_yhi, "gy", 1)
    grid_out = turn(total)
    grid_out, back_ylo, back_yhi = lax.optimization_barrier((grid_out, back_ylo, back_yhi))
    near, far_w = own_read(tile_ids, table, weights, particles)
    to_lo = jnp.stack([back_ylo[0], ans_x[0], back_yhi[0]])
    to_hi = jnp.stack([back_ylo[2], ans_x[1], back_yhi[2]])
    back_xhi = step(to_lo, "gx", -1)
    back_xlo = step(to_hi, "gx", 1)
    velocity = far_read(slots, counts, back_xlo, back_xhi, back_ylo, back_yhi, far_w, near)
    return grid_out, velocity


def solution(mesh):
    in_specs = (
        P(None, ("gx", "gy")),
        P(("gx", "gy"), None),
        P(("gx", "gy")),
        P(("gx", "gy")),
        P(("gx", "gy")),
        P(),
        P(),
        P(),
        P(),
        P(),
    )
    out_specs = (P(None, None, "gx", "gy"), P(None, ("gx", "gy")))
    return jax.shard_map(
        on_device, mesh=mesh, in_specs=in_specs, out_specs=out_specs, check_vma=False
    )
```

```python
import jax
import jax.numpy as jnp
import numpy as np
from jax import lax
from jax.experimental import pallas as pl
from jax.experimental.pallas import tpu as pltpu
from jax.sharding import PartitionSpec as P

C = 32
SLAB = 16
BY = 128
SLOTS = 16
PAY = SLOTS * 32 + 16
ROWS = 144
STEP = 16
STEPS = 8
MIB = 1 << 20
F32 = jnp.float32
BF16 = jnp.bfloat16
VMEM = pltpu.VMEM
SMEM = pltpu.SMEM


def lanes_of(shape):
    return lax.broadcasted_iota(jnp.int32, shape, len(shape) - 1)


def params(limit, grid=False):
    if grid:
        return pltpu.CompilerParams(
            dimension_semantics=("arbitrary",), vmem_limit_bytes=limit * MIB
        )
    return pltpu.CompilerParams(vmem_limit_bytes=limit * MIB)


def cost(flops, nbytes):
    return pl.CostEstimate(flops=flops, bytes_accessed=nbytes, transcendentals=0)


def upward(i):
    return jnp.where(i % 2 == 0, 2, 0)


def splat_four(f, w_ref, first):
    parts = []
    for j in (0, 2):
        at = (first + j) * 128
        fa = f[:, at : at + 128]
        fb = f[:, at + 128 : at + 256]
        none = jnp.zeros_like(fa)
        lhs = jnp.concatenate(
            [jnp.concatenate([fa, none], 1), jnp.concatenate([none, fb], 1)], 0
        )
        parts.append(jnp.dot(lhs, w_ref[at : at + 256, :], preferred_element_type=F32))
    a = jnp.concatenate(parts, 0).astype(BF16).T.astype(F32)
    a = a.reshape(4, 2, 2, 8, 128)
    lane = lanes_of((4, 2, 8, 128))
    v0, v1 = a[:, 0], a[:, 1]
    n0 = jnp.where(lane < 64, v0, pltpu.roll(v1, 64, 3))
    n1 = jnp.where(lane < 64, pltpu.roll(v0, 64, 3), v1)
    lane = lanes_of((4, 8, 128))
    tiles = []
    for n in (n0, n1):
        v0, v1 = n[:, 0], n[:, 1]
        tiles.append(jnp.where(lane % 64 < 32, v0, pltpu.roll(v1, 32, 2)))
        tiles.append(jnp.where(lane % 64 < 32, pltpu.roll(v0, 96, 2), v1))
    return tiles


def chunk_copies(f_hbm, w_hbm, fv, wv, sems, first):
    rows = STEP * 128
    pairs = []
    for c in range(STEPS):
        at = first * 128 + c * rows
        pairs.append(
            (
                pltpu.make_async_copy(
                    w_hbm.at[pl.ds(at, rows)], wv.at[pl.ds(c * rows, rows)], sems.at[c]
                ),
                pltpu.make_async_copy(f_hbm.at[:, pl.ds(at, rows)], fv.at[c], sems.at[STEPS + c]),
            )
        )
    return pairs


def far_splat_kernel(
    owners_h, ids_h, counts_h, f_hbm, w_hbm, out_a, mid, out_b, slots,
    fv, wv, tiles, idrows, filled, owners, ids, counts, sems, isems,
):
    ix = lax.axis_index("gx")
    iy = lax.axis_index("gy")
    copies = chunk_copies(f_hbm, w_hbm, fv, wv, sems, 128)
    small = [
        pltpu.make_async_copy(src, dst, isems.at[k])
        for k, (src, dst) in enumerate(((owners_h, owners), (ids_h, ids), (counts_h, counts)))
    ]
    for copy in small:
        copy.start()
    for pair in copies:
        for copy in pair:
            copy.start()
    tiles[...] = jnp.zeros_like(tiles)
    idrows[...] = jnp.zeros_like(idrows)
    for k in range(9):
        filled[k] = 0
    for copy in small:
        copy.wait()
    lane = lanes_of((1, 128))
    count = counts[0]
    for c, pair in enumerate(copies):
        for copy in pair:
            copy.wait()
        got = []
        for group in range(STEP // 4):
            got += splat_four(fv.at[c], wv.at[pl.ds(c * STEP * 128, STEP * 128)], group * 4)
        for j in range(STEP):
            block = c * STEP + j
            owner = owners[128 + block]
            live = 128 + block < count
            target = ((owner >> 3) - ix + 1) * 3 + (owner & 7) - iy + 1
            target = jnp.where(live, target, 4)
            rank = filled[target]
            filled[target] = jnp.where(live, rank + 1, 0)
            slot = target * SLOTS + rank
            slots[block] = slot
            tiles[slot] = got[j].reshape(32, 128).astype(BF16)
            row = idrows[pl.ds(target, 1), :]
            idrows[pl.ds(target, 1), :] = jnp.where(
                lane == rank, ids[128 + block].astype(F32), row
            )
    toward = upward(ix)
    for dx, out in ((toward, out_a), (1, mid), (2 - toward, out_b)):
        for dy in range(3):
            k = dx * 3 + dy
            out[dy, 0 : SLOTS * 32, :] = tiles[pl.ds(k * SLOTS, SLOTS)].reshape(SLOTS * 32, 128)
            out[dy, SLOTS * 32 : PAY, :] = jnp.broadcast_to(
                idrows[pl.ds(k, 1), :], (16, 128)
            ).astype(BF16)


def far_splat(features, weights, owners, ids, counts):
    pay = jax.ShapeDtypeStruct((3, PAY, 128), BF16)
    vm = pl.BlockSpec(memory_space=VMEM)
    anywhere = pl.BlockSpec(memory_space=pl.ANY)
    return pl.pallas_call(
        far_splat_kernel,
        in_specs=[anywhere] * 5,
        out_specs=[vm, vm, vm, pl.BlockSpec(memory_space=SMEM)],
        out_shape=[pay, pay, pay, jax.ShapeDtypeStruct((128,), jnp.int32)],
        scratch_shapes=[
            VMEM((STEPS, C, STEP * 128), BF16),
            VMEM((STEPS * STEP * 128, 128), BF16),
            VMEM((9 * SLOTS, 32, 128), BF16),
            VMEM((16, 128), F32),
            SMEM((9,), jnp.int32),
            SMEM((256,), jnp.int32),
            SMEM((256,), jnp.int32),
            SMEM((1,), jnp.int32),
            pltpu.SemaphoreType.DMA((2 * STEPS,)),
            pltpu.SemaphoreType.DMA((3,)),
        ],
        compiler_params=params(56),
        cost_estimate=cost(2 * 128 * 32 * 128 * 128, 6 * MIB),
        name="far_splat",
    )(owners, ids, counts, features, weights)


def tile_place(tile):
    return (tile >> 5) * 4, (tile >> 4) & 1, pl.multiple_of((tile & 15) * 8, 8)


def own_splat_kernel(ids, f_hbm, w_hbm, out, fv, wv, grid, sems):
    copies = chunk_copies(f_hbm, w_hbm, fv, wv, sems, 0)
    for pair in copies:
        for copy in pair:
            copy.start()
    for c, pair in enumerate(copies):
        for copy in pair:
            copy.wait()
        got = []
        for group in range(STEP // 4):
            got += splat_four(fv.at[c], wv.at[pl.ds(c * STEP * 128, STEP * 128)], group * 4)
        for j in range(STEP):
            z, tx, y = tile_place(ids[c * STEP + j])
            grid[tx, pl.ds(z, 4), pl.ds(y, 8), :] = got[j]
    out[...] = grid[...].astype(BF16)


def own_splat(features, weights, ids):
    anywhere = pl.BlockSpec(memory_space=pl.ANY)
    return pl.pallas_call(
        own_splat_kernel,
        in_specs=[pl.BlockSpec(memory_space=SMEM), anywhere, anywhere],
        out_specs=pl.BlockSpec(memory_space=VMEM),
        out_shape=jax.ShapeDtypeStruct((2, SLAB, BY, 128), BF16),
        scratch_shapes=[
            VMEM((STEPS, C, STEP * 128), BF16),
            VMEM((STEPS * STEP * 128, 128), BF16),
            VMEM((2, SLAB, BY, 128), F32),
            pltpu.SemaphoreType.DMA((2 * STEPS,)),
        ],
        compiler_params=params(56),
        cost_estimate=cost(2 * 128 * 32 * 128 * 128, 6 * MIB),
        name="own_splat",
    )(ids, features, weights)


BUNDLE = 3 * PAY + 64


def ids_of(groups):
    rows = [ref[pl.ds(at + SLOTS * 32, 16), :].astype(F32)[0:1] for ref, at in groups]
    return jnp.concatenate(rows, 0).astype(jnp.int32)


def tile_of(ref, at, j):
    rows = ref[pl.ds(pl.multiple_of(at + j * 32, 16), 32), :]
    return rows.astype(F32).reshape(4, 8, 128)


def add_tiles(grid, ids, n, ref, at):
    def add(j, carry):
        z, tx, y = tile_place(ids[n, j])
        grid[tx, pl.ds(z, 4), pl.ds(y, 8), :] += tile_of(ref, at, j)
        return carry

    lax.fori_loop(0, SLOTS, add, 0, unroll=4)


def column_kernel(
    own, xa, xb, mid, g, ids, to_a, to_b, fwd_a, fwd_b, keep_lo, keep_hi, acc, idv, sem
):
    iy = lax.axis_index("gy")
    even = iy % 2 == 0
    first = pl.multiple_of(upward(iy) * PAY, 16)
    second = pl.multiple_of((2 - upward(iy)) * PAY, 16)
    groups = [(xa, PAY), (xb, PAY)]
    groups += [(xa, first), (mid, first), (xb, first), (xa, second), (mid, second), (xb, second)]
    idv[...] = ids_of(groups)
    copy = pltpu.make_async_copy(idv, ids, sem)
    copy.start()
    g[...] = own[...].astype(F32)
    acc[...] = jnp.zeros_like(acc)
    for n, (ref, at) in enumerate(groups[2:]):
        out, k = (to_a, n) if n < 3 else (to_b, n - 3)
        out[k * PAY : (k + 1) * PAY, :] = ref[pl.ds(at, PAY), :]
    copy.wait()
    for n, (ref, at) in enumerate(groups):
        if n < 2:
            add_tiles(g, ids, n, ref, at)
            continue

        def add(j, carry, n=n, ref=ref, at=at):
            tile = ids[n, j]
            ty = tile & 15
            place = jnp.where(ty == 0, 0, jnp.where(ty == 15, 1, 2)) + (0 if n < 5 else 3)
            acc[place, (tile >> 4) & 1, pl.ds((tile >> 5) * 4, 4)] += tile_of(ref, at, j)
            return carry

        lax.fori_loop(0, SLOTS, add, 0, unroll=4)
    above = jnp.where(even, 0, 3)
    below = 3 - above
    for tx in range(2):
        for r in range(2):
            k = tx * 2 + r
            rows = slice(3 * PAY + k * 16, 3 * PAY + k * 16 + 16)
            low, high = g[tx, :, r, :], g[tx, :, BY - 2 + r, :]
            to_a[rows, :] = jnp.where(even, high, low).astype(BF16)
            to_b[rows, :] = jnp.where(even, low, high).astype(BF16)
            keep_hi[k] = acc[above, tx, :, r, :]
            keep_lo[k] = acc[below + 1, tx, :, 6 + r, :]
            high = acc[above + 1, tx, :, 6 + r, :]
            low = acc[below, tx, :, r, :]
            up = (iy >> 1) % 2 == 0
            fwd_a[k] = jnp.where(up, high, low).astype(BF16)
            fwd_b[k] = jnp.where(up, low, high).astype(BF16)


def column(own, xa, xb, mid):
    vm = pl.BlockSpec(memory_space=VMEM)
    bundle = jax.ShapeDtypeStruct((BUNDLE, 128), BF16)
    flat = [v.reshape(3 * PAY, 128) for v in (xa, xb, mid)]
    return pl.pallas_call(
        column_kernel,
        in_specs=[vm] * 4,
        out_specs=[vm, pl.BlockSpec(memory_space=SMEM)] + [vm] * 6,
        out_shape=[
            jax.ShapeDtypeStruct((2, SLAB, BY, 128), F32),
            jax.ShapeDtypeStruct((8, 128), jnp.int32),
            bundle,
            bundle,
            jax.ShapeDtypeStruct((4, SLAB, 128), BF16),
            jax.ShapeDtypeStruct((4, SLAB, 128), BF16),
            jax.ShapeDtypeStruct((4, SLAB, 128), F32),
            jax.ShapeDtypeStruct((4, SLAB, 128), F32),
        ],
        scratch_shapes=[
            VMEM((6, 2, SLAB, 8, 128), F32),
            VMEM((8, 128), jnp.int32),
            pltpu.SemaphoreType.DMA,
        ],
        compiler_params=params(16),
        cost_estimate=cost(1000, 4 * MIB),
        name="column",
    )(own, *flat)


def sum_kernel(
    part, ya, yb, far_a, far_b, keep_lo, keep_hi, g, x, to_a, to_b, ids, grid, edge, idv, sem
):
    even_x = lax.axis_index("gx") % 2 == 0
    iy = lax.axis_index("gy")
    even = iy % 2 == 0
    up = (iy >> 1) % 2 == 0
    groups = [(ref, k * PAY) for ref in (ya, yb) for k in range(3)]
    idv[0:6, :] = ids_of(groups)
    idv[6:8, :] = jnp.zeros((2, 128), jnp.int32)
    copy = pltpu.make_async_copy(idv, ids, sem)
    copy.start()
    grid[...] = part[...]
    edge[...] = jnp.zeros_like(edge)
    for tx in range(2):
        for r in range(2):
            k = tx * 2 + r
            rows = slice(3 * PAY + k * 16, 3 * PAY + k * 16 + 16)
            near_a, near_b = ya[rows, :].astype(F32), yb[rows, :].astype(F32)
            away_a, away_b = far_a[k].astype(F32), far_b[k].astype(F32)
            low = jnp.where(iy >= 2, jnp.where(up, away_b, away_a), 0.0)
            low = low + jnp.where(even, near_b, near_a) + keep_lo[k]
            high = jnp.where(iy < 6, jnp.where(up, away_a, away_b), 0.0)
            high = high + jnp.where(even, near_a, near_b) + keep_hi[k]
            edge[tx, 0, :, 6 + r, :] = jnp.where(iy > 0, low, 0.0)
            edge[tx, 1, :, r, :] = jnp.where(iy < 7, high, 0.0)
    copy.wait()
    for n, (ref, at) in enumerate(groups):
        add_tiles(grid, ids, n, ref, at)
    lane = lanes_of((ROWS, 128))

    def plane(tx, z):
        return jnp.concatenate([edge[tx, 0, z], grid[tx, z], edge[tx, 1, z]], 0)

    def pair(z, carry):
        sides = []
        for tx in range(2):
            a, b = plane(tx, z), plane(tx, z + 8)
            x[tx, z] = a.astype(BF16)
            x[tx, z + 8] = b.astype(BF16)
            g[tx, z] = a[8 : 8 + BY].astype(BF16)
            g[tx, z + 8] = b[8 : 8 + BY].astype(BF16)
            if tx == 0:
                sides.append(jnp.where(lane < 64, a, pltpu.roll(b, 64, 1)))
            else:
                sides.append(jnp.where(lane < 64, pltpu.roll(a, 64, 1), b))
        to_a[z] = jnp.where(even_x, sides[1], sides[0]).astype(BF16)
        to_b[z] = jnp.where(even_x, sides[0], sides[1]).astype(BF16)
        return carry

    lax.fori_loop(0, 8, pair, 0, unroll=2)


def sum_tiles(part, ya, yb, far_a, far_b, keep_lo, keep_hi):
    vm = pl.BlockSpec(memory_space=VMEM)
    side = jax.ShapeDtypeStruct((SLAB // 2, ROWS, 128), BF16)
    return pl.pallas_call(
        sum_kernel,
        in_specs=[vm] * 7,
        out_specs=[vm] * 4 + [pl.BlockSpec(memory_space=SMEM)],
        out_shape=[
            jax.ShapeDtypeStruct((2, SLAB, BY, 128), BF16),
            jax.ShapeDtypeStruct((2, SLAB, ROWS, 128), BF16),
            side,
            side,
            jax.ShapeDtypeStruct((8, 128), jnp.int32),
        ],
        scratch_shapes=[
            VMEM((2, SLAB, BY, 128), F32),
            VMEM((2, 2, SLAB, 8, 128), F32),
            VMEM((8, 128), jnp.int32),
            pltpu.SemaphoreType.DMA,
        ],
        compiler_params=params(16),
        cost_estimate=cost(1000, 4 * MIB),
        name="sum_tiles",
    )(part, ya, yb, far_a, far_b, keep_lo, keep_hi)


def rows_inside(shape, iy):
    row = lax.broadcasted_iota(jnp.int32, shape, 1)
    return ((row != 7) | (iy > 0)) & ((row != 136) | (iy < 7))


def shifted(v):
    return (pltpu.roll(v, 1, 1), v, pltpu.roll(v, ROWS - 1, 1))


PAIRS = SLAB // 2


def window(ref, n, k):
    m = n * 4 + k // 2
    out = []
    for dy in range(3):
        v = ref[dy, m : m + 4, k % 2]
        out.append(v.reshape(4 * v.shape[1], v.shape[2]))
    return out


def inner_kernel(x, g, t1, t1o, b1, t2, b2, part, pre, xs, hs):
    iy = lax.axis_index("gy")
    for dy in range(3):
        xs[dy, 0, 0] = jnp.zeros((ROWS, 256), BF16)
        xs[dy, PAIRS, 1] = jnp.zeros((ROWS, 256), BF16)
        hs[dy, 0, 0] = jnp.zeros((BY, 256), BF16)
        hs[dy, PAIRS, 1] = jnp.zeros((BY, 256), BF16)

    def shift(n, carry):
        for k in range(2):
            for tx in range(2):
                v = x[tx, pl.ds(2 * n + k, 1)].astype(F32)
                for dy, s in enumerate(shifted(v)):
                    xs[dy, pl.ds(n + k, 1), 1 - k, :, tx * 128 : tx * 128 + 128] = s.astype(BF16)
        return carry

    lax.fori_loop(0, PAIRS, shift, 0)
    for n in range(2):
        for zo in range(2):
            taps = window(xs, n, zo) + window(xs, n, zo + 1) + window(xs, n, zo + 2)
            acc = jnp.dot(jnp.concatenate(taps, 1), t1[...], preferred_element_type=F32) + b1[...]
            h = jax.nn.gelu(acc).reshape(4, ROWS, 256)
            h = jnp.where(rows_inside(h.shape, iy), h, 0.0)
            for dy, s in enumerate(shifted(h)):
                m = n * 4 + zo
                hs[dy, m : m + 4, 1 - zo] = s[:, 8 : 8 + BY].astype(BF16)
    for n in range(2):
        taps = sum([window(xs, n, zi) for zi in range(4)], [])
        acc = jnp.dot(jnp.concatenate(taps, 1), t1o[...], preferred_element_type=F32) + b1[...]
        pre[n] = acc
    for n in range(2):
        for zo in range(2):
            taps = window(hs, n, zo) + window(hs, n, zo + 1) + window(hs, n, zo + 2)
            taps += [g[tx, n * 4 : n * 4 + 4, zo].reshape(4 * BY, 128) for tx in range(2)]
            acc = jnp.dot(jnp.concatenate(taps, 1), t2[...], preferred_element_type=F32) + b2[...]
            part[n * 4 : n * 4 + 4, zo] = acc.reshape(4, BY, 256)


def inner_convs(x, g, t1, t1o, b1, t2, b2):
    vm = pl.BlockSpec(memory_space=VMEM)
    return pl.pallas_call(
        inner_kernel,
        in_specs=[vm] * 7,
        out_specs=[vm, vm],
        out_shape=[
            jax.ShapeDtypeStruct((PAIRS, 2, BY, 256), F32),
            jax.ShapeDtypeStruct((2, 4 * ROWS, 256), F32),
        ],
        scratch_shapes=[
            VMEM((3, PAIRS + 1, 2, ROWS, 256), BF16),
            VMEM((3, PAIRS + 1, 2, BY, 256), BF16),
        ],
        compiler_params=params(32),
        cost_estimate=cost(2 * 20 * 256 * 256 * 2304, 6 * MIB),
        name="inner_convs",
    )(x, g.reshape(2, PAIRS, 2, BY, 128), t1, t1o, b1, t2, b2)


def tile_row(tile):
    return ((tile >> 5) * 4 + ((tile >> 2) & 3)) * 8 + ((tile >> 4) & 1) * 4 + (tile & 3)


def edge_kernel(
    ra, rb, part, pre, t1, t2, headx, ids, idx, total, table, ans_ya, ans_yb, ans_x, es, hs, vel
):
    ix = lax.axis_index("gx")
    iy = lax.axis_index("gy")
    for dy in range(3):
        es[dy, 0, 0] = jnp.zeros((ROWS, 128), BF16)
        es[dy, PAIRS, 1] = jnp.zeros((ROWS, 128), BF16)
        hs[dy, 0, 0] = jnp.zeros((BY, 128), BF16)
        hs[dy, PAIRS, 1] = jnp.zeros((BY, 128), BF16)
    lane = lanes_of((1, ROWS, 128))
    for z in range(8):
        va, vb = ra[z : z + 1].astype(F32), rb[z : z + 1].astype(F32)
        a = jnp.where(ix > 0, jnp.where(ix % 2 == 0, vb, va), 0.0)
        b = jnp.where(ix < 15, jnp.where(ix % 2 == 0, va, vb), 0.0)
        near = jnp.where(lane < 64, a, pltpu.roll(b, 64, 2))
        far = jnp.where(lane < 64, pltpu.roll(a, 64, 2), b)
        for zz, v in ((z, near), (z + 8, far)):
            m = (zz + 1) // 2
            for dy, s in enumerate(shifted(v)):
                es[dy, m : m + 1, (zz + 1) % 2] = s.astype(BF16)
    for n in range(2):
        taps = sum([window(es, n, zi) for zi in range(4)], [])
        acc = jnp.dot(jnp.concatenate(taps, 1), t1[...], preferred_element_type=F32) + pre[n]
        h = jax.nn.gelu(acc).reshape(4, ROWS, 256)
        ln = lanes_of(h.shape) & 127
        keep = ((ln >= 32) | (ix > 0)) & ((ln < 96) | (ix < 15))
        h = jnp.where(rows_inside(h.shape, iy) & keep, h, 0.0)
        for dy, s in enumerate(shifted(h)):
            s = s[:, 8 : 8 + BY].astype(BF16)
            hs[dy, n * 4 : n * 4 + 4, 1] = s[:, :, 0:128]
            hs[dy, n * 4 + 1 : n * 4 + 5, 0] = s[:, :, 128:256]
    for n in range(2):
        for zo in range(2):
            taps = window(hs, n, zo) + window(hs, n, zo + 1) + window(hs, n, zo + 2)
            acc = jnp.dot(jnp.concatenate(taps, 1), t2[...], preferred_element_type=F32)
            acc = acc.reshape(4, BY, 256) + part[n * 4 : n * 4 + 4, zo]
            acc = acc.astype(BF16)
            total[n * 4 : n * 4 + 4, zo] = acc
            v = jnp.concatenate([acc[p] for p in range(4)], 1)
            v = jnp.dot(v, headx[...], preferred_element_type=F32).T
            for p in range(4):
                for a in range(3):
                    at = p * 32 + a * 8
                    vel[a, 2 * (n * 4 + p) + zo] = v[at : at + 8]

    table[...] = jnp.zeros_like(table)
    sub = lax.broadcasted_iota(jnp.int32, (4, 8, 128), 1)
    ln = lanes_of((4, 8, 128))
    for a in range(3):
        v = vel[a].reshape(4, 2, 2, 8, 128)
        v0, v1 = v[:, 0], v[:, 1]
        l2 = lanes_of(v0.shape)
        m0 = jnp.where(l2 < 64, v0, pltpu.roll(v1, 64, 3))
        m1 = jnp.where(l2 < 64, pltpu.roll(v0, 64, 3), v1)
        for k, m in enumerate((m0, m1)):
            v0, v1 = m[:, 0], m[:, 1]
            n0 = jnp.where(ln % 64 < 32, v0, pltpu.roll(v1, 32, 2))
            n1 = jnp.where(ln % 64 < 32, pltpu.roll(v0, 96, 2), v1)
            for kk, w in enumerate((n0, n1)):
                for bit, step in ((2, 16), (1, 8)):
                    up = pltpu.roll(pltpu.roll(w, 8 - bit, 1), step, 2)
                    down = pltpu.roll(pltpu.roll(w, bit, 1), 128 - step, 2)
                    s1 = (sub & bit) != 0
                    l1 = (ln & step) != 0
                    w = jnp.where(s1 == l1, w, jnp.where(l1, up, down))
                for tz in range(4):
                    row = (tz * 4 + k * 2 + kk) * 8
                    table[row : row + 8, a, :] = w[tz]

    places = [(ans_ya, 0), (ans_ya, 1), (ans_ya, 2), (ans_yb, 0), (ans_yb, 1), (ans_yb, 2)]
    places += [(ans_x, 0), (ans_x, 1)]
    for n, (ref, k) in enumerate(places):
        source, row = (ids, n) if n < 6 else (idx, n - 6)

        def answer(j, carry, source=source, row=row, ref=ref, k=k):
            halves = []
            for h in range(2):
                r0 = table[tile_row(source[row, j * 4 + 2 * h])]
                r1 = table[tile_row(source[row, j * 4 + 2 * h + 1])]
                halves.append(two_blocks(r0, r1))
            ref[k, pl.ds(pl.multiple_of(j * 16, 16), 16), :] = jnp.concatenate(halves, 0).astype(
                BF16
            )
            return carry

        lax.fori_loop(0, SLOTS // 4, answer, 0, unroll=4)


def edge_convs(ra, rb, part, pre, t1, t2, headx, ids, idx):
    vm = pl.BlockSpec(memory_space=VMEM)
    ans = jax.ShapeDtypeStruct((3, 64, 128), BF16)
    return pl.pallas_call(
        edge_kernel,
        in_specs=[vm] * 7 + [pl.BlockSpec(memory_space=SMEM)] * 2,
        out_specs=[vm] * 5,
        out_shape=[
            jax.ShapeDtypeStruct((SLAB // 2, 2, BY, 256), BF16),
            jax.ShapeDtypeStruct((128, 8, 128), F32),
            ans,
            ans,
            jax.ShapeDtypeStruct((2, 64, 128), BF16),
        ],
        scratch_shapes=[
            VMEM((3, PAIRS + 1, 2, ROWS, 128), BF16),
            VMEM((3, PAIRS + 1, 2, BY, 128), BF16),
            VMEM((3, SLAB, 8, 128), F32),
        ],
        compiler_params=params(32),
        cost_estimate=cost(2 * 9 * 256 * 256 * 2304, 6 * MIB),
        name="edge_convs",
    )(ra, rb, part, pre, t1, t2, headx, ids, idx)


def turn_kernel(total, out):
    for k in range(4):
        out[:, k] = total[k // 2, k % 2].T.reshape(32, 8, 128)


def turn(total):
    return pl.pallas_call(
        turn_kernel,
        grid=(4,),
        in_specs=[pl.BlockSpec((2, 2, BY, 256), lambda i: (i, 0, 0, 0))],
        out_specs=pl.BlockSpec((C, 4, 8, BY), lambda i: (0, i, 0, 0)),
        out_shape=jax.ShapeDtypeStruct((C, SLAB, 8, BY), BF16),
        compiler_params=params(8, True),
        cost_estimate=cost(1000, 8 * MIB),
        name="turn",
    )(total)


BATCH = 32


def read_batch(rows, w_ref, first, out, at, count):
    cells = rows.astype(BF16).T
    owner = lanes_of((128, 128)) >> 2
    right = jnp.concatenate(
        [jnp.where(owner == b, cells, jnp.zeros_like(cells)) for b in range(BATCH)], 0
    )
    left = jnp.concatenate(
        [w_ref[(first + b) * 128 : (first + b + 1) * 128, :] for b in range(BATCH)], 1
    )
    r = jnp.dot(left, right, preferred_element_type=F32).T
    for b in range(BATCH):
        v = r[4 * b : 4 * b + 3]
        if count is not None:
            v = jnp.where(128 + first + b < count, v, 0.0)
        out[:, at + b * 128 : at + (b + 1) * 128] = v


def two_blocks(r0, r1):
    row = lax.broadcasted_iota(jnp.int32, (8, 128), 0)
    return jnp.where(row < 4, r0, pltpu.roll(r1, 4, 0))


def weight_copies(w_hbm, wv, sems, first):
    n = 128 // BATCH
    rows = BATCH * 128
    return [
        pltpu.make_async_copy(
            w_hbm.at[pl.ds(first * 128 + k * rows, rows)], wv.at[pl.ds(k * rows, rows)], sems.at[k]
        )
        for k in range(n)
    ]


def own_read_kernel(ids, table, w_hbm, out, far_w, wv, sems, fsems):
    copies = weight_copies(w_hbm, wv, sems, 0)
    later = weight_copies(w_hbm, far_w, fsems, 128)
    for copy in copies + later:
        copy.start()
    for k, copy in enumerate(copies):
        rows = [
            two_blocks(
                table[tile_row(ids[k * BATCH + 2 * j])], table[tile_row(ids[k * BATCH + 2 * j + 1])]
            )
            for j in range(BATCH // 2)
        ]
        copy.wait()
        read_batch(jnp.concatenate(rows, 0), wv, k * BATCH, out, k * BATCH * 128, None)
    for copy in later:
        copy.wait()


def own_read(ids, table, weights, particles):
    vm = pl.BlockSpec(memory_space=VMEM)
    return pl.pallas_call(
        own_read_kernel,
        in_specs=[pl.BlockSpec(memory_space=SMEM), vm, pl.BlockSpec(memory_space=pl.ANY)],
        out_specs=[vm, vm],
        out_shape=[
            jax.ShapeDtypeStruct((3, particles // 2), F32),
            jax.ShapeDtypeStruct((particles // 2, 128), BF16),
        ],
        scratch_shapes=[
            VMEM((particles // 2, 128), BF16),
            pltpu.SemaphoreType.DMA((128 // BATCH,)),
            pltpu.SemaphoreType.DMA((128 // BATCH,)),
        ],
        compiler_params=params(48),
        cost_estimate=cost(2 * 128 * 32 * 128 * 128, 9 * MIB),
        name="own_read",
    )(ids, table, weights)


def far_read_kernel(slots, counts, xa, xb, ya, yb, w, near, out, table):
    dx = upward(lax.axis_index("gx"))
    dy = upward(lax.axis_index("gy"))
    places = [(ya, 1, 3 + dy), (yb, 1, 5 - dy)]
    for ref, d in ((xa, dx), (xb, 2 - dx)):
        places += [(ref, 0, d * 3 + dy), (ref, 1, d * 3 + 1), (ref, 2, d * 3 + 2 - dy)]
    table[4 * SLOTS : 5 * SLOTS] = jnp.zeros((SLOTS, 8, 128), F32)
    for ref, k, place in places:
        v = ref[k].astype(F32).reshape(8, 8, 128)
        turned = pltpu.roll(v, 4, 1)
        for j in range(8):
            table[place * SLOTS + 2 * j] = v[j]
            table[place * SLOTS + 2 * j + 1] = turned[j]
    half = near.shape[1]
    out[:, 0:half] = near[...]
    for k in range(128 // BATCH):
        rows = [
            two_blocks(table[slots[k * BATCH + 2 * j]], table[slots[k * BATCH + 2 * j + 1]])
            for j in range(BATCH // 2)
        ]
        read_batch(
            jnp.concatenate(rows, 0), w, k * BATCH, out, half + k * BATCH * 128, counts[0]
        )


def far_read(slots, counts, xa, xb, ya, yb, w, near):
    vm = pl.BlockSpec(memory_space=VMEM)
    smem = pl.BlockSpec(memory_space=SMEM)
    return pl.pallas_call(
        far_read_kernel,
        in_specs=[smem, smem] + [vm] * 6,
        out_specs=vm,
        out_shape=jax.ShapeDtypeStruct((3, 2 * near.shape[1]), F32),
        scratch_shapes=[VMEM((9 * SLOTS, 8, 128), F32)],
        compiler_params=params(24),
        cost_estimate=cost(2 * 128 * 32 * 128 * 128, 5 * MIB),
        name="far_read",
    )(slots, counts, xa, xb, ya, yb, w, near)


def band(pin, pout, out_last):
    out = np.zeros((4, C, len(pin), len(pout), C), np.float32)
    for i, p in enumerate(pin):
        for j, q in enumerate(pout):
            if p is not None and q is not None and abs(p - q) <= 1:
                out[p - q + 1, np.arange(C), i, j, np.arange(C)] = 1
    if out_last:
        out = out.swapaxes(3, 4)
    return jnp.asarray(out.reshape(4 * C, -1), BF16)


def prepare_kernel(
    c1, c2, bias1, bias2, head, e1a, e1o, e1r, e2a, e2b, t1a, t1o, t1r, t2a, t2b, hx, b1, b2
):
    one = (
        lax.broadcasted_iota(jnp.int32, (C, C), 0) == lax.broadcasted_iota(jnp.int32, (C, C), 1)
    ).astype(BF16)
    nothing = jnp.zeros((C, C), BF16)
    for t in (t1o, t1r):
        third = t.shape[0] // 4
        t[0:third, 128:256] = jnp.zeros((third, 128), BF16)
        t[3 * third : 4 * third, 0:128] = jnp.zeros((third, 128), BF16)
    plans = (
        (c1, ((e1a, t1a, 256), (e1o, t1o, 128), (e1r, t1r, 128))),
        (c2, ((e2a, t2a, 256), (e2b, t2b, 256))),
    )
    for conv, made in plans:
        pieces = []
        for k in range(9):
            pieces += [conv[k // 3 * 9 + d * 3 + k % 3] for d in range(3)] + [nothing]
        turned = lax.dot_general(
            one, jnp.concatenate(pieces, 0), (((1,), (1,)), ((), ())), preferred_element_type=F32
        ).astype(BF16)
        lhs = jnp.concatenate([turned[:, 128 * k : 128 * k + 128] for k in range(9)], 0)
        for e, t, width in made:
            planes = e.shape[1] // width
            for p in range(planes):
                r = jnp.dot(lhs, e[:, p * width : (p + 1) * width], preferred_element_type=F32)
                r = r.astype(BF16)
                for k in range(9):
                    block = r[C * k : C * k + C]
                    at = (k * planes + p) * C
                    if width == 256:
                        t[at : at + C, :] = block
                        continue
                    for zo in range(2):
                        down = at + zo * 3 * planes * C
                        t[down : down + C, zo * 128 : zo * 128 + 128] = block
    row = lax.broadcasted_iota(jnp.int32, (256, 256), 0)
    col = lanes_of((256, 256))
    t2a[2304:2560, :] = ((row & 31) == (col >> 3)).astype(F32).astype(BF16) * (
        (row >> 5) == (col & 7)
    ).astype(F32).astype(BF16)
    spread = (
        lax.broadcasted_iota(jnp.int32, (C, 256), 0) == (lanes_of((C, 256)) >> 3)
    ).astype(F32)
    wide = jnp.dot(head[...], spread.astype(BF16), preferred_element_type=F32)
    keep = (lanes_of((8, 256)) & 7) == lax.broadcasted_iota(jnp.int32, (8, 256), 0)
    parts = [jnp.where(keep, jnp.broadcast_to(wide[a : a + 1], (8, 256)), 0.0) for a in range(3)]
    one_z = jnp.concatenate(parts + [jnp.zeros((8, 256), F32)], 0)
    turned = jnp.concatenate([one_z] * 4, 0).T
    group = lanes_of((256, 128)) >> 5
    for p in range(4):
        hx[p * 256 : p * 256 + 256, :] = jnp.where(group == p, turned, 0.0).astype(BF16)
    b1[...] = jnp.concatenate([bias1[...]] * 8, 1)
    b2[...] = jnp.dot(
        bias2[...], spread, preferred_element_type=F32, precision=lax.Precision.HIGHEST
    )


def prepare(conv_first, conv_second, bias_first, bias_second, head):
    none = None
    inner = [none, 1, 2, 3, 4, 5, 6, none]
    every = list(range(8))
    e1a = band(every, inner, False)
    e1o = band(every, [-1, 0, 7, 8], False)
    e1r = band([-2, -1, 8, 9], [-1, 0, 7, 8], False)
    e2a = band(inner, every, True)
    e2b = band([-1, 0, 7, 8], every, True)
    vm = pl.BlockSpec(memory_space=VMEM)
    return pl.pallas_call(
        prepare_kernel,
        in_specs=[vm] * 10,
        out_specs=[vm] * 8,
        out_shape=[
            jax.ShapeDtypeStruct((2304, 256), BF16),
            jax.ShapeDtypeStruct((3072, 256), BF16),
            jax.ShapeDtypeStruct((1536, 256), BF16),
            jax.ShapeDtypeStruct((2560, 256), BF16),
            jax.ShapeDtypeStruct((1152, 256), BF16),
            jax.ShapeDtypeStruct((1024, 128), BF16),
            jax.ShapeDtypeStruct((1, 256), F32),
            jax.ShapeDtypeStruct((1, 256), F32),
        ],
        compiler_params=params(16),
        cost_estimate=cost(2 * 300 * 128 * 6144, 5 * MIB),
        name="prepare",
    )(conv_first, conv_second, bias_first[None], bias_second[None], head, e1a, e1o, e1r, e2a, e2b)


def on_device(
    features,
    weights,
    owners,
    tile_ids,
    counts,
    conv_first,
    bias_first,
    conv_second,
    bias_second,
    head,
):
    particles = features.shape[1]

    def swap(x, axis, partner, reach=1):
        size = lax.axis_size(axis)
        route = []
        for i in range(size):
            up = (i // reach) % 2 == (0 if partner == "a" else 1)
            route.append((i, (i + (reach if up else -reach)) % size))
        return lax.ppermute(x, axis, route)

    to_a, mid, to_b, slots = far_splat(features, weights, owners, tile_ids, counts)
    from_xb = swap(to_b, "gx", "b")
    from_xa = swap(to_a, "gx", "a")
    made = prepare(conv_first, conv_second, bias_first, bias_second, head)
    own = own_splat(features, weights, tile_ids)
    own, made, from_xa, from_xb = lax.optimization_barrier((own, made, from_xa, from_xb))
    t1a, t1o, t1r, t2a, t2b, headx, b1, b2 = made

    g, idx, to_a, to_b, fwd_a, fwd_b, keep_lo, keep_hi = column(own, from_xa, from_xb, mid)
    from_ya = swap(to_a, "gy", "a")
    from_yb = swap(to_b, "gy", "b")
    far_a = swap(fwd_a, "gy", "a", 2)
    far_b = swap(fwd_b, "gy", "b", 2)
    g, x, to_a, to_b, ids = sum_tiles(g, from_ya, from_yb, far_a, far_b, keep_lo, keep_hi)

    xb = swap(to_b, "gx", "b")
    xa = swap(to_a, "gx", "a")
    part, pre = inner_convs(x, g, t1a, t1o, b1, t2a, b2)
    total, table, ans_ya, ans_yb, ans_x = edge_convs(xa, xb, part, pre, t1r, t2b, headx, ids, idx)

    back_ya = swap(ans_ya, "gy", "a")
    back_yb = swap(ans_yb, "gy", "b")
    grid_out = turn(total)
    grid_out, back_ya, back_yb = lax.optimization_barrier((grid_out, back_ya, back_yb))
    near, far_w = own_read(tile_ids, table, weights, particles)
    to_a = jnp.stack([back_ya[0], ans_x[0], back_yb[0]])
    to_b = jnp.stack([back_ya[2], ans_x[1], back_yb[2]])
    back_xb = swap(to_b, "gx", "b")
    back_xa = swap(to_a, "gx", "a")
    velocity = far_read(slots, counts, back_xa, back_xb, back_ya, back_yb, far_w, near)
    return grid_out, velocity


def solution(mesh):
    in_specs = (
        P(None, ("gx", "gy")),
        P(("gx", "gy"), None),
        P(("gx", "gy")),
        P(("gx", "gy")),
        P(("gx", "gy")),
        P(),
        P(),
        P(),
        P(),
        P(),
    )
    out_specs = (P(None, None, "gx", "gy"), P(None, ("gx", "gy")))
    return jax.shard_map(
        on_device, mesh=mesh, in_specs=in_specs, out_specs=out_specs, check_vma=False
    )
```

```python
import jax
import jax.numpy as jnp
import numpy as np
from jax import lax
from jax.experimental import pallas as pl
from jax.experimental.pallas import tpu as pltpu
from jax.sharding import PartitionSpec as P

C = 32
SLAB = 16
BY = 128
SLOTS = 16
PAY = SLOTS * 32 + 16
ROWS = 144
STEP = 32
STEPS = 4
MIB = 1 << 20
F32 = jnp.float32
BF16 = jnp.bfloat16
VMEM = pltpu.VMEM
SMEM = pltpu.SMEM


def lanes_of(shape):
    return lax.broadcasted_iota(jnp.int32, shape, len(shape) - 1)


def params(limit, grid=False):
    if grid:
        return pltpu.CompilerParams(
            dimension_semantics=("arbitrary",), vmem_limit_bytes=limit * MIB
        )
    return pltpu.CompilerParams(vmem_limit_bytes=limit * MIB)


def cost(flops, nbytes):
    return pl.CostEstimate(flops=flops, bytes_accessed=nbytes, transcendentals=0)


def upward(i):
    return jnp.where(i % 2 == 0, 2, 0)


def splat_four(f, w_ref, first):
    parts = []
    for j in (0, 2):
        at = (first + j) * 128
        fa = f[:, at : at + 128]
        fb = f[:, at + 128 : at + 256]
        none = jnp.zeros_like(fa)
        lhs = jnp.concatenate(
            [jnp.concatenate([fa, none], 1), jnp.concatenate([none, fb], 1)], 0
        )
        parts.append(jnp.dot(lhs, w_ref[at : at + 256, :], preferred_element_type=F32))
    a = jnp.concatenate(parts, 0).astype(BF16).T.astype(F32)
    a = a.reshape(4, 2, 2, 8, 128)
    lane = lanes_of((4, 2, 8, 128))
    v0, v1 = a[:, 0], a[:, 1]
    n0 = jnp.where(lane < 64, v0, pltpu.roll(v1, 64, 3))
    n1 = jnp.where(lane < 64, pltpu.roll(v0, 64, 3), v1)
    lane = lanes_of((4, 8, 128))
    tiles = []
    for n in (n0, n1):
        v0, v1 = n[:, 0], n[:, 1]
        tiles.append(jnp.where(lane % 64 < 32, v0, pltpu.roll(v1, 32, 2)))
        tiles.append(jnp.where(lane % 64 < 32, pltpu.roll(v0, 96, 2), v1))
    return tiles


def chunk_copies(f_hbm, w_hbm, fv, wv, sems, first):
    rows = STEP * 128
    pairs = []
    for c in range(STEPS):
        at = first * 128 + c * rows
        pairs.append(
            (
                pltpu.make_async_copy(
                    w_hbm.at[pl.ds(at, rows)], wv.at[pl.ds(c * rows, rows)], sems.at[c]
                ),
                pltpu.make_async_copy(f_hbm.at[:, pl.ds(at, rows)], fv.at[c], sems.at[STEPS + c]),
            )
        )
    return pairs


def far_splat_kernel(
    owners_h, ids_h, counts_h, f_hbm, w_hbm, out_a, mid, out_b, slots,
    fv, wv, tiles, idrows, filled, owners, ids, counts, sems, isems,
):
    ix = lax.axis_index("gx")
    iy = lax.axis_index("gy")
    copies = chunk_copies(f_hbm, w_hbm, fv, wv, sems, 128)
    small = [
        pltpu.make_async_copy(src, dst, isems.at[k])
        for k, (src, dst) in enumerate(((owners_h, owners), (ids_h, ids), (counts_h, counts)))
    ]
    for copy in small:
        copy.start()
    for pair in copies:
        for copy in pair:
            copy.start()
    tiles[...] = jnp.zeros_like(tiles)
    idrows[...] = jnp.zeros_like(idrows)
    for k in range(9):
        filled[k] = 0
    for copy in small:
        copy.wait()
    lane = lanes_of((1, 128))
    count = counts[0]
    for c, pair in enumerate(copies):
        for copy in pair:
            copy.wait()
        got = []
        for group in range(STEP // 4):
            got += splat_four(fv.at[c], wv.at[pl.ds(c * STEP * 128, STEP * 128)], group * 4)
        for j in range(STEP):
            block = c * STEP + j
            owner = owners[128 + block]
            live = 128 + block < count
            target = ((owner >> 3) - ix + 1) * 3 + (owner & 7) - iy + 1
            target = jnp.where(live, target, 4)
            rank = filled[target]
            filled[target] = jnp.where(live, rank + 1, 0)
            slot = target * SLOTS + rank
            slots[block] = slot
            tiles[slot] = got[j].reshape(32, 128).astype(BF16)
            row = idrows[pl.ds(target, 1), :]
            idrows[pl.ds(target, 1), :] = jnp.where(
                lane == rank, ids[128 + block].astype(F32), row
            )
    toward = upward(ix)
    for dx, out in ((toward, out_a), (1, mid), (2 - toward, out_b)):
        for dy in range(3):
            k = dx * 3 + dy
            at = dy * PAY
            out[at : at + SLOTS * 32, :] = tiles[pl.ds(k * SLOTS, SLOTS)].reshape(SLOTS * 32, 128)
            out[at + SLOTS * 32 : at + PAY, :] = jnp.broadcast_to(
                idrows[pl.ds(k, 1), :], (16, 128)
            ).astype(BF16)


def far_splat(features, weights, owners, ids, counts):
    pay = jax.ShapeDtypeStruct((3 * PAY, 128), BF16)
    vm = pl.BlockSpec(memory_space=VMEM)
    anywhere = pl.BlockSpec(memory_space=pl.ANY)
    return pl.pallas_call(
        far_splat_kernel,
        in_specs=[anywhere] * 5,
        out_specs=[vm, vm, vm, pl.BlockSpec(memory_space=SMEM)],
        out_shape=[pay, pay, pay, jax.ShapeDtypeStruct((128,), jnp.int32)],
        scratch_shapes=[
            VMEM((STEPS, C, STEP * 128), BF16),
            VMEM((STEPS * STEP * 128, 128), BF16),
            VMEM((9 * SLOTS, 32, 128), BF16),
            VMEM((16, 128), F32),
            SMEM((9,), jnp.int32),
            SMEM((256,), jnp.int32),
            SMEM((256,), jnp.int32),
            SMEM((1,), jnp.int32),
            pltpu.SemaphoreType.DMA((2 * STEPS,)),
            pltpu.SemaphoreType.DMA((3,)),
        ],
        compiler_params=params(56),
        cost_estimate=cost(2 * 128 * 32 * 128 * 128, 6 * MIB),
        name="far_splat",
    )(owners, ids, counts, features, weights)


def tile_place(tile):
    return (tile >> 5) * 4, (tile >> 4) & 1, pl.multiple_of((tile & 15) * 8, 8)


def own_splat_kernel(ids, f_hbm, w_hbm, out, fv, wv, grid, sems):
    copies = chunk_copies(f_hbm, w_hbm, fv, wv, sems, 0)
    for pair in copies:
        for copy in pair:
            copy.start()
    for c, pair in enumerate(copies):
        for copy in pair:
            copy.wait()
        got = []
        for group in range(STEP // 4):
            got += splat_four(fv.at[c], wv.at[pl.ds(c * STEP * 128, STEP * 128)], group * 4)
        for j in range(STEP):
            z, tx, y = tile_place(ids[c * STEP + j])
            grid[tx, pl.ds(z, 4), pl.ds(y, 8), :] = got[j]
    out[...] = grid[...].astype(BF16)


def own_splat(features, weights, ids):
    anywhere = pl.BlockSpec(memory_space=pl.ANY)
    return pl.pallas_call(
        own_splat_kernel,
        in_specs=[pl.BlockSpec(memory_space=SMEM), anywhere, anywhere],
        out_specs=pl.BlockSpec(memory_space=VMEM),
        out_shape=jax.ShapeDtypeStruct((2, SLAB, BY, 128), BF16),
        scratch_shapes=[
            VMEM((STEPS, C, STEP * 128), BF16),
            VMEM((STEPS * STEP * 128, 128), BF16),
            VMEM((2, SLAB, BY, 128), F32),
            pltpu.SemaphoreType.DMA((2 * STEPS,)),
        ],
        compiler_params=params(56),
        cost_estimate=cost(2 * 128 * 32 * 128 * 128, 6 * MIB),
        name="own_splat",
    )(ids, features, weights)


def bundle_kernel(xa, xb, mid, to_a, to_b):
    toward = upward(lax.axis_index("gy"))
    for out, dy in ((to_a, toward), (to_b, 2 - toward)):
        at = pl.multiple_of(dy * PAY, 16)
        for k, ref in enumerate((xa, mid, xb)):
            out[k * PAY : (k + 1) * PAY, :] = ref[pl.ds(at, PAY), :]


def bundle(xa, xb, mid):
    vm = pl.BlockSpec(memory_space=VMEM)
    shape = jax.ShapeDtypeStruct((3 * PAY, 128), BF16)
    return pl.pallas_call(
        bundle_kernel,
        in_specs=[vm] * 3,
        out_specs=[vm, vm],
        out_shape=[shape, shape],
        compiler_params=params(8),
        cost_estimate=cost(1000, 2 * MIB),
        name="bundle",
    )(xa, xb, mid)


def ids_of(groups):
    rows = [ref[pl.ds(at + SLOTS * 32, 16), :].astype(F32)[0:1] for ref, at in groups]
    return jnp.concatenate(rows, 0).astype(jnp.int32)


def tile_of(ref, at, j):
    rows = ref[pl.ds(pl.multiple_of(at + j * 32, 16), 32), :]
    return rows.astype(F32).reshape(4, 8, 128)


def put_tile(grid, tile, new):
    z, tx, y = tile_place(tile)
    grid[tx, pl.ds(z, 4), pl.ds(y, 8), :] += new


def column_kernel(
    own, xa, xb, mid,
    g, ids, near_a, near_b, fwd_a, fwd_b, keep_lo, keep_hi, acc_a, acc_b, idv, sem,
):
    iy = lax.axis_index("gy")
    even = iy % 2 == 0
    first = pl.multiple_of(upward(iy) * PAY, 16)
    second = pl.multiple_of((2 - upward(iy)) * PAY, 16)
    groups = [(xa, PAY), (xb, PAY)]
    groups += [(xa, first), (mid, first), (xb, first), (xa, second), (mid, second), (xb, second)]
    idv[...] = ids_of(groups)
    copy = pltpu.make_async_copy(idv, ids, sem)
    copy.start()
    g[...] = own[...].astype(F32)
    acc_a[...] = jnp.zeros_like(acc_a)
    acc_b[...] = jnp.zeros_like(acc_b)
    copy.wait()
    for k in range(3):

        def add(j, carry, k=k):
            if k < 2:
                put_tile(g, ids[k, j], tile_of(groups[k][0], groups[k][1], j))
            for n, acc in ((2 + k, acc_a), (5 + k, acc_b)):
                tile = ids[n, j]
                ty = tile & 15
                place = jnp.where(ty == 0, 0, jnp.where(ty == 15, 1, 2))
                new = tile_of(groups[n][0], groups[n][1], j)
                acc[place, (tile >> 4) & 1, pl.ds((tile >> 5) * 4, 4)] += new
            return carry

        lax.fori_loop(0, SLOTS, add, 0, unroll=8)
    for tx in range(2):
        for r in range(2):
            k = tx * 2 + r
            low, high = g[tx, :, r, :], g[tx, :, BY - 2 + r, :]
            near_a[k] = jnp.where(even, high, low).astype(BF16)
            near_b[k] = jnp.where(even, low, high).astype(BF16)
            keep_hi[k] = jnp.where(even, acc_a[0, tx, :, r, :], acc_b[0, tx, :, r, :])
            keep_lo[k] = jnp.where(even, acc_b[1, tx, :, 6 + r, :], acc_a[1, tx, :, 6 + r, :])
            high = jnp.where(even, acc_a[1, tx, :, 6 + r, :], acc_b[1, tx, :, 6 + r, :])
            low = jnp.where(even, acc_b[0, tx, :, r, :], acc_a[0, tx, :, r, :])
            up = (iy >> 1) % 2 == 0
            fwd_a[k] = jnp.where(up, high, low).astype(BF16)
            fwd_b[k] = jnp.where(up, low, high).astype(BF16)


def column(own, xa, xb, mid):
    vm = pl.BlockSpec(memory_space=VMEM)
    return pl.pallas_call(
        column_kernel,
        in_specs=[vm] * 4,
        out_specs=[vm, pl.BlockSpec(memory_space=SMEM)] + [vm] * 6,
        out_shape=[
            jax.ShapeDtypeStruct((2, SLAB, BY, 128), F32),
            jax.ShapeDtypeStruct((8, 128), jnp.int32),
        ]
        + [jax.ShapeDtypeStruct((4, SLAB, 128), BF16)] * 4
        + [jax.ShapeDtypeStruct((4, SLAB, 128), F32)] * 2,
        scratch_shapes=[
            VMEM((3, 2, SLAB, 8, 128), F32),
            VMEM((3, 2, SLAB, 8, 128), F32),
            VMEM((8, 128), jnp.int32),
            pltpu.SemaphoreType.DMA,
        ],
        compiler_params=params(16),
        cost_estimate=cost(1000, 4 * MIB),
        name="column",
    )(own, xa, xb, mid)


def sum_kernel(
    part, ya, yb, next_a, next_b, far_a, far_b, keep_lo, keep_hi,
    g, x, to_a, to_b, ids, grid, more, edge, idv, sem,
):
    even_x = lax.axis_index("gx") % 2 == 0
    iy = lax.axis_index("gy")
    even = iy % 2 == 0
    up = (iy >> 1) % 2 == 0
    groups = [(ref, k * PAY) for ref in (ya, yb) for k in range(3)]
    idv[0:6, :] = ids_of(groups)
    idv[6:8, :] = jnp.zeros((2, 128), jnp.int32)
    copy = pltpu.make_async_copy(idv, ids, sem)
    copy.start()
    grid[...] = part[...]
    more[...] = jnp.zeros_like(more)
    edge[...] = jnp.zeros_like(edge)
    for tx in range(2):
        for r in range(2):
            k = tx * 2 + r
            near_a, near_b = next_a[k].astype(F32), next_b[k].astype(F32)
            away_a, away_b = far_a[k].astype(F32), far_b[k].astype(F32)
            low = jnp.where(iy >= 2, jnp.where(up, away_b, away_a), 0.0)
            low = low + jnp.where(even, near_b, near_a) + keep_lo[k]
            high = jnp.where(iy < 6, jnp.where(up, away_a, away_b), 0.0)
            high = high + jnp.where(even, near_a, near_b) + keep_hi[k]
            edge[tx, 0, :, 6 + r, :] = jnp.where(iy > 0, low, 0.0)
            edge[tx, 1, :, r, :] = jnp.where(iy < 7, high, 0.0)
    copy.wait()
    for k in range(3):

        def add(j, carry, k=k):
            put_tile(grid, ids[k, j], tile_of(ya, k * PAY, j))
            put_tile(more, ids[3 + k, j], tile_of(yb, k * PAY, j))
            return carry

        lax.fori_loop(0, SLOTS, add, 0, unroll=8)
    lane = lanes_of((ROWS, 128))

    def plane(tx, z):
        return jnp.concatenate([edge[tx, 0, z], grid[tx, z] + more[tx, z], edge[tx, 1, z]], 0)

    def pair(z, carry):
        sides = []
        for tx in range(2):
            a, b = plane(tx, z), plane(tx, z + 8)
            x[tx, z] = a.astype(BF16)
            x[tx, z + 8] = b.astype(BF16)
            g[tx, z] = a[8 : 8 + BY].astype(BF16)
            g[tx, z + 8] = b[8 : 8 + BY].astype(BF16)
            if tx == 0:
                sides.append(jnp.where(lane < 64, a, pltpu.roll(b, 64, 1)))
            else:
                sides.append(jnp.where(lane < 64, pltpu.roll(a, 64, 1), b))
        to_a[z] = jnp.where(even_x, sides[1], sides[0]).astype(BF16)
        to_b[z] = jnp.where(even_x, sides[0], sides[1]).astype(BF16)
        return carry

    lax.fori_loop(0, 8, pair, 0, unroll=2)


def sum_tiles(part, ya, yb, near_a, near_b, far_a, far_b, keep_lo, keep_hi):
    vm = pl.BlockSpec(memory_space=VMEM)
    side = jax.ShapeDtypeStruct((SLAB // 2, ROWS, 128), BF16)
    return pl.pallas_call(
        sum_kernel,
        in_specs=[vm] * 9,
        out_specs=[vm] * 4 + [pl.BlockSpec(memory_space=SMEM)],
        out_shape=[
            jax.ShapeDtypeStruct((2, SLAB, BY, 128), BF16),
            jax.ShapeDtypeStruct((2, SLAB, ROWS, 128), BF16),
            side,
            side,
            jax.ShapeDtypeStruct((8, 128), jnp.int32),
        ],
        scratch_shapes=[
            VMEM((2, SLAB, BY, 128), F32),
            VMEM((2, SLAB, BY, 128), F32),
            VMEM((2, 2, SLAB, 8, 128), F32),
            VMEM((8, 128), jnp.int32),
            pltpu.SemaphoreType.DMA,
        ],
        compiler_params=params(16),
        cost_estimate=cost(1000, 4 * MIB),
        name="sum_tiles",
    )(part, ya, yb, near_a, near_b, far_a, far_b, keep_lo, keep_hi)


def rows_inside(shape, iy):
    row = lax.broadcasted_iota(jnp.int32, shape, 1)
    return ((row != 7) | (iy > 0)) & ((row != 136) | (iy < 7))


def shifted(v):
    return (pltpu.roll(v, 1, 1), v, pltpu.roll(v, ROWS - 1, 1))


PAIRS = SLAB // 2


def window(ref, n, k):
    m = n * 4 + k // 2
    out = []
    for dy in range(3):
        v = ref[dy, m : m + 4, k % 2]
        out.append(v.reshape(4 * v.shape[1], v.shape[2]))
    return out


def inner_kernel(x, g, t1, t1o, b1, t2, b2, part, pre, xs, hs):
    iy = lax.axis_index("gy")
    for dy in range(3):
        xs[dy, 0, 0] = jnp.zeros((ROWS, 256), BF16)
        xs[dy, PAIRS, 1] = jnp.zeros((ROWS, 256), BF16)
        hs[dy, 0, 0] = jnp.zeros((BY, 256), BF16)
        hs[dy, PAIRS, 1] = jnp.zeros((BY, 256), BF16)

    def shift(n, carry):
        for k in range(2):
            for tx in range(2):
                v = x[tx, pl.ds(2 * n + k, 1)].astype(F32)
                for dy, s in enumerate(shifted(v)):
                    xs[dy, pl.ds(n + k, 1), 1 - k, :, tx * 128 : tx * 128 + 128] = s.astype(BF16)
        return carry

    lax.fori_loop(0, PAIRS, shift, 0)
    for n in range(2):
        for zo in range(2):
            taps = window(xs, n, zo) + window(xs, n, zo + 1) + window(xs, n, zo + 2)
            acc = jnp.dot(jnp.concatenate(taps, 1), t1[...], preferred_element_type=F32) + b1[...]
            h = jax.nn.gelu(acc).reshape(4, ROWS, 256)
            h = jnp.where(rows_inside(h.shape, iy), h, 0.0)
            for dy, s in enumerate(shifted(h)):
                m = n * 4 + zo
                hs[dy, m : m + 4, 1 - zo] = s[:, 8 : 8 + BY].astype(BF16)
    for n in range(2):
        taps = sum([window(xs, n, zi) for zi in range(4)], [])
        acc = jnp.dot(jnp.concatenate(taps, 1), t1o[...], preferred_element_type=F32) + b1[...]
        pre[n] = acc
    for n in range(2):
        for zo in range(2):
            taps = window(hs, n, zo) + window(hs, n, zo + 1) + window(hs, n, zo + 2)
            taps += [g[tx, n * 4 : n * 4 + 4, zo].reshape(4 * BY, 128) for tx in range(2)]
            acc = jnp.dot(jnp.concatenate(taps, 1), t2[...], preferred_element_type=F32) + b2[...]
            part[n * 4 : n * 4 + 4, zo] = acc.reshape(4, BY, 256)


def inner_convs(x, g, t1, t1o, b1, t2, b2):
    vm = pl.BlockSpec(memory_space=VMEM)
    return pl.pallas_call(
        inner_kernel,
        in_specs=[vm] * 7,
        out_specs=[vm, vm],
        out_shape=[
            jax.ShapeDtypeStruct((PAIRS, 2, BY, 256), F32),
            jax.ShapeDtypeStruct((2, 4 * ROWS, 256), F32),
        ],
        scratch_shapes=[
            VMEM((3, PAIRS + 1, 2, ROWS, 256), BF16),
            VMEM((3, PAIRS + 1, 2, BY, 256), BF16),
        ],
        compiler_params=params(32),
        cost_estimate=cost(2 * 20 * 256 * 256 * 2304, 6 * MIB),
        name="inner_convs",
    )(x, g.reshape(2, PAIRS, 2, BY, 128), t1, t1o, b1, t2, b2)


def tile_row(tile):
    return ((tile >> 5) * 4 + ((tile >> 2) & 3)) * 8 + ((tile >> 4) & 1) * 4 + (tile & 3)


def edge_kernel(
    ra, rb, part, pre, t1, t2, headx, ids, idx, total, table, ans_ya, ans_yb, ans_x, es, hs, vel
):
    ix = lax.axis_index("gx")
    iy = lax.axis_index("gy")
    for dy in range(3):
        es[dy, 0, 0] = jnp.zeros((ROWS, 128), BF16)
        es[dy, PAIRS, 1] = jnp.zeros((ROWS, 128), BF16)
        hs[dy, 0, 0] = jnp.zeros((BY, 128), BF16)
        hs[dy, PAIRS, 1] = jnp.zeros((BY, 128), BF16)
    lane = lanes_of((1, ROWS, 128))
    for z in range(8):
        va, vb = ra[z : z + 1].astype(F32), rb[z : z + 1].astype(F32)
        a = jnp.where(ix > 0, jnp.where(ix % 2 == 0, vb, va), 0.0)
        b = jnp.where(ix < 15, jnp.where(ix % 2 == 0, va, vb), 0.0)
        near = jnp.where(lane < 64, a, pltpu.roll(b, 64, 2))
        far = jnp.where(lane < 64, pltpu.roll(a, 64, 2), b)
        for zz, v in ((z, near), (z + 8, far)):
            m = (zz + 1) // 2
            for dy, s in enumerate(shifted(v)):
                es[dy, m : m + 1, (zz + 1) % 2] = s.astype(BF16)
    for n in range(2):
        taps = sum([window(es, n, zi) for zi in range(4)], [])
        acc = jnp.dot(jnp.concatenate(taps, 1), t1[...], preferred_element_type=F32) + pre[n]
        h = jax.nn.gelu(acc).reshape(4, ROWS, 256)
        ln = lanes_of(h.shape) & 127
        keep = ((ln >= 32) | (ix > 0)) & ((ln < 96) | (ix < 15))
        h = jnp.where(rows_inside(h.shape, iy) & keep, h, 0.0)
        for dy, s in enumerate(shifted(h)):
            s = s[:, 8 : 8 + BY].astype(BF16)
            hs[dy, n * 4 : n * 4 + 4, 1] = s[:, :, 0:128]
            hs[dy, n * 4 + 1 : n * 4 + 5, 0] = s[:, :, 128:256]
    rows = []
    for n in range(2):
        for zo in range(2):
            taps = window(hs, n, zo) + window(hs, n, zo + 1) + window(hs, n, zo + 2)
            acc = jnp.dot(jnp.concatenate(taps, 1), t2[...], preferred_element_type=F32)
            acc = acc.reshape(4, BY, 256) + part[n * 4 : n * 4 + 4, zo]
            acc = acc.astype(BF16)
            total[n * 4 : n * 4 + 4, zo] = acc
            rows.append(jnp.concatenate([acc[p] for p in range(4)], 1))
    v = jnp.dot(jnp.concatenate(rows, 0), headx[...], preferred_element_type=F32).T
    for n in range(2):
        for zo in range(2):
            q = (n * 2 + zo) * BY
            for p in range(4):
                for a in range(3):
                    at = p * 32 + a * 8
                    vel[a, 2 * (n * 4 + p) + zo] = v[at : at + 8, q : q + BY]

    table[...] = jnp.zeros_like(table)
    sub = lax.broadcasted_iota(jnp.int32, (4, 8, 128), 1)
    ln = lanes_of((4, 8, 128))
    for a in range(3):
        v = vel[a].reshape(4, 2, 2, 8, 128)
        v0, v1 = v[:, 0], v[:, 1]
        l2 = lanes_of(v0.shape)
        m0 = jnp.where(l2 < 64, v0, pltpu.roll(v1, 64, 3))
        m1 = jnp.where(l2 < 64, pltpu.roll(v0, 64, 3), v1)
        for k, m in enumerate((m0, m1)):
            v0, v1 = m[:, 0], m[:, 1]
            n0 = jnp.where(ln % 64 < 32, v0, pltpu.roll(v1, 32, 2))
            n1 = jnp.where(ln % 64 < 32, pltpu.roll(v0, 96, 2), v1)
            for kk, w in enumerate((n0, n1)):
                for bit, step in ((2, 16), (1, 8)):
                    up = pltpu.roll(pltpu.roll(w, 8 - bit, 1), step, 2)
                    down = pltpu.roll(pltpu.roll(w, bit, 1), 128 - step, 2)
                    s1 = (sub & bit) != 0
                    l1 = (ln & step) != 0
                    w = jnp.where(s1 == l1, w, jnp.where(l1, up, down))
                for tz in range(4):
                    row = (tz * 4 + k * 2 + kk) * 8
                    table[row : row + 8, a, :] = w[tz]

    places = [(ans_ya, 0), (ans_ya, 1), (ans_ya, 2), (ans_yb, 0), (ans_yb, 1), (ans_yb, 2)]
    places += [(ans_x, 0), (ans_x, 1)]
    for n, (ref, k) in enumerate(places):
        source, row = (ids, n) if n < 6 else (idx, n - 6)

        def answer(j, carry, source=source, row=row, ref=ref, k=k):
            halves = []
            for h in range(2):
                r0 = table[tile_row(source[row, j * 4 + 2 * h])]
                r1 = table[tile_row(source[row, j * 4 + 2 * h + 1])]
                halves.append(two_blocks(r0, r1))
            ref[k, pl.ds(pl.multiple_of(j * 16, 16), 16), :] = jnp.concatenate(halves, 0).astype(
                BF16
            )
            return carry

        lax.fori_loop(0, SLOTS // 4, answer, 0, unroll=4)


def edge_convs(ra, rb, part, pre, t1, t2, headx, ids, idx):
    vm = pl.BlockSpec(memory_space=VMEM)
    ans = jax.ShapeDtypeStruct((3, 64, 128), BF16)
    return pl.pallas_call(
        edge_kernel,
        in_specs=[vm] * 7 + [pl.BlockSpec(memory_space=SMEM)] * 2,
        out_specs=[vm] * 5,
        out_shape=[
            jax.ShapeDtypeStruct((SLAB // 2, 2, BY, 256), BF16),
            jax.ShapeDtypeStruct((128, 8, 128), F32),
            ans,
            ans,
            jax.ShapeDtypeStruct((2, 64, 128), BF16),
        ],
        scratch_shapes=[
            VMEM((3, PAIRS + 1, 2, ROWS, 128), BF16),
            VMEM((3, PAIRS + 1, 2, BY, 128), BF16),
            VMEM((3, SLAB, 8, 128), F32),
        ],
        compiler_params=params(32),
        cost_estimate=cost(2 * 9 * 256 * 256 * 2304, 6 * MIB),
        name="edge_convs",
    )(ra, rb, part, pre, t1, t2, headx, ids, idx)


def turn_kernel(total, out):
    for k in range(4):
        out[:, k] = total[k // 2, k % 2].T.reshape(32, 8, 128)


def turn(total):
    return pl.pallas_call(
        turn_kernel,
        grid=(4,),
        in_specs=[pl.BlockSpec((2, 2, BY, 256), lambda i: (i, 0, 0, 0))],
        out_specs=pl.BlockSpec((C, 4, 8, BY), lambda i: (0, i, 0, 0)),
        out_shape=jax.ShapeDtypeStruct((C, SLAB, 8, BY), BF16),
        compiler_params=params(8, True),
        cost_estimate=cost(1000, 8 * MIB),
        name="turn",
    )(total)


BATCH = 32


def read_batch(rows, w_ref, first, out, at, count):
    cells = rows.astype(BF16).T
    owner = lanes_of((128, 128)) >> 2
    right = jnp.concatenate(
        [jnp.where(owner == b, cells, jnp.zeros_like(cells)) for b in range(BATCH)], 0
    )
    left = jnp.concatenate(
        [w_ref[(first + b) * 128 : (first + b + 1) * 128, :] for b in range(BATCH)], 1
    )
    r = jnp.dot(left, right, preferred_element_type=F32).T
    for b in range(BATCH):
        v = r[4 * b : 4 * b + 3]
        if count is not None:
            v = jnp.where(128 + first + b < count, v, 0.0)
        out[:, at + b * 128 : at + (b + 1) * 128] = v


def two_blocks(r0, r1):
    row = lax.broadcasted_iota(jnp.int32, (8, 128), 0)
    return jnp.where(row < 4, r0, pltpu.roll(r1, 4, 0))


def weight_copies(w_hbm, wv, sems, first):
    n = 128 // BATCH
    rows = BATCH * 128
    return [
        pltpu.make_async_copy(
            w_hbm.at[pl.ds(first * 128 + k * rows, rows)], wv.at[pl.ds(k * rows, rows)], sems.at[k]
        )
        for k in range(n)
    ]


def own_read_kernel(ids, table, w_hbm, out, far_w, wv, sems, fsems):
    copies = weight_copies(w_hbm, wv, sems, 0)
    later = weight_copies(w_hbm, far_w, fsems, 128)
    for copy in copies + later:
        copy.start()
    for k, copy in enumerate(copies):
        rows = [
            two_blocks(
                table[tile_row(ids[k * BATCH + 2 * j])], table[tile_row(ids[k * BATCH + 2 * j + 1])]
            )
            for j in range(BATCH // 2)
        ]
        copy.wait()
        read_batch(jnp.concatenate(rows, 0), wv, k * BATCH, out, k * BATCH * 128, None)
    for copy in later:
        copy.wait()


def own_read(ids, table, weights, particles):
    vm = pl.BlockSpec(memory_space=VMEM)
    return pl.pallas_call(
        own_read_kernel,
        in_specs=[pl.BlockSpec(memory_space=SMEM), vm, pl.BlockSpec(memory_space=pl.ANY)],
        out_specs=[vm, vm],
        out_shape=[
            jax.ShapeDtypeStruct((3, particles // 2), F32),
            jax.ShapeDtypeStruct((particles // 2, 128), BF16),
        ],
        scratch_shapes=[
            VMEM((particles // 2, 128), BF16),
            pltpu.SemaphoreType.DMA((128 // BATCH,)),
            pltpu.SemaphoreType.DMA((128 // BATCH,)),
        ],
        compiler_params=params(48),
        cost_estimate=cost(2 * 128 * 32 * 128 * 128, 9 * MIB),
        name="own_read",
    )(ids, table, weights)


def far_read_kernel(slots, counts, xa, xb, ya, yb, w, near, out, table, made, sems):
    dx = upward(lax.axis_index("gx"))
    dy = upward(lax.axis_index("gy"))
    places = [(ya, 1, 3 + dy), (yb, 1, 5 - dy)]
    for ref, d in ((xa, dx), (xb, 2 - dx)):
        places += [(ref, 0, d * 3 + dy), (ref, 1, d * 3 + 1), (ref, 2, d * 3 + 2 - dy)]
    table[4 * SLOTS : 5 * SLOTS] = jnp.zeros((SLOTS, 8, 128), F32)
    for ref, k, place in places:
        v = ref[k].astype(F32).reshape(8, 8, 128)
        turned = pltpu.roll(v, 4, 1)
        for j in range(8):
            table[place * SLOTS + 2 * j] = v[j]
            table[place * SLOTS + 2 * j + 1] = turned[j]
    half = near.shape[1]
    size = BATCH * 128
    copies = [pltpu.make_async_copy(near, out.at[:, pl.ds(0, half)], sems.at[128 // BATCH])]
    copies[0].start()
    for k in range(128 // BATCH):
        rows = [
            two_blocks(table[slots[k * BATCH + 2 * j]], table[slots[k * BATCH + 2 * j + 1]])
            for j in range(BATCH // 2)
        ]
        read_batch(jnp.concatenate(rows, 0), w, k * BATCH, made.at[k], 0, counts[0])
        copies.append(
            pltpu.make_async_copy(
                made.at[k], out.at[:, pl.ds(half + k * size, size)], sems.at[k]
            )
        )
        copies[-1].start()
    for copy in copies:
        copy.wait()


def far_read(slots, counts, xa, xb, ya, yb, w, near):
    vm = pl.BlockSpec(memory_space=VMEM)
    smem = pl.BlockSpec(memory_space=SMEM)
    return pl.pallas_call(
        far_read_kernel,
        in_specs=[smem, smem] + [vm] * 6,
        out_specs=pl.BlockSpec(memory_space=pl.ANY),
        out_shape=jax.ShapeDtypeStruct((3, 2 * near.shape[1]), F32),
        scratch_shapes=[
            VMEM((9 * SLOTS, 8, 128), F32),
            VMEM((128 // BATCH, 3, BATCH * 128), F32),
            pltpu.SemaphoreType.DMA((128 // BATCH + 1,)),
        ],
        compiler_params=params(24),
        cost_estimate=cost(2 * 128 * 32 * 128 * 128, 5 * MIB),
        name="far_read",
    )(slots, counts, xa, xb, ya, yb, w, near)


def band(pin, pout, out_last):
    out = np.zeros((4, C, len(pin), len(pout), C), np.float32)
    for i, p in enumerate(pin):
        for j, q in enumerate(pout):
            if p is not None and q is not None and abs(p - q) <= 1:
                out[p - q + 1, np.arange(C), i, j, np.arange(C)] = 1
    if out_last:
        out = out.swapaxes(3, 4)
    return jnp.asarray(out.reshape(4 * C, -1), BF16)


def prepare_kernel(
    c1, c2, bias1, bias2, head, e1a, e1o, e1r, e2a, e2b, t1a, t1o, t1r, t2a, t2b, hx, b1, b2
):
    one = (
        lax.broadcasted_iota(jnp.int32, (C, C), 0) == lax.broadcasted_iota(jnp.int32, (C, C), 1)
    ).astype(BF16)
    nothing = jnp.zeros((C, C), BF16)
    for t in (t1o, t1r):
        third = t.shape[0] // 4
        t[0:third, 128:256] = jnp.zeros((third, 128), BF16)
        t[3 * third : 4 * third, 0:128] = jnp.zeros((third, 128), BF16)
    plans = (
        (c1, ((e1a, t1a, 256), (e1o, t1o, 128), (e1r, t1r, 128))),
        (c2, ((e2a, t2a, 256), (e2b, t2b, 256))),
    )
    for conv, made in plans:
        pieces = []
        for k in range(9):
            pieces += [conv[k // 3 * 9 + d * 3 + k % 3] for d in range(3)] + [nothing]
        turned = lax.dot_general(
            one, jnp.concatenate(pieces, 0), (((1,), (1,)), ((), ())), preferred_element_type=F32
        ).astype(BF16)
        lhs = jnp.concatenate([turned[:, 128 * k : 128 * k + 128] for k in range(9)], 0)
        for e, t, width in made:
            planes = e.shape[1] // width
            for p in range(planes):
                r = jnp.dot(lhs, e[:, p * width : (p + 1) * width], preferred_element_type=F32)
                r = r.astype(BF16)
                for k in range(9):
                    block = r[C * k : C * k + C]
                    at = (k * planes + p) * C
                    if width == 256:
                        t[at : at + C, :] = block
                        continue
                    for zo in range(2):
                        down = at + zo * 3 * planes * C
                        t[down : down + C, zo * 128 : zo * 128 + 128] = block
    row = lax.broadcasted_iota(jnp.int32, (256, 256), 0)
    col = lanes_of((256, 256))
    t2a[2304:2560, :] = ((row & 31) == (col >> 3)).astype(F32).astype(BF16) * (
        (row >> 5) == (col & 7)
    ).astype(F32).astype(BF16)
    spread = (
        lax.broadcasted_iota(jnp.int32, (C, 256), 0) == (lanes_of((C, 256)) >> 3)
    ).astype(F32)
    wide = jnp.dot(head[...], spread.astype(BF16), preferred_element_type=F32)
    keep = (lanes_of((8, 256)) & 7) == lax.broadcasted_iota(jnp.int32, (8, 256), 0)
    parts = [jnp.where(keep, jnp.broadcast_to(wide[a : a + 1], (8, 256)), 0.0) for a in range(3)]
    one_z = jnp.concatenate(parts + [jnp.zeros((8, 256), F32)], 0)
    turned = jnp.concatenate([one_z] * 4, 0).T
    group = lanes_of((256, 128)) >> 5
    for p in range(4):
        hx[p * 256 : p * 256 + 256, :] = jnp.where(group == p, turned, 0.0).astype(BF16)
    b1[...] = jnp.concatenate([bias1[...]] * 8, 1)
    b2[...] = jnp.dot(
        bias2[...], spread, preferred_element_type=F32, precision=lax.Precision.HIGHEST
    )


def prepare(conv_first, conv_second, bias_first, bias_second, head):
    none = None
    inner = [none, 1, 2, 3, 4, 5, 6, none]
    every = list(range(8))
    e1a = band(every, inner, False)
    e1o = band(every, [-1, 0, 7, 8], False)
    e1r = band([-2, -1, 8, 9], [-1, 0, 7, 8], False)
    e2a = band(inner, every, True)
    e2b = band([-1, 0, 7, 8], every, True)
    vm = pl.BlockSpec(memory_space=VMEM)
    return pl.pallas_call(
        prepare_kernel,
        in_specs=[vm] * 10,
        out_specs=[vm] * 8,
        out_shape=[
            jax.ShapeDtypeStruct((2304, 256), BF16),
            jax.ShapeDtypeStruct((3072, 256), BF16),
            jax.ShapeDtypeStruct((1536, 256), BF16),
            jax.ShapeDtypeStruct((2560, 256), BF16),
            jax.ShapeDtypeStruct((1152, 256), BF16),
            jax.ShapeDtypeStruct((1024, 128), BF16),
            jax.ShapeDtypeStruct((1, 256), F32),
            jax.ShapeDtypeStruct((1, 256), F32),
        ],
        compiler_params=params(16),
        cost_estimate=cost(2 * 300 * 128 * 6144, 5 * MIB),
        name="prepare",
    )(conv_first, conv_second, bias_first[None], bias_second[None], head, e1a, e1o, e1r, e2a, e2b)


def on_device(
    features,
    weights,
    owners,
    tile_ids,
    counts,
    conv_first,
    bias_first,
    conv_second,
    bias_second,
    head,
):
    particles = features.shape[1]

    def swap(x, axis, partner, reach=1):
        size = lax.axis_size(axis)
        route = []
        for i in range(size):
            up = (i // reach) % 2 == (0 if partner == "a" else 1)
            route.append((i, (i + (reach if up else -reach)) % size))
        return lax.ppermute(x, axis, route)

    to_a, mid, to_b, slots = far_splat(features, weights, owners, tile_ids, counts)
    xb = swap(to_b, "gx", "b")
    xa = swap(to_a, "gx", "a")
    made = prepare(conv_first, conv_second, bias_first, bias_second, head)
    own = own_splat(features, weights, tile_ids)
    own, made, xa, xb = lax.optimization_barrier((own, made, xa, xb))
    t1a, t1o, t1r, t2a, t2b, headx, b1, b2 = made
    to_a, to_b = bundle(xa, xb, mid)
    from_ya = swap(to_a, "gy", "a")
    from_yb = swap(to_b, "gy", "b")
    own, to_a, to_b = lax.optimization_barrier((own, to_a, to_b))

    g, idx, near_a, near_b, fwd_a, fwd_b, keep_lo, keep_hi = column(own, xa, xb, mid)
    near_a = swap(near_a, "gy", "a")
    near_b = swap(near_b, "gy", "b")
    far_a = swap(fwd_a, "gy", "a", 2)
    far_b = swap(fwd_b, "gy", "b", 2)
    g, x, to_a, to_b, ids = sum_tiles(
        g, from_ya, from_yb, near_a, near_b, far_a, far_b, keep_lo, keep_hi
    )

    xb = swap(to_b, "gx", "b")
    xa = swap(to_a, "gx", "a")
    part, pre = inner_convs(x, g, t1a, t1o, b1, t2a, b2)
    total, table, ans_ya, ans_yb, ans_x = edge_convs(xa, xb, part, pre, t1r, t2b, headx, ids, idx)

    back_ya = swap(ans_ya, "gy", "a")
    back_yb = swap(ans_yb, "gy", "b")
    grid_out = turn(total)
    grid_out, back_ya, back_yb = lax.optimization_barrier((grid_out, back_ya, back_yb))
    near, far_w = own_read(tile_ids, table, weights, particles)
    to_a = jnp.stack([back_ya[0], ans_x[0], back_yb[0]])
    to_b = jnp.stack([back_ya[2], ans_x[1], back_yb[2]])
    back_xb = swap(to_b, "gx", "b")
    back_xa = swap(to_a, "gx", "a")
    velocity = far_read(slots, counts, back_xa, back_xb, back_ya, back_yb, far_w, near)
    return grid_out, velocity


def solution(mesh):
    in_specs = (
        P(None, ("gx", "gy")),
        P(("gx", "gy"), None),
        P(("gx", "gy")),
        P(("gx", "gy")),
        P(("gx", "gy")),
        P(),
        P(),
        P(),
        P(),
        P(),
    )
    out_specs = (P(None, None, "gx", "gy"), P(None, ("gx", "gy")))
    return jax.shard_map(
        on_device, mesh=mesh, in_specs=in_specs, out_specs=out_specs, check_vma=False
    )
```

```python
import jax
import jax.numpy as jnp
import numpy as np
from jax import lax
from jax.experimental import pallas as pl
from jax.experimental.pallas import tpu as pltpu
from jax.sharding import PartitionSpec as P

C = 32
SLAB = 16
BY = 128
SLOTS = 16
PAY = SLOTS * 32 + 16
ROWS = 144
STEP = 32
STEPS = 4
MIB = 1 << 20
F32 = jnp.float32
BF16 = jnp.bfloat16
VMEM = pltpu.VMEM
SMEM = pltpu.SMEM


def lanes_of(shape):
    return lax.broadcasted_iota(jnp.int32, shape, len(shape) - 1)


def params(limit, grid=False):
    if grid:
        return pltpu.CompilerParams(
            dimension_semantics=("arbitrary",), vmem_limit_bytes=limit * MIB
        )
    return pltpu.CompilerParams(vmem_limit_bytes=limit * MIB)


def cost(flops, nbytes):
    return pl.CostEstimate(flops=flops, bytes_accessed=nbytes, transcendentals=0)


def upward(i):
    return jnp.where(i % 2 == 0, 2, 0)


def splat_four(f, w_ref, first):
    parts = []
    for j in (0, 2):
        at = (first + j) * 128
        fa = f[:, at : at + 128]
        fb = f[:, at + 128 : at + 256]
        none = jnp.zeros_like(fa)
        lhs = jnp.concatenate(
            [jnp.concatenate([fa, none], 1), jnp.concatenate([none, fb], 1)], 0
        )
        parts.append(jnp.dot(lhs, w_ref[at : at + 256, :], preferred_element_type=F32))
    a = jnp.concatenate(parts, 0).astype(BF16).T.astype(F32)
    a = a.reshape(4, 2, 2, 8, 128)
    lane = lanes_of((4, 2, 8, 128))
    v0, v1 = a[:, 0], a[:, 1]
    n0 = jnp.where(lane < 64, v0, pltpu.roll(v1, 64, 3))
    n1 = jnp.where(lane < 64, pltpu.roll(v0, 64, 3), v1)
    lane = lanes_of((4, 8, 128))
    tiles = []
    for n in (n0, n1):
        v0, v1 = n[:, 0], n[:, 1]
        tiles.append(jnp.where(lane % 64 < 32, v0, pltpu.roll(v1, 32, 2)))
        tiles.append(jnp.where(lane % 64 < 32, pltpu.roll(v0, 96, 2), v1))
    return tiles


def chunk_copies(f_hbm, w_hbm, fv, wv, sems, first):
    rows = STEP * 128
    pairs = []
    for c in range(STEPS):
        at = first * 128 + c * rows
        pairs.append(
            (
                pltpu.make_async_copy(
                    w_hbm.at[pl.ds(at, rows)], wv.at[pl.ds(c * rows, rows)], sems.at[c]
                ),
                pltpu.make_async_copy(f_hbm.at[:, pl.ds(at, rows)], fv.at[c], sems.at[STEPS + c]),
            )
        )
    return pairs


def far_splat_kernel(
    owners_h, ids_h, counts_h, f_hbm, w_hbm, out_a, mid, out_b, slots,
    fv, wv, tiles, idrows, filled, owners, ids, counts, sems, isems,
):
    ix = lax.axis_index("gx")
    iy = lax.axis_index("gy")
    copies = chunk_copies(f_hbm, w_hbm, fv, wv, sems, 128)
    small = [
        pltpu.make_async_copy(src, dst, isems.at[k])
        for k, (src, dst) in enumerate(((owners_h, owners), (ids_h, ids), (counts_h, counts)))
    ]
    for copy in small:
        copy.start()
    for pair in copies:
        for copy in pair:
            copy.start()
    tiles[...] = jnp.zeros_like(tiles)
    idrows[...] = jnp.zeros_like(idrows)
    for k in range(9):
        filled[k] = 0
    for copy in small:
        copy.wait()
    lane = lanes_of((1, 128))
    count = counts[0]
    for c, pair in enumerate(copies):
        for copy in pair:
            copy.wait()
        got = []
        for group in range(STEP // 4):
            got += splat_four(fv.at[c], wv.at[pl.ds(c * STEP * 128, STEP * 128)], group * 4)
        for j in range(STEP):
            block = c * STEP + j
            owner = owners[128 + block]
            live = 128 + block < count
            target = ((owner >> 3) - ix + 1) * 3 + (owner & 7) - iy + 1
            target = jnp.where(live, target, 4)
            rank = filled[target]
            filled[target] = jnp.where(live, rank + 1, 0)
            slot = target * SLOTS + rank
            slots[block] = slot
            tiles[slot] = got[j].reshape(32, 128).astype(BF16)
            row = idrows[pl.ds(target, 1), :]
            idrows[pl.ds(target, 1), :] = jnp.where(
                lane == rank, ids[128 + block].astype(F32), row
            )
    toward = upward(ix)
    for dx, out in ((toward, out_a), (1, mid), (2 - toward, out_b)):
        for dy in range(3):
            k = dx * 3 + dy
            at = dy * PAY
            out[at : at + SLOTS * 32, :] = tiles[pl.ds(k * SLOTS, SLOTS)].reshape(SLOTS * 32, 128)
            out[at + SLOTS * 32 : at + PAY, :] = jnp.broadcast_to(
                idrows[pl.ds(k, 1), :], (16, 128)
            ).astype(BF16)


def far_splat(features, weights, owners, ids, counts):
    pay = jax.ShapeDtypeStruct((3 * PAY, 128), BF16)
    vm = pl.BlockSpec(memory_space=VMEM)
    anywhere = pl.BlockSpec(memory_space=pl.ANY)
    return pl.pallas_call(
        far_splat_kernel,
        in_specs=[anywhere] * 5,
        out_specs=[vm, vm, vm, pl.BlockSpec(memory_space=SMEM)],
        out_shape=[pay, pay, pay, jax.ShapeDtypeStruct((128,), jnp.int32)],
        scratch_shapes=[
            VMEM((STEPS, C, STEP * 128), BF16),
            VMEM((STEPS * STEP * 128, 128), BF16),
            VMEM((9 * SLOTS, 32, 128), BF16),
            VMEM((16, 128), F32),
            SMEM((9,), jnp.int32),
            SMEM((256,), jnp.int32),
            SMEM((256,), jnp.int32),
            SMEM((1,), jnp.int32),
            pltpu.SemaphoreType.DMA((2 * STEPS,)),
            pltpu.SemaphoreType.DMA((3,)),
        ],
        compiler_params=params(56),
        cost_estimate=cost(2 * 128 * 32 * 128 * 128, 6 * MIB),
        name="far_splat",
    )(owners, ids, counts, features, weights)


def tile_place(tile):
    return (tile >> 5) * 4, (tile >> 4) & 1, pl.multiple_of((tile & 15) * 8, 8)


def own_splat_kernel(ids, f_hbm, w_hbm, out, fv, wv, grid, sems):
    copies = chunk_copies(f_hbm, w_hbm, fv, wv, sems, 0)
    for pair in copies:
        for copy in pair:
            copy.start()
    for c, pair in enumerate(copies):
        for copy in pair:
            copy.wait()
        got = []
        for group in range(STEP // 4):
            got += splat_four(fv.at[c], wv.at[pl.ds(c * STEP * 128, STEP * 128)], group * 4)
        for j in range(STEP):
            z, tx, y = tile_place(ids[c * STEP + j])
            grid[tx, pl.ds(z, 4), pl.ds(y, 8), :] = got[j]
    out[...] = grid[...].astype(BF16)


def own_splat(features, weights, ids):
    anywhere = pl.BlockSpec(memory_space=pl.ANY)
    return pl.pallas_call(
        own_splat_kernel,
        in_specs=[pl.BlockSpec(memory_space=SMEM), anywhere, anywhere],
        out_specs=pl.BlockSpec(memory_space=VMEM),
        out_shape=jax.ShapeDtypeStruct((2, SLAB, BY, 128), BF16),
        scratch_shapes=[
            VMEM((STEPS, C, STEP * 128), BF16),
            VMEM((STEPS * STEP * 128, 128), BF16),
            VMEM((2, SLAB, BY, 128), F32),
            pltpu.SemaphoreType.DMA((2 * STEPS,)),
        ],
        compiler_params=params(56),
        cost_estimate=cost(2 * 128 * 32 * 128 * 128, 6 * MIB),
        name="own_splat",
    )(ids, features, weights)


def bundle_kernel(xa, xb, mid, to_a, to_b):
    toward = upward(lax.axis_index("gy"))
    for out, dy in ((to_a, toward), (to_b, 2 - toward)):
        at = pl.multiple_of(dy * PAY, 16)
        for k, ref in enumerate((xa, mid, xb)):
            out[k * PAY : (k + 1) * PAY, :] = ref[pl.ds(at, PAY), :]


def bundle(xa, xb, mid):
    vm = pl.BlockSpec(memory_space=VMEM)
    shape = jax.ShapeDtypeStruct((3 * PAY, 128), BF16)
    return pl.pallas_call(
        bundle_kernel,
        in_specs=[vm] * 3,
        out_specs=[vm, vm],
        out_shape=[shape, shape],
        compiler_params=params(8),
        cost_estimate=cost(1000, 2 * MIB),
        name="bundle",
    )(xa, xb, mid)


def ids_of(groups):
    rows = [ref[pl.ds(at + SLOTS * 32, 16), :].astype(F32)[0:1] for ref, at in groups]
    return jnp.concatenate(rows, 0).astype(jnp.int32)


def tile_of(ref, at, j):
    rows = ref[pl.ds(pl.multiple_of(at + j * 32, 16), 32), :]
    return rows.astype(F32).reshape(4, 8, 128)


def put_tile(grid, tile, new):
    z, tx, y = tile_place(tile)
    grid[tx, pl.ds(z, 4), pl.ds(y, 8), :] += new


def column_kernel(
    own, xa, xb, mid,
    g, ids, near_a, near_b, fwd_a, fwd_b, keep_lo, keep_hi, acc_a, acc_b, idv, sem,
):
    iy = lax.axis_index("gy")
    even = iy % 2 == 0
    first = pl.multiple_of(upward(iy) * PAY, 16)
    second = pl.multiple_of((2 - upward(iy)) * PAY, 16)
    groups = [(xa, PAY), (xb, PAY)]
    groups += [(xa, first), (mid, first), (xb, first), (xa, second), (mid, second), (xb, second)]
    idv[...] = ids_of(groups)
    copy = pltpu.make_async_copy(idv, ids, sem)
    copy.start()
    g[...] = own[...].astype(F32)
    acc_a[...] = jnp.zeros_like(acc_a)
    acc_b[...] = jnp.zeros_like(acc_b)
    copy.wait()
    for k in range(3):

        def add(j, carry, k=k):
            if k < 2:
                put_tile(g, ids[k, j], tile_of(groups[k][0], groups[k][1], j))
            for n, acc in ((2 + k, acc_a), (5 + k, acc_b)):
                tile = ids[n, j]
                ty = tile & 15
                place = jnp.where(ty == 0, 0, jnp.where(ty == 15, 1, 2))
                new = tile_of(groups[n][0], groups[n][1], j)
                acc[place, (tile >> 4) & 1, pl.ds((tile >> 5) * 4, 4)] += new
            return carry

        lax.fori_loop(0, SLOTS, add, 0, unroll=8)
    for tx in range(2):
        for r in range(2):
            k = tx * 2 + r
            low, high = g[tx, :, r, :], g[tx, :, BY - 2 + r, :]
            near_a[k] = jnp.where(even, high, low).astype(BF16)
            near_b[k] = jnp.where(even, low, high).astype(BF16)
            keep_hi[k] = jnp.where(even, acc_a[0, tx, :, r, :], acc_b[0, tx, :, r, :])
            keep_lo[k] = jnp.where(even, acc_b[1, tx, :, 6 + r, :], acc_a[1, tx, :, 6 + r, :])
            high = jnp.where(even, acc_a[1, tx, :, 6 + r, :], acc_b[1, tx, :, 6 + r, :])
            low = jnp.where(even, acc_b[0, tx, :, r, :], acc_a[0, tx, :, r, :])
            up = (iy >> 1) % 2 == 0
            fwd_a[k] = jnp.where(up, high, low).astype(BF16)
            fwd_b[k] = jnp.where(up, low, high).astype(BF16)


def column(own, xa, xb, mid):
    vm = pl.BlockSpec(memory_space=VMEM)
    return pl.pallas_call(
        column_kernel,
        in_specs=[vm] * 4,
        out_specs=[vm, pl.BlockSpec(memory_space=SMEM)] + [vm] * 6,
        out_shape=[
            jax.ShapeDtypeStruct((2, SLAB, BY, 128), F32),
            jax.ShapeDtypeStruct((8, 128), jnp.int32),
        ]
        + [jax.ShapeDtypeStruct((4, SLAB, 128), BF16)] * 4
        + [jax.ShapeDtypeStruct((4, SLAB, 128), F32)] * 2,
        scratch_shapes=[
            VMEM((3, 2, SLAB, 8, 128), F32),
            VMEM((3, 2, SLAB, 8, 128), F32),
            VMEM((8, 128), jnp.int32),
            pltpu.SemaphoreType.DMA,
        ],
        compiler_params=params(16),
        cost_estimate=cost(1000, 4 * MIB),
        name="column",
    )(own, xa, xb, mid)


def sum_kernel(
    part, ya, yb, next_a, next_b, far_a, far_b, keep_lo, keep_hi,
    g, x, to_a, to_b, ids, grid, more, edge, idv, sem,
):
    even_x = lax.axis_index("gx") % 2 == 0
    iy = lax.axis_index("gy")
    even = iy % 2 == 0
    up = (iy >> 1) % 2 == 0
    groups = [(ref, k * PAY) for ref in (ya, yb) for k in range(3)]
    idv[0:6, :] = ids_of(groups)
    idv[6:8, :] = jnp.zeros((2, 128), jnp.int32)
    copy = pltpu.make_async_copy(idv, ids, sem)
    copy.start()
    grid[...] = part[...]
    more[...] = jnp.zeros_like(more)
    edge[...] = jnp.zeros_like(edge)
    for tx in range(2):
        for r in range(2):
            k = tx * 2 + r
            near_a, near_b = next_a[k].astype(F32), next_b[k].astype(F32)
            away_a, away_b = far_a[k].astype(F32), far_b[k].astype(F32)
            low = jnp.where(iy >= 2, jnp.where(up, away_b, away_a), 0.0)
            low = low + jnp.where(even, near_b, near_a) + keep_lo[k]
            high = jnp.where(iy < 6, jnp.where(up, away_a, away_b), 0.0)
            high = high + jnp.where(even, near_a, near_b) + keep_hi[k]
            edge[tx, 0, :, 6 + r, :] = jnp.where(iy > 0, low, 0.0)
            edge[tx, 1, :, r, :] = jnp.where(iy < 7, high, 0.0)
    copy.wait()
    for k in range(3):

        def add(j, carry, k=k):
            put_tile(grid, ids[k, j], tile_of(ya, k * PAY, j))
            put_tile(more, ids[3 + k, j], tile_of(yb, k * PAY, j))
            return carry

        lax.fori_loop(0, SLOTS, add, 0, unroll=8)
    lane = lanes_of((ROWS, 128))

    def plane(tx, z):
        return jnp.concatenate([edge[tx, 0, z], grid[tx, z] + more[tx, z], edge[tx, 1, z]], 0)

    def pair(z, carry):
        sides = []
        for tx in range(2):
            a, b = plane(tx, z), plane(tx, z + 8)
            x[tx, z] = a.astype(BF16)
            x[tx, z + 8] = b.astype(BF16)
            g[tx, z] = a[8 : 8 + BY].astype(BF16)
            g[tx, z + 8] = b[8 : 8 + BY].astype(BF16)
            if tx == 0:
                sides.append(jnp.where(lane < 64, a, pltpu.roll(b, 64, 1)))
            else:
                sides.append(jnp.where(lane < 64, pltpu.roll(a, 64, 1), b))
        to_a[z] = jnp.where(even_x, sides[1], sides[0]).astype(BF16)
        to_b[z] = jnp.where(even_x, sides[0], sides[1]).astype(BF16)
        return carry

    lax.fori_loop(0, 8, pair, 0, unroll=2)


def sum_tiles(part, ya, yb, near_a, near_b, far_a, far_b, keep_lo, keep_hi):
    vm = pl.BlockSpec(memory_space=VMEM)
    side = jax.ShapeDtypeStruct((SLAB // 2, ROWS, 128), BF16)
    return pl.pallas_call(
        sum_kernel,
        in_specs=[vm] * 9,
        out_specs=[vm] * 4 + [pl.BlockSpec(memory_space=SMEM)],
        out_shape=[
            jax.ShapeDtypeStruct((2, SLAB, BY, 128), BF16),
            jax.ShapeDtypeStruct((2, SLAB, ROWS, 128), BF16),
            side,
            side,
            jax.ShapeDtypeStruct((8, 128), jnp.int32),
        ],
        scratch_shapes=[
            VMEM((2, SLAB, BY, 128), F32),
            VMEM((2, SLAB, BY, 128), F32),
            VMEM((2, 2, SLAB, 8, 128), F32),
            VMEM((8, 128), jnp.int32),
            pltpu.SemaphoreType.DMA,
        ],
        compiler_params=params(16),
        cost_estimate=cost(1000, 4 * MIB),
        name="sum_tiles",
    )(part, ya, yb, near_a, near_b, far_a, far_b, keep_lo, keep_hi)


def rows_inside(shape, iy):
    row = lax.broadcasted_iota(jnp.int32, shape, 1)
    return ((row != 7) | (iy > 0)) & ((row != 136) | (iy < 7))


def shifted(v):
    return (pltpu.roll(v, 1, 1), v, pltpu.roll(v, ROWS - 1, 1))


PAIRS = SLAB // 2
FETCHES = 8


def window(ref, n, k):
    m = n * 4 + k // 2
    out = []
    for dy in range(3):
        v = ref[dy, m : m + 4, k % 2]
        out.append(v.reshape(4 * v.shape[1], v.shape[2]))
    return out


def inner_kernel(x, g, t1, t1o, b1, t2, b2, w_hbm, part, pre, w, xs, xe, hs, sems):
    lane = lanes_of((1, ROWS, 128))
    rows = w.shape[0] // FETCHES
    fetches = [
        pltpu.make_async_copy(
            w_hbm.at[pl.ds(k * rows, rows)], w.at[pl.ds(k * rows, rows)], sems.at[k]
        )
        for k in range(FETCHES)
    ]
    for fetch in fetches:
        fetch.start()
    iy = lax.axis_index("gy")
    for dy in range(3):
        xs[dy, 0, 0] = jnp.zeros((ROWS, 256), BF16)
        xs[dy, PAIRS, 1] = jnp.zeros((ROWS, 256), BF16)
        xe[dy, 0, 0] = jnp.zeros((ROWS, 128), BF16)
        xe[dy, PAIRS, 1] = jnp.zeros((ROWS, 128), BF16)
        hs[dy, 0, 0] = jnp.zeros((BY, 256), BF16)
        hs[dy, PAIRS, 1] = jnp.zeros((BY, 256), BF16)

    def shift(n, carry):
        for k in range(2):
            both = [shifted(x[tx, pl.ds(2 * n + k, 1)].astype(F32)) for tx in range(2)]
            for dy in range(3):
                s0, s1 = both[0][dy], both[1][dy]
                xs[dy, pl.ds(n + k, 1), 1 - k, :, 0:128] = s0.astype(BF16)
                xs[dy, pl.ds(n + k, 1), 1 - k, :, 128:256] = s1.astype(BF16)
                xe[dy, pl.ds(n + k, 1), 1 - k] = jnp.where(lane < 64, s0, s1).astype(BF16)
        return carry

    lax.fori_loop(0, PAIRS, shift, 0)
    for n in range(2):
        for zo in range(2):
            taps = window(xs, n, zo) + window(xs, n, zo + 1) + window(xs, n, zo + 2)
            acc = jnp.dot(jnp.concatenate(taps, 1), t1[...], preferred_element_type=F32) + b1[...]
            h = jax.nn.gelu(acc).reshape(4, ROWS, 256)
            h = jnp.where(rows_inside(h.shape, iy), h, 0.0)
            for dy, s in enumerate(shifted(h)):
                m = n * 4 + zo
                hs[dy, m : m + 4, 1 - zo] = s[:, 8 : 8 + BY].astype(BF16)
    for n in range(2):
        taps = sum([window(xe, n, zi) for zi in range(4)], [])
        acc = jnp.dot(jnp.concatenate(taps, 1), t1o[...], preferred_element_type=F32) + b1[...]
        pre[n] = acc
    for n in range(2):
        for zo in range(2):
            taps = window(hs, n, zo) + window(hs, n, zo + 1) + window(hs, n, zo + 2)
            taps += [g[tx, n * 4 : n * 4 + 4, zo].reshape(4 * BY, 128) for tx in range(2)]
            acc = jnp.dot(jnp.concatenate(taps, 1), t2[...], preferred_element_type=F32) + b2[...]
            part[n * 4 : n * 4 + 4, zo] = acc.reshape(4, BY, 256)
    for fetch in fetches:
        fetch.wait()


def inner_convs(x, g, t1, t1o, b1, t2, b2, weights):
    vm = pl.BlockSpec(memory_space=VMEM)
    return pl.pallas_call(
        inner_kernel,
        in_specs=[vm] * 7 + [pl.BlockSpec(memory_space=pl.ANY)],
        out_specs=[vm, vm, vm],
        out_shape=[
            jax.ShapeDtypeStruct((PAIRS, 2, BY, 256), F32),
            jax.ShapeDtypeStruct((2, 4 * ROWS, 256), F32),
            jax.ShapeDtypeStruct(weights.shape, BF16),
        ],
        scratch_shapes=[
            VMEM((3, PAIRS + 1, 2, ROWS, 256), BF16),
            VMEM((3, PAIRS + 1, 2, ROWS, 128), BF16),
            VMEM((3, PAIRS + 1, 2, BY, 256), BF16),
            pltpu.SemaphoreType.DMA((FETCHES,)),
        ],
        compiler_params=params(32),
        cost_estimate=cost(2 * 20 * 256 * 256 * 2304, 6 * MIB),
        name="inner_convs",
    )(x, g.reshape(2, PAIRS, 2, BY, 128), t1, t1o, b1, t2, b2, weights)


def tile_row(tile):
    return ((tile >> 5) * 4 + ((tile >> 2) & 3)) * 8 + ((tile >> 4) & 1) * 4 + (tile & 3)


def edge_kernel(
    ra, rb, part, pre, t1, t2, headx, ids, idx, total, table, ans_ya, ans_yb, ans_x, es, hs, vel
):
    ix = lax.axis_index("gx")
    iy = lax.axis_index("gy")
    for dy in range(3):
        es[dy, 0, 0] = jnp.zeros((ROWS, 128), BF16)
        es[dy, PAIRS, 1] = jnp.zeros((ROWS, 128), BF16)
        hs[dy, 0, 0] = jnp.zeros((BY, 128), BF16)
        hs[dy, PAIRS, 1] = jnp.zeros((BY, 128), BF16)
    lane = lanes_of((1, ROWS, 128))
    for z in range(8):
        va, vb = ra[z : z + 1].astype(F32), rb[z : z + 1].astype(F32)
        a = jnp.where(ix > 0, jnp.where(ix % 2 == 0, vb, va), 0.0)
        b = jnp.where(ix < 15, jnp.where(ix % 2 == 0, va, vb), 0.0)
        near = jnp.where(lane < 64, a, pltpu.roll(b, 64, 2))
        far = jnp.where(lane < 64, pltpu.roll(a, 64, 2), b)
        for zz, v in ((z, near), (z + 8, far)):
            m = (zz + 1) // 2
            for dy, s in enumerate(shifted(v)):
                es[dy, m : m + 1, (zz + 1) % 2] = s.astype(BF16)
    for n in range(2):
        taps = sum([window(es, n, zi) for zi in range(4)], [])
        acc = jnp.dot(jnp.concatenate(taps, 1), t1[...], preferred_element_type=F32) + pre[n]
        h = jax.nn.gelu(acc).reshape(4, ROWS, 256)
        ln = lanes_of(h.shape) & 127
        keep = ((ln >= 32) | (ix > 0)) & ((ln < 96) | (ix < 15))
        h = jnp.where(rows_inside(h.shape, iy) & keep, h, 0.0)
        for dy, s in enumerate(shifted(h)):
            s = s[:, 8 : 8 + BY].astype(BF16)
            hs[dy, n * 4 : n * 4 + 4, 1] = s[:, :, 0:128]
            hs[dy, n * 4 + 1 : n * 4 + 5, 0] = s[:, :, 128:256]
    rows = []
    for n in range(2):
        for zo in range(2):
            taps = window(hs, n, zo) + window(hs, n, zo + 1) + window(hs, n, zo + 2)
            acc = jnp.dot(jnp.concatenate(taps, 1), t2[...], preferred_element_type=F32)
            acc = acc.reshape(4, BY, 256) + part[n * 4 : n * 4 + 4, zo]
            acc = acc.astype(BF16)
            total[n * 4 : n * 4 + 4, zo] = acc
            rows.append(jnp.concatenate([acc[p] for p in range(4)], 1))
    v = jnp.dot(jnp.concatenate(rows, 0), headx[...], preferred_element_type=F32).T
    for n in range(2):
        for zo in range(2):
            q = (n * 2 + zo) * BY
            for p in range(4):
                for a in range(3):
                    at = p * 32 + a * 8
                    vel[a, 2 * (n * 4 + p) + zo] = v[at : at + 8, q : q + BY]

    table[...] = jnp.zeros_like(table)
    sub = lax.broadcasted_iota(jnp.int32, (4, 8, 128), 1)
    ln = lanes_of((4, 8, 128))
    for a in range(3):
        v = vel[a].reshape(4, 2, 2, 8, 128)
        v0, v1 = v[:, 0], v[:, 1]
        l2 = lanes_of(v0.shape)
        m0 = jnp.where(l2 < 64, v0, pltpu.roll(v1, 64, 3))
        m1 = jnp.where(l2 < 64, pltpu.roll(v0, 64, 3), v1)
        for k, m in enumerate((m0, m1)):
            v0, v1 = m[:, 0], m[:, 1]
            n0 = jnp.where(ln % 64 < 32, v0, pltpu.roll(v1, 32, 2))
            n1 = jnp.where(ln % 64 < 32, pltpu.roll(v0, 96, 2), v1)
            for kk, w in enumerate((n0, n1)):
                for bit, step in ((2, 16), (1, 8)):
                    up = pltpu.roll(pltpu.roll(w, 8 - bit, 1), step, 2)
                    down = pltpu.roll(pltpu.roll(w, bit, 1), 128 - step, 2)
                    s1 = (sub & bit) != 0
                    l1 = (ln & step) != 0
                    w = jnp.where(s1 == l1, w, jnp.where(l1, up, down))
                for tz in range(4):
                    row = (tz * 4 + k * 2 + kk) * 8
                    table[row : row + 8, a, :] = w[tz]

    places = [(ans_ya, 0), (ans_ya, 1), (ans_ya, 2), (ans_yb, 0), (ans_yb, 1), (ans_yb, 2)]
    places += [(ans_x, 0), (ans_x, 1)]
    for n, (ref, k) in enumerate(places):
        source, row = (ids, n) if n < 6 else (idx, n - 6)

        def answer(j, carry, source=source, row=row, ref=ref, k=k):
            halves = []
            for h in range(2):
                r0 = table[tile_row(source[row, j * 4 + 2 * h])]
                r1 = table[tile_row(source[row, j * 4 + 2 * h + 1])]
                halves.append(two_blocks(r0, r1))
            ref[k, pl.ds(pl.multiple_of(j * 16, 16), 16), :] = jnp.concatenate(halves, 0).astype(
                BF16
            )
            return carry

        lax.fori_loop(0, SLOTS // 4, answer, 0, unroll=4)


def edge_convs(ra, rb, part, pre, t1, t2, headx, ids, idx):
    vm = pl.BlockSpec(memory_space=VMEM)
    ans = jax.ShapeDtypeStruct((3, 64, 128), BF16)
    return pl.pallas_call(
        edge_kernel,
        in_specs=[vm] * 7 + [pl.BlockSpec(memory_space=SMEM)] * 2,
        out_specs=[vm] * 5,
        out_shape=[
            jax.ShapeDtypeStruct((SLAB // 2, 2, BY, 256), BF16),
            jax.ShapeDtypeStruct((128, 8, 128), F32),
            ans,
            ans,
            jax.ShapeDtypeStruct((2, 64, 128), BF16),
        ],
        scratch_shapes=[
            VMEM((3, PAIRS + 1, 2, ROWS, 128), BF16),
            VMEM((3, PAIRS + 1, 2, BY, 128), BF16),
            VMEM((3, SLAB, 8, 128), F32),
        ],
        compiler_params=params(32),
        cost_estimate=cost(2 * 9 * 256 * 256 * 2304, 6 * MIB),
        name="edge_convs",
    )(ra, rb, part, pre, t1, t2, headx, ids, idx)


def turn_kernel(total, out):
    for k in range(4):
        out[:, k] = total[k // 2, k % 2].T.reshape(32, 8, 128)


def turn(total):
    return pl.pallas_call(
        turn_kernel,
        grid=(4,),
        in_specs=[pl.BlockSpec((2, 2, BY, 256), lambda i: (i, 0, 0, 0))],
        out_specs=pl.BlockSpec((C, 4, 8, BY), lambda i: (0, i, 0, 0)),
        out_shape=jax.ShapeDtypeStruct((C, SLAB, 8, BY), BF16),
        compiler_params=params(8, True),
        cost_estimate=cost(1000, 8 * MIB),
        name="turn",
    )(total)


BATCH = 32


def read_batch(rows, w_ref, first, out, at, count):
    cells = rows.astype(BF16).T
    owner = lanes_of((128, 128)) >> 2
    right = jnp.concatenate(
        [jnp.where(owner == b, cells, jnp.zeros_like(cells)) for b in range(BATCH)], 0
    )
    left = jnp.concatenate(
        [w_ref[(first + b) * 128 : (first + b + 1) * 128, :] for b in range(BATCH)], 1
    )
    r = jnp.dot(left, right, preferred_element_type=F32).T
    for b in range(BATCH):
        v = r[4 * b : 4 * b + 3]
        if count is not None:
            v = jnp.where(first + b < count, v, 0.0)
        out[:, at + b * 128 : at + (b + 1) * 128] = v


def two_blocks(r0, r1):
    row = lax.broadcasted_iota(jnp.int32, (8, 128), 0)
    return jnp.where(row < 4, r0, pltpu.roll(r1, 4, 0))


def own_read_kernel(ids, table, w, out):
    for k in range(128 // BATCH):
        rows = [
            two_blocks(
                table[tile_row(ids[k * BATCH + 2 * j])], table[tile_row(ids[k * BATCH + 2 * j + 1])]
            )
            for j in range(BATCH // 2)
        ]
        read_batch(jnp.concatenate(rows, 0), w, k * BATCH, out, k * BATCH * 128, None)


def own_read(ids, table, w):
    vm = pl.BlockSpec(memory_space=VMEM)
    return pl.pallas_call(
        own_read_kernel,
        in_specs=[pl.BlockSpec(memory_space=SMEM), vm, vm],
        out_specs=vm,
        out_shape=jax.ShapeDtypeStruct((3, w.shape[0] // 2), F32),
        compiler_params=params(24),
        cost_estimate=cost(2 * 128 * 32 * 128 * 128, 9 * MIB),
        name="own_read",
    )(ids, table, w)


def far_read_kernel(slots, counts, xa, xb, ya, yb, w, near, out, table, made, sems):
    dx = upward(lax.axis_index("gx"))
    dy = upward(lax.axis_index("gy"))
    places = [(ya, 1, 3 + dy), (yb, 1, 5 - dy)]
    for ref, d in ((xa, dx), (xb, 2 - dx)):
        places += [(ref, 0, d * 3 + dy), (ref, 1, d * 3 + 1), (ref, 2, d * 3 + 2 - dy)]
    table[4 * SLOTS : 5 * SLOTS] = jnp.zeros((SLOTS, 8, 128), F32)
    for ref, k, place in places:
        v = ref[k].astype(F32).reshape(8, 8, 128)
        turned = pltpu.roll(v, 4, 1)
        for j in range(8):
            table[place * SLOTS + 2 * j] = v[j]
            table[place * SLOTS + 2 * j + 1] = turned[j]
    half = near.shape[1]
    size = BATCH * 128
    copies = [pltpu.make_async_copy(near, out.at[:, pl.ds(0, half)], sems.at[128 // BATCH])]
    copies[0].start()
    for k in range(128 // BATCH):
        rows = [
            two_blocks(table[slots[k * BATCH + 2 * j]], table[slots[k * BATCH + 2 * j + 1]])
            for j in range(BATCH // 2)
        ]
        read_batch(jnp.concatenate(rows, 0), w, 128 + k * BATCH, made.at[k], 0, counts[0])
        copies.append(
            pltpu.make_async_copy(
                made.at[k], out.at[:, pl.ds(half + k * size, size)], sems.at[k]
            )
        )
        copies[-1].start()
    for copy in copies:
        copy.wait()


def far_read(slots, counts, xa, xb, ya, yb, w, near):
    vm = pl.BlockSpec(memory_space=VMEM)
    smem = pl.BlockSpec(memory_space=SMEM)
    return pl.pallas_call(
        far_read_kernel,
        in_specs=[smem, smem] + [vm] * 6,
        out_specs=pl.BlockSpec(memory_space=pl.ANY),
        out_shape=jax.ShapeDtypeStruct((3, 2 * near.shape[1]), F32),
        scratch_shapes=[
            VMEM((9 * SLOTS, 8, 128), F32),
            VMEM((128 // BATCH, 3, BATCH * 128), F32),
            pltpu.SemaphoreType.DMA((128 // BATCH + 1,)),
        ],
        compiler_params=params(24),
        cost_estimate=cost(2 * 128 * 32 * 128 * 128, 5 * MIB),
        name="far_read",
    )(slots, counts, xa, xb, ya, yb, w, near)


def band(pin, pout, out_last):
    out = np.zeros((4, C, len(pin), len(pout), C), np.float32)
    for i, p in enumerate(pin):
        for j, q in enumerate(pout):
            if p is not None and q is not None and abs(p - q) <= 1:
                out[p - q + 1, np.arange(C), i, j, np.arange(C)] = 1
    if out_last:
        out = out.swapaxes(3, 4)
    return jnp.asarray(out.reshape(4 * C, -1), BF16)


def prepare_kernel(
    c1, c2, bias1, bias2, head, e1a, e1o, e1r, e2a, e2b, t1a, t1o, t1r, t2a, t2b, hx, b1, b2
):
    one = (
        lax.broadcasted_iota(jnp.int32, (C, C), 0) == lax.broadcasted_iota(jnp.int32, (C, C), 1)
    ).astype(BF16)
    nothing = jnp.zeros((C, C), BF16)
    for t in (t1o, t1r):
        third = t.shape[0] // 4
        t[0:third, 128:256] = jnp.zeros((third, 128), BF16)
        t[3 * third : 4 * third, 0:128] = jnp.zeros((third, 128), BF16)
    plans = (
        (c1, ((e1a, t1a, 256), (e1o, t1o, 128), (e1r, t1r, 128))),
        (c2, ((e2a, t2a, 256), (e2b, t2b, 256))),
    )
    for conv, made in plans:
        pieces = []
        for k in range(9):
            pieces += [conv[k // 3 * 9 + d * 3 + k % 3] for d in range(3)] + [nothing]
        turned = lax.dot_general(
            one, jnp.concatenate(pieces, 0), (((1,), (1,)), ((), ())), preferred_element_type=F32
        ).astype(BF16)
        lhs = jnp.concatenate([turned[:, 128 * k : 128 * k + 128] for k in range(9)], 0)
        for e, t, width in made:
            planes = e.shape[1] // width
            for p in range(planes):
                r = jnp.dot(lhs, e[:, p * width : (p + 1) * width], preferred_element_type=F32)
                r = r.astype(BF16)
                for k in range(9):
                    block = r[C * k : C * k + C]
                    at = (k * planes + p) * C
                    if width == 256:
                        t[at : at + C, :] = block
                        continue
                    for zo in range(2):
                        down = at + zo * 3 * planes * C
                        t[down : down + C, zo * 128 : zo * 128 + 128] = block
    row = lax.broadcasted_iota(jnp.int32, (256, 256), 0)
    col = lanes_of((256, 256))
    t2a[2304:2560, :] = ((row & 31) == (col >> 3)).astype(F32).astype(BF16) * (
        (row >> 5) == (col & 7)
    ).astype(F32).astype(BF16)
    spread = (
        lax.broadcasted_iota(jnp.int32, (C, 256), 0) == (lanes_of((C, 256)) >> 3)
    ).astype(F32)
    wide = jnp.dot(head[...], spread.astype(BF16), preferred_element_type=F32)
    keep = (lanes_of((8, 256)) & 7) == lax.broadcasted_iota(jnp.int32, (8, 256), 0)
    parts = [jnp.where(keep, jnp.broadcast_to(wide[a : a + 1], (8, 256)), 0.0) for a in range(3)]
    one_z = jnp.concatenate(parts + [jnp.zeros((8, 256), F32)], 0)
    turned = jnp.concatenate([one_z] * 4, 0).T
    group = lanes_of((256, 128)) >> 5
    for p in range(4):
        hx[p * 256 : p * 256 + 256, :] = jnp.where(group == p, turned, 0.0).astype(BF16)
    b1[...] = jnp.concatenate([bias1[...]] * 8, 1)
    b2[...] = jnp.dot(
        bias2[...], spread, preferred_element_type=F32, precision=lax.Precision.HIGHEST
    )


def prepare(conv_first, conv_second, bias_first, bias_second, head):
    none = None
    inner = [none, 1, 2, 3, 4, 5, 6, none]
    every = list(range(8))
    e1a = band(every, inner, False)
    e1o = band([0, 1, 6, 7], [-1, 0, 7, 8], False)
    e1r = band([-2, -1, 8, 9], [-1, 0, 7, 8], False)
    e2a = band(inner, every, True)
    e2b = band([-1, 0, 7, 8], every, True)
    vm = pl.BlockSpec(memory_space=VMEM)
    return pl.pallas_call(
        prepare_kernel,
        in_specs=[vm] * 10,
        out_specs=[vm] * 8,
        out_shape=[
            jax.ShapeDtypeStruct((2304, 256), BF16),
            jax.ShapeDtypeStruct((1536, 256), BF16),
            jax.ShapeDtypeStruct((1536, 256), BF16),
            jax.ShapeDtypeStruct((2560, 256), BF16),
            jax.ShapeDtypeStruct((1152, 256), BF16),
            jax.ShapeDtypeStruct((1024, 128), BF16),
            jax.ShapeDtypeStruct((1, 256), F32),
            jax.ShapeDtypeStruct((1, 256), F32),
        ],
        compiler_params=params(16),
        cost_estimate=cost(2 * 300 * 128 * 6144, 5 * MIB),
        name="prepare",
    )(conv_first, conv_second, bias_first[None], bias_second[None], head, e1a, e1o, e1r, e2a, e2b)


def on_device(
    features,
    weights,
    owners,
    tile_ids,
    counts,
    conv_first,
    bias_first,
    conv_second,
    bias_second,
    head,
):

    def swap(x, axis, partner, reach=1):
        size = lax.axis_size(axis)
        route = []
        for i in range(size):
            up = (i // reach) % 2 == (0 if partner == "a" else 1)
            route.append((i, (i + (reach if up else -reach)) % size))
        return lax.ppermute(x, axis, route)

    to_a, mid, to_b, slots = far_splat(features, weights, owners, tile_ids, counts)
    xb = swap(to_b, "gx", "b")
    xa = swap(to_a, "gx", "a")
    made = prepare(conv_first, conv_second, bias_first, bias_second, head)
    own = own_splat(features, weights, tile_ids)
    own, made, xa, xb = lax.optimization_barrier((own, made, xa, xb))
    t1a, t1o, t1r, t2a, t2b, headx, b1, b2 = made
    to_a, to_b = bundle(xa, xb, mid)
    from_ya = swap(to_a, "gy", "a")
    from_yb = swap(to_b, "gy", "b")
    own, to_a, to_b = lax.optimization_barrier((own, to_a, to_b))

    g, idx, near_a, near_b, fwd_a, fwd_b, keep_lo, keep_hi = column(own, xa, xb, mid)
    near_a = swap(near_a, "gy", "a")
    near_b = swap(near_b, "gy", "b")
    far_a = swap(fwd_a, "gy", "a", 2)
    far_b = swap(fwd_b, "gy", "b", 2)
    g, x, to_a, to_b, ids = sum_tiles(
        g, from_ya, from_yb, near_a, near_b, far_a, far_b, keep_lo, keep_hi
    )

    xb = swap(to_b, "gx", "b")
    xa = swap(to_a, "gx", "a")
    part, pre, w = inner_convs(x, g, t1a, t1o, b1, t2a, b2, weights)
    total, table, ans_ya, ans_yb, ans_x = edge_convs(xa, xb, part, pre, t1r, t2b, headx, ids, idx)

    back_ya = swap(ans_ya, "gy", "a")
    back_yb = swap(ans_yb, "gy", "b")
    grid_out = turn(total)
    grid_out, back_ya, back_yb = lax.optimization_barrier((grid_out, back_ya, back_yb))
    near = own_read(tile_ids, table, w)
    to_a = jnp.stack([back_ya[0], ans_x[0], back_yb[0]])
    to_b = jnp.stack([back_ya[2], ans_x[1], back_yb[2]])
    back_xb = swap(to_b, "gx", "b")
    back_xa = swap(to_a, "gx", "a")
    velocity = far_read(slots, counts, back_xa, back_xb, back_ya, back_yb, w, near)
    return grid_out, velocity


def solution(mesh):
    in_specs = (
        P(None, ("gx", "gy")),
        P(("gx", "gy"), None),
        P(("gx", "gy")),
        P(("gx", "gy")),
        P(("gx", "gy")),
        P(),
        P(),
        P(),
        P(),
        P(),
    )
    out_specs = (P(None, None, "gx", "gy"), P(None, ("gx", "gy")))
    return jax.shard_map(
        on_device, mesh=mesh, in_specs=in_specs, out_specs=out_specs, check_vma=False
    )
```

```python
import jax
import jax.numpy as jnp
import numpy as np
from jax import lax
from jax.experimental import pallas as pl
from jax.experimental.pallas import tpu as pltpu
from jax.sharding import PartitionSpec as P

C = 32
SLAB = 16
BY = 128
SLOTS = 16
PAY = SLOTS * 32 + 16
ROWS = 144
STEP = 32
STEPS = 4
MIB = 1 << 20
F32 = jnp.float32
BF16 = jnp.bfloat16
VMEM = pltpu.VMEM
SMEM = pltpu.SMEM


def lanes_of(shape):
    return lax.broadcasted_iota(jnp.int32, shape, len(shape) - 1)


def params(limit, grid=False):
    if grid:
        return pltpu.CompilerParams(
            dimension_semantics=("arbitrary",), vmem_limit_bytes=limit * MIB
        )
    return pltpu.CompilerParams(vmem_limit_bytes=limit * MIB)


def cost(flops, nbytes):
    return pl.CostEstimate(flops=flops, bytes_accessed=nbytes, transcendentals=0)


def upward(i):
    return jnp.where(i % 2 == 0, 2, 0)


def splat_four(f, w_ref, first):
    parts = []
    for j in (0, 2):
        at = (first + j) * 128
        fa = f[:, at : at + 128]
        fb = f[:, at + 128 : at + 256]
        none = jnp.zeros_like(fa)
        lhs = jnp.concatenate(
            [jnp.concatenate([fa, none], 1), jnp.concatenate([none, fb], 1)], 0
        )
        parts.append(jnp.dot(lhs, w_ref[at : at + 256, :], preferred_element_type=F32))
    a = jnp.concatenate(parts, 0).astype(BF16).T.astype(F32)
    a = a.reshape(4, 2, 2, 8, 128)
    lane = lanes_of((4, 2, 8, 128))
    v0, v1 = a[:, 0], a[:, 1]
    n0 = jnp.where(lane < 64, v0, pltpu.roll(v1, 64, 3))
    n1 = jnp.where(lane < 64, pltpu.roll(v0, 64, 3), v1)
    lane = lanes_of((4, 8, 128))
    tiles = []
    for n in (n0, n1):
        v0, v1 = n[:, 0], n[:, 1]
        tiles.append(jnp.where(lane % 64 < 32, v0, pltpu.roll(v1, 32, 2)))
        tiles.append(jnp.where(lane % 64 < 32, pltpu.roll(v0, 96, 2), v1))
    return tiles


def chunk_copies(f_hbm, w_hbm, fv, wv, sems, first):
    rows = STEP * 128
    pairs = []
    for c in range(STEPS):
        at = first * 128 + c * rows
        pairs.append(
            (
                pltpu.make_async_copy(
                    w_hbm.at[pl.ds(at, rows)], wv.at[pl.ds(c * rows, rows)], sems.at[c]
                ),
                pltpu.make_async_copy(f_hbm.at[:, pl.ds(at, rows)], fv.at[c], sems.at[STEPS + c]),
            )
        )
    return pairs


def far_splat_kernel(
    owners_h, ids_h, counts_h, f_hbm, w_hbm, out_a, mid, out_b, slots,
    fv, wv, tiles, idrows, filled, owners, ids, counts, sems, isems,
):
    ix = lax.axis_index("gx")
    iy = lax.axis_index("gy")
    copies = chunk_copies(f_hbm, w_hbm, fv, wv, sems, 128)
    small = [
        pltpu.make_async_copy(src, dst, isems.at[k])
        for k, (src, dst) in enumerate(((owners_h, owners), (ids_h, ids), (counts_h, counts)))
    ]
    for copy in small:
        copy.start()
    for pair in copies:
        for copy in pair:
            copy.start()
    tiles[...] = jnp.zeros_like(tiles)
    idrows[...] = jnp.zeros_like(idrows)
    for k in range(9):
        filled[k] = 0
    for copy in small:
        copy.wait()
    lane = lanes_of((1, 128))
    count = counts[0]
    for c, pair in enumerate(copies):
        for copy in pair:
            copy.wait()
        got = []
        for group in range(STEP // 4):
            got += splat_four(fv.at[c], wv.at[pl.ds(c * STEP * 128, STEP * 128)], group * 4)
        for j in range(STEP):
            block = c * STEP + j
            owner = owners[128 + block]
            live = 128 + block < count
            target = ((owner >> 3) - ix + 1) * 3 + (owner & 7) - iy + 1
            target = jnp.where(live, target, 4)
            rank = filled[target]
            filled[target] = jnp.where(live, rank + 1, 0)
            slot = target * SLOTS + rank
            slots[block] = slot
            tiles[slot] = got[j].reshape(32, 128).astype(BF16)
            row = idrows[pl.ds(target, 1), :]
            idrows[pl.ds(target, 1), :] = jnp.where(
                lane == rank, ids[128 + block].astype(F32), row
            )
    toward = upward(ix)
    for dx, out in ((toward, out_a), (1, mid), (2 - toward, out_b)):
        for dy in range(3):
            k = dx * 3 + dy
            at = dy * PAY
            out[at : at + SLOTS * 32, :] = tiles[pl.ds(k * SLOTS, SLOTS)].reshape(SLOTS * 32, 128)
            out[at + SLOTS * 32 : at + PAY, :] = jnp.broadcast_to(
                idrows[pl.ds(k, 1), :], (16, 128)
            ).astype(BF16)


def far_splat(features, weights, owners, ids, counts):
    pay = jax.ShapeDtypeStruct((3 * PAY, 128), BF16)
    vm = pl.BlockSpec(memory_space=VMEM)
    anywhere = pl.BlockSpec(memory_space=pl.ANY)
    return pl.pallas_call(
        far_splat_kernel,
        in_specs=[anywhere] * 5,
        out_specs=[vm, vm, vm, pl.BlockSpec(memory_space=SMEM)],
        out_shape=[pay, pay, pay, jax.ShapeDtypeStruct((128,), jnp.int32)],
        scratch_shapes=[
            VMEM((STEPS, C, STEP * 128), BF16),
            VMEM((STEPS * STEP * 128, 128), BF16),
            VMEM((9 * SLOTS, 32, 128), BF16),
            VMEM((16, 128), F32),
            SMEM((9,), jnp.int32),
            SMEM((256,), jnp.int32),
            SMEM((256,), jnp.int32),
            SMEM((1,), jnp.int32),
            pltpu.SemaphoreType.DMA((2 * STEPS,)),
            pltpu.SemaphoreType.DMA((3,)),
        ],
        compiler_params=params(56),
        cost_estimate=cost(2 * 128 * 32 * 128 * 128, 6 * MIB),
        name="far_splat",
    )(owners, ids, counts, features, weights)


def tile_place(tile):
    return (tile >> 5) * 4, (tile >> 4) & 1, pl.multiple_of((tile & 15) * 8, 8)


def own_splat_kernel(ids, f_hbm, w_hbm, out, fv, wv, grid, sems):
    copies = chunk_copies(f_hbm, w_hbm, fv, wv, sems, 0)
    for pair in copies:
        for copy in pair:
            copy.start()
    for c, pair in enumerate(copies):
        for copy in pair:
            copy.wait()
        got = []
        for group in range(STEP // 4):
            got += splat_four(fv.at[c], wv.at[pl.ds(c * STEP * 128, STEP * 128)], group * 4)
        for j in range(STEP):
            z, tx, y = tile_place(ids[c * STEP + j])
            grid[tx, pl.ds(z, 4), pl.ds(y, 8), :] = got[j]
    out[...] = grid[...].astype(BF16)


def own_splat(features, weights, ids):
    anywhere = pl.BlockSpec(memory_space=pl.ANY)
    return pl.pallas_call(
        own_splat_kernel,
        in_specs=[pl.BlockSpec(memory_space=SMEM), anywhere, anywhere],
        out_specs=pl.BlockSpec(memory_space=VMEM),
        out_shape=jax.ShapeDtypeStruct((2, SLAB, BY, 128), BF16),
        scratch_shapes=[
            VMEM((STEPS, C, STEP * 128), BF16),
            VMEM((STEPS * STEP * 128, 128), BF16),
            VMEM((2, SLAB, BY, 128), F32),
            pltpu.SemaphoreType.DMA((2 * STEPS,)),
        ],
        compiler_params=params(56),
        cost_estimate=cost(2 * 128 * 32 * 128 * 128, 6 * MIB),
        name="own_splat",
    )(ids, features, weights)


def bundle_kernel(xa, xb, mid, to_a, to_b):
    toward = upward(lax.axis_index("gy"))
    for out, dy in ((to_a, toward), (to_b, 2 - toward)):
        at = pl.multiple_of(dy * PAY, 16)
        for k, ref in enumerate((xa, mid, xb)):
            out[k * PAY : (k + 1) * PAY, :] = ref[pl.ds(at, PAY), :]


def bundle(xa, xb, mid):
    vm = pl.BlockSpec(memory_space=VMEM)
    shape = jax.ShapeDtypeStruct((3 * PAY, 128), BF16)
    return pl.pallas_call(
        bundle_kernel,
        in_specs=[vm] * 3,
        out_specs=[vm, vm],
        out_shape=[shape, shape],
        compiler_params=params(8),
        cost_estimate=cost(1000, 2 * MIB),
        name="bundle",
    )(xa, xb, mid)


def ids_of(groups):
    rows = [ref[pl.ds(at + SLOTS * 32, 16), :].astype(F32)[0:1] for ref, at in groups]
    return jnp.concatenate(rows, 0).astype(jnp.int32)


def tile_of(ref, at, j):
    rows = ref[pl.ds(pl.multiple_of(at + j * 32, 16), 32), :]
    return rows.astype(F32).reshape(4, 8, 128)


def put_tile(grid, tile, new):
    z, tx, y = tile_place(tile)
    grid[tx, pl.ds(z, 4), pl.ds(y, 8), :] += new


def column_kernel(
    own, xa, xb, mid,
    g, ids, near_a, near_b, fwd_a, fwd_b, keep_lo, keep_hi, acc_a, acc_b, idv, sem,
):
    iy = lax.axis_index("gy")
    even = iy % 2 == 0
    first = pl.multiple_of(upward(iy) * PAY, 16)
    second = pl.multiple_of((2 - upward(iy)) * PAY, 16)
    groups = [(xa, PAY), (xb, PAY)]
    groups += [(xa, first), (mid, first), (xb, first), (xa, second), (mid, second), (xb, second)]
    idv[...] = ids_of(groups)
    copy = pltpu.make_async_copy(idv, ids, sem)
    copy.start()
    g[...] = own[...].astype(F32)
    acc_a[...] = jnp.zeros_like(acc_a)
    acc_b[...] = jnp.zeros_like(acc_b)
    copy.wait()
    for k in range(3):

        def add(j, carry, k=k):
            if k < 2:
                put_tile(g, ids[k, j], tile_of(groups[k][0], groups[k][1], j))
            for n, acc in ((2 + k, acc_a), (5 + k, acc_b)):
                tile = ids[n, j]
                ty = tile & 15
                place = jnp.where(ty == 0, 0, jnp.where(ty == 15, 1, 2))
                new = tile_of(groups[n][0], groups[n][1], j)
                acc[place, (tile >> 4) & 1, pl.ds((tile >> 5) * 4, 4)] += new
            return carry

        lax.fori_loop(0, SLOTS, add, 0, unroll=8)
    for tx in range(2):
        for r in range(2):
            k = tx * 2 + r
            low, high = g[tx, :, r, :], g[tx, :, BY - 2 + r, :]
            near_a[k] = jnp.where(even, high, low).astype(BF16)
            near_b[k] = jnp.where(even, low, high).astype(BF16)
            keep_hi[k] = jnp.where(even, acc_a[0, tx, :, r, :], acc_b[0, tx, :, r, :])
            keep_lo[k] = jnp.where(even, acc_b[1, tx, :, 6 + r, :], acc_a[1, tx, :, 6 + r, :])
            high = jnp.where(even, acc_a[1, tx, :, 6 + r, :], acc_b[1, tx, :, 6 + r, :])
            low = jnp.where(even, acc_b[0, tx, :, r, :], acc_a[0, tx, :, r, :])
            up = (iy >> 1) % 2 == 0
            fwd_a[k] = jnp.where(up, high, low).astype(BF16)
            fwd_b[k] = jnp.where(up, low, high).astype(BF16)


def column(own, xa, xb, mid):
    vm = pl.BlockSpec(memory_space=VMEM)
    return pl.pallas_call(
        column_kernel,
        in_specs=[vm] * 4,
        out_specs=[vm, pl.BlockSpec(memory_space=SMEM)] + [vm] * 6,
        out_shape=[
            jax.ShapeDtypeStruct((2, SLAB, BY, 128), F32),
            jax.ShapeDtypeStruct((8, 128), jnp.int32),
        ]
        + [jax.ShapeDtypeStruct((4, SLAB, 128), BF16)] * 4
        + [jax.ShapeDtypeStruct((4, SLAB, 128), F32)] * 2,
        scratch_shapes=[
            VMEM((3, 2, SLAB, 8, 128), F32),
            VMEM((3, 2, SLAB, 8, 128), F32),
            VMEM((8, 128), jnp.int32),
            pltpu.SemaphoreType.DMA,
        ],
        compiler_params=params(16),
        cost_estimate=cost(1000, 4 * MIB),
        name="column",
    )(own, xa, xb, mid)


def sum_kernel(
    part, ya, yb, next_a, next_b, far_a, far_b, keep_lo, keep_hi,
    g, x, to_a, to_b, ids, grid, more, edge, idv, sem,
):
    even_x = lax.axis_index("gx") % 2 == 0
    iy = lax.axis_index("gy")
    even = iy % 2 == 0
    up = (iy >> 1) % 2 == 0
    groups = [(ref, k * PAY) for ref in (ya, yb) for k in range(3)]
    idv[0:6, :] = ids_of(groups)
    idv[6:8, :] = jnp.zeros((2, 128), jnp.int32)
    copy = pltpu.make_async_copy(idv, ids, sem)
    copy.start()
    grid[...] = part[...]
    more[...] = jnp.zeros_like(more)
    edge[...] = jnp.zeros_like(edge)
    for tx in range(2):
        for r in range(2):
            k = tx * 2 + r
            near_a, near_b = next_a[k].astype(F32), next_b[k].astype(F32)
            away_a, away_b = far_a[k].astype(F32), far_b[k].astype(F32)
            low = jnp.where(iy >= 2, jnp.where(up, away_b, away_a), 0.0)
            low = low + jnp.where(even, near_b, near_a) + keep_lo[k]
            high = jnp.where(iy < 6, jnp.where(up, away_a, away_b), 0.0)
            high = high + jnp.where(even, near_a, near_b) + keep_hi[k]
            edge[tx, 0, :, 6 + r, :] = jnp.where(iy > 0, low, 0.0)
            edge[tx, 1, :, r, :] = jnp.where(iy < 7, high, 0.0)
    copy.wait()
    for k in range(3):

        def add(j, carry, k=k):
            put_tile(grid, ids[k, j], tile_of(ya, k * PAY, j))
            put_tile(more, ids[3 + k, j], tile_of(yb, k * PAY, j))
            return carry

        lax.fori_loop(0, SLOTS, add, 0, unroll=8)
    lane = lanes_of((ROWS, 128))

    def plane(tx, z):
        return jnp.concatenate([edge[tx, 0, z], grid[tx, z] + more[tx, z], edge[tx, 1, z]], 0)

    def pair(z, carry):
        sides = []
        for tx in range(2):
            a, b = plane(tx, z), plane(tx, z + 8)
            x[tx, z] = a.astype(BF16)
            x[tx, z + 8] = b.astype(BF16)
            g[tx, z] = a[8 : 8 + BY].astype(BF16)
            g[tx, z + 8] = b[8 : 8 + BY].astype(BF16)
            if tx == 0:
                sides.append(jnp.where(lane < 64, a, pltpu.roll(b, 64, 1)))
            else:
                sides.append(jnp.where(lane < 64, pltpu.roll(a, 64, 1), b))
        to_a[z] = jnp.where(even_x, sides[1], sides[0]).astype(BF16)
        to_b[z] = jnp.where(even_x, sides[0], sides[1]).astype(BF16)
        return carry

    lax.fori_loop(0, 8, pair, 0, unroll=2)


def sum_tiles(part, ya, yb, near_a, near_b, far_a, far_b, keep_lo, keep_hi):
    vm = pl.BlockSpec(memory_space=VMEM)
    side = jax.ShapeDtypeStruct((SLAB // 2, ROWS, 128), BF16)
    return pl.pallas_call(
        sum_kernel,
        in_specs=[vm] * 9,
        out_specs=[vm] * 4 + [pl.BlockSpec(memory_space=SMEM)],
        out_shape=[
            jax.ShapeDtypeStruct((2, SLAB, BY, 128), BF16),
            jax.ShapeDtypeStruct((2, SLAB, ROWS, 128), BF16),
            side,
            side,
            jax.ShapeDtypeStruct((8, 128), jnp.int32),
        ],
        scratch_shapes=[
            VMEM((2, SLAB, BY, 128), F32),
            VMEM((2, SLAB, BY, 128), F32),
            VMEM((2, 2, SLAB, 8, 128), F32),
            VMEM((8, 128), jnp.int32),
            pltpu.SemaphoreType.DMA,
        ],
        compiler_params=params(16),
        cost_estimate=cost(1000, 4 * MIB),
        name="sum_tiles",
    )(part, ya, yb, near_a, near_b, far_a, far_b, keep_lo, keep_hi)


def rows_inside(shape, iy):
    row = lax.broadcasted_iota(jnp.int32, shape, 1)
    return ((row != 7) | (iy > 0)) & ((row != 136) | (iy < 7))


def shifted(v):
    return (pltpu.roll(v, 1, 1), v, pltpu.roll(v, ROWS - 1, 1))


PAIRS = SLAB // 2


def window(ref, n, k):
    m = n * 4 + k // 2
    out = []
    for dy in range(3):
        v = ref[dy, m : m + 4, k % 2]
        out.append(v.reshape(4 * v.shape[1], v.shape[2]))
    return out


def inner_kernel(x, g, t1, t1o, b1, t2, b2, part, pre, xs, xe, hs):
    iy = lax.axis_index("gy")
    lane = lanes_of((1, ROWS, 128))
    for dy in range(3):
        xs[dy, 0, 0] = jnp.zeros((ROWS, 256), BF16)
        xs[dy, PAIRS, 1] = jnp.zeros((ROWS, 256), BF16)
        xe[dy, 0, 0] = jnp.zeros((ROWS, 128), BF16)
        xe[dy, PAIRS, 1] = jnp.zeros((ROWS, 128), BF16)
        hs[dy, 0, 0] = jnp.zeros((BY, 256), BF16)
        hs[dy, PAIRS, 1] = jnp.zeros((BY, 256), BF16)

    def shift(n, carry):
        for k in range(2):
            both = [shifted(x[tx, pl.ds(2 * n + k, 1)].astype(F32)) for tx in range(2)]
            for dy in range(3):
                s0, s1 = both[0][dy], both[1][dy]
                xs[dy, pl.ds(n + k, 1), 1 - k, :, 0:128] = s0.astype(BF16)
                xs[dy, pl.ds(n + k, 1), 1 - k, :, 128:256] = s1.astype(BF16)
                xe[dy, pl.ds(n + k, 1), 1 - k] = jnp.where(lane < 64, s0, s1).astype(BF16)
        return carry

    lax.fori_loop(0, PAIRS, shift, 0)
    for n in range(2):
        for zo in range(2):
            taps = window(xs, n, zo) + window(xs, n, zo + 1) + window(xs, n, zo + 2)
            acc = jnp.dot(jnp.concatenate(taps, 1), t1[...], preferred_element_type=F32) + b1[...]
            h = jax.nn.gelu(acc).reshape(4, ROWS, 256)
            h = jnp.where(rows_inside(h.shape, iy), h, 0.0)
            for dy, s in enumerate(shifted(h)):
                m = n * 4 + zo
                hs[dy, m : m + 4, 1 - zo] = s[:, 8 : 8 + BY].astype(BF16)
    for n in range(2):
        taps = sum([window(xe, n, zi) for zi in range(4)], [])
        acc = jnp.dot(jnp.concatenate(taps, 1), t1o[...], preferred_element_type=F32) + b1[...]
        pre[n] = acc
    for n in range(2):
        for zo in range(2):
            taps = window(hs, n, zo) + window(hs, n, zo + 1) + window(hs, n, zo + 2)
            taps += [g[tx, n * 4 : n * 4 + 4, zo].reshape(4 * BY, 128) for tx in range(2)]
            acc = jnp.dot(jnp.concatenate(taps, 1), t2[...], preferred_element_type=F32) + b2[...]
            part[n * 4 : n * 4 + 4, zo] = acc.reshape(4, BY, 256)


def inner_convs(x, g, t1, t1o, b1, t2, b2):
    vm = pl.BlockSpec(memory_space=VMEM)
    return pl.pallas_call(
        inner_kernel,
        in_specs=[vm] * 7,
        out_specs=[vm, vm],
        out_shape=[
            jax.ShapeDtypeStruct((PAIRS, 2, BY, 256), F32),
            jax.ShapeDtypeStruct((2, 4 * ROWS, 256), F32),
        ],
        scratch_shapes=[
            VMEM((3, PAIRS + 1, 2, ROWS, 256), BF16),
            VMEM((3, PAIRS + 1, 2, ROWS, 128), BF16),
            VMEM((3, PAIRS + 1, 2, BY, 256), BF16),
        ],
        compiler_params=params(32),
        cost_estimate=cost(2 * 20 * 256 * 256 * 2304, 6 * MIB),
        name="inner_convs",
    )(x, g.reshape(2, PAIRS, 2, BY, 128), t1, t1o, b1, t2, b2)


def tile_row(tile):
    return ((tile >> 5) * 4 + ((tile >> 2) & 3)) * 8 + ((tile >> 4) & 1) * 4 + (tile & 3)


def edge_kernel(
    ra, rb, part, pre, t1, t2, headx, ids, idx, total, table, ans_ya, ans_yb, ans_x, es, hs, vel
):
    ix = lax.axis_index("gx")
    iy = lax.axis_index("gy")
    for dy in range(3):
        es[dy, 0, 0] = jnp.zeros((ROWS, 128), BF16)
        es[dy, PAIRS, 1] = jnp.zeros((ROWS, 128), BF16)
        hs[dy, 0, 0] = jnp.zeros((BY, 128), BF16)
        hs[dy, PAIRS, 1] = jnp.zeros((BY, 128), BF16)
    lane = lanes_of((1, ROWS, 128))
    for z in range(8):
        va, vb = ra[z : z + 1].astype(F32), rb[z : z + 1].astype(F32)
        a = jnp.where(ix > 0, jnp.where(ix % 2 == 0, vb, va), 0.0)
        b = jnp.where(ix < 15, jnp.where(ix % 2 == 0, va, vb), 0.0)
        near = jnp.where(lane < 64, a, pltpu.roll(b, 64, 2))
        far = jnp.where(lane < 64, pltpu.roll(a, 64, 2), b)
        for zz, v in ((z, near), (z + 8, far)):
            m = (zz + 1) // 2
            for dy, s in enumerate(shifted(v)):
                es[dy, m : m + 1, (zz + 1) % 2] = s.astype(BF16)
    for n in range(2):
        taps = sum([window(es, n, zi) for zi in range(4)], [])
        acc = jnp.dot(jnp.concatenate(taps, 1), t1[...], preferred_element_type=F32) + pre[n]
        h = jax.nn.gelu(acc).reshape(4, ROWS, 256)
        ln = lanes_of(h.shape) & 127
        keep = ((ln >= 32) | (ix > 0)) & ((ln < 96) | (ix < 15))
        h = jnp.where(rows_inside(h.shape, iy) & keep, h, 0.0)
        for dy, s in enumerate(shifted(h)):
            s = s[:, 8 : 8 + BY].astype(BF16)
            hs[dy, n * 4 : n * 4 + 4, 1] = s[:, :, 0:128]
            hs[dy, n * 4 + 1 : n * 4 + 5, 0] = s[:, :, 128:256]
    rows = []
    for n in range(2):
        for zo in range(2):
            taps = window(hs, n, zo) + window(hs, n, zo + 1) + window(hs, n, zo + 2)
            acc = jnp.dot(jnp.concatenate(taps, 1), t2[...], preferred_element_type=F32)
            acc = acc.reshape(4, BY, 256) + part[n * 4 : n * 4 + 4, zo]
            acc = acc.astype(BF16)
            total[n * 4 : n * 4 + 4, zo] = acc
            rows.append(jnp.concatenate([acc[p] for p in range(4)], 1))
    v = jnp.dot(jnp.concatenate(rows, 0), headx[...], preferred_element_type=F32).T
    for n in range(2):
        for zo in range(2):
            q = (n * 2 + zo) * BY
            for p in range(4):
                for a in range(3):
                    at = p * 32 + a * 8
                    vel[a, 2 * (n * 4 + p) + zo] = v[at : at + 8, q : q + BY]

    table[...] = jnp.zeros_like(table)
    sub = lax.broadcasted_iota(jnp.int32, (4, 8, 128), 1)
    ln = lanes_of((4, 8, 128))
    for a in range(3):
        v = vel[a].reshape(4, 2, 2, 8, 128)
        v0, v1 = v[:, 0], v[:, 1]
        l2 = lanes_of(v0.shape)
        m0 = jnp.where(l2 < 64, v0, pltpu.roll(v1, 64, 3))
        m1 = jnp.where(l2 < 64, pltpu.roll(v0, 64, 3), v1)
        for k, m in enumerate((m0, m1)):
            v0, v1 = m[:, 0], m[:, 1]
            n0 = jnp.where(ln % 64 < 32, v0, pltpu.roll(v1, 32, 2))
            n1 = jnp.where(ln % 64 < 32, pltpu.roll(v0, 96, 2), v1)
            for kk, w in enumerate((n0, n1)):
                for bit, step in ((2, 16), (1, 8)):
                    up = pltpu.roll(pltpu.roll(w, 8 - bit, 1), step, 2)
                    down = pltpu.roll(pltpu.roll(w, bit, 1), 128 - step, 2)
                    s1 = (sub & bit) != 0
                    l1 = (ln & step) != 0
                    w = jnp.where(s1 == l1, w, jnp.where(l1, up, down))
                for tz in range(4):
                    row = (tz * 4 + k * 2 + kk) * 8
                    table[row : row + 8, a, :] = w[tz]

    places = [(ans_ya, 0), (ans_ya, 1), (ans_ya, 2), (ans_yb, 0), (ans_yb, 1), (ans_yb, 2)]
    places += [(ans_x, 0), (ans_x, 1)]
    for n, (ref, k) in enumerate(places):
        source, row = (ids, n) if n < 6 else (idx, n - 6)

        def answer(j, carry, source=source, row=row, ref=ref, k=k):
            halves = []
            for h in range(2):
                r0 = table[tile_row(source[row, j * 4 + 2 * h])]
                r1 = table[tile_row(source[row, j * 4 + 2 * h + 1])]
                halves.append(two_blocks(r0, r1))
            ref[k, pl.ds(pl.multiple_of(j * 16, 16), 16), :] = jnp.concatenate(halves, 0).astype(
                BF16
            )
            return carry

        lax.fori_loop(0, SLOTS // 4, answer, 0, unroll=4)


def edge_convs(ra, rb, part, pre, t1, t2, headx, ids, idx):
    vm = pl.BlockSpec(memory_space=VMEM)
    ans = jax.ShapeDtypeStruct((3, 64, 128), BF16)
    return pl.pallas_call(
        edge_kernel,
        in_specs=[vm] * 7 + [pl.BlockSpec(memory_space=SMEM)] * 2,
        out_specs=[vm] * 5,
        out_shape=[
            jax.ShapeDtypeStruct((SLAB // 2, 2, BY, 256), BF16),
            jax.ShapeDtypeStruct((128, 8, 128), F32),
            ans,
            ans,
            jax.ShapeDtypeStruct((2, 64, 128), BF16),
        ],
        scratch_shapes=[
            VMEM((3, PAIRS + 1, 2, ROWS, 128), BF16),
            VMEM((3, PAIRS + 1, 2, BY, 128), BF16),
            VMEM((3, SLAB, 8, 128), F32),
        ],
        compiler_params=params(32),
        cost_estimate=cost(2 * 9 * 256 * 256 * 2304, 6 * MIB),
        name="edge_convs",
    )(ra, rb, part, pre, t1, t2, headx, ids, idx)


def turn_kernel(total, out):
    for k in range(4):
        out[:, k] = total[k // 2, k % 2].T.reshape(32, 8, 128)


def turn(total):
    return pl.pallas_call(
        turn_kernel,
        grid=(4,),
        in_specs=[pl.BlockSpec((2, 2, BY, 256), lambda i: (i, 0, 0, 0))],
        out_specs=pl.BlockSpec((C, 4, 8, BY), lambda i: (0, i, 0, 0)),
        out_shape=jax.ShapeDtypeStruct((C, SLAB, 8, BY), BF16),
        compiler_params=params(8, True),
        cost_estimate=cost(1000, 8 * MIB),
        name="turn",
    )(total)


BATCH = 32


def read_batch(rows, w_ref, first, out, at, count):
    cells = rows.astype(BF16).T
    owner = lanes_of((128, 128)) >> 2
    right = jnp.concatenate(
        [jnp.where(owner == b, cells, jnp.zeros_like(cells)) for b in range(BATCH)], 0
    )
    left = jnp.concatenate(
        [w_ref[(first + b) * 128 : (first + b + 1) * 128, :] for b in range(BATCH)], 1
    )
    r = jnp.dot(left, right, preferred_element_type=F32).T
    for b in range(BATCH):
        v = r[4 * b : 4 * b + 3]
        if count is not None:
            v = jnp.where(128 + first + b < count, v, 0.0)
        out[:, at + b * 128 : at + (b + 1) * 128] = v


def two_blocks(r0, r1):
    row = lax.broadcasted_iota(jnp.int32, (8, 128), 0)
    return jnp.where(row < 4, r0, pltpu.roll(r1, 4, 0))


def weight_copies(w_hbm, wv, sems, first):
    n = 128 // BATCH
    rows = BATCH * 128
    return [
        pltpu.make_async_copy(
            w_hbm.at[pl.ds(first * 128 + k * rows, rows)], wv.at[pl.ds(k * rows, rows)], sems.at[k]
        )
        for k in range(n)
    ]


def own_read_kernel(ids, table, w_hbm, out, far_w, wv, sems, fsems):
    copies = weight_copies(w_hbm, wv, sems, 0)
    later = weight_copies(w_hbm, far_w, fsems, 128)
    for copy in copies + later:
        copy.start()
    for k, copy in enumerate(copies):
        rows = [
            two_blocks(
                table[tile_row(ids[k * BATCH + 2 * j])], table[tile_row(ids[k * BATCH + 2 * j + 1])]
            )
            for j in range(BATCH // 2)
        ]
        copy.wait()
        read_batch(jnp.concatenate(rows, 0), wv, k * BATCH, out, k * BATCH * 128, None)
    for copy in later:
        copy.wait()


def own_read(ids, table, weights, particles):
    vm = pl.BlockSpec(memory_space=VMEM)
    return pl.pallas_call(
        own_read_kernel,
        in_specs=[pl.BlockSpec(memory_space=SMEM), vm, pl.BlockSpec(memory_space=pl.ANY)],
        out_specs=[vm, vm],
        out_shape=[
            jax.ShapeDtypeStruct((3, particles // 2), F32),
            jax.ShapeDtypeStruct((particles // 2, 128), BF16),
        ],
        scratch_shapes=[
            VMEM((particles // 2, 128), BF16),
            pltpu.SemaphoreType.DMA((128 // BATCH,)),
            pltpu.SemaphoreType.DMA((128 // BATCH,)),
        ],
        compiler_params=params(48),
        cost_estimate=cost(2 * 128 * 32 * 128 * 128, 9 * MIB),
        name="own_read",
    )(ids, table, weights)


def far_read_kernel(slots, counts, xa, xb, ya, yb, w, near, out, table, made, sems):
    dx = upward(lax.axis_index("gx"))
    dy = upward(lax.axis_index("gy"))
    places = [(ya, 1, 3 + dy), (yb, 1, 5 - dy)]
    for ref, d in ((xa, dx), (xb, 2 - dx)):
        places += [(ref, 0, d * 3 + dy), (ref, 1, d * 3 + 1), (ref, 2, d * 3 + 2 - dy)]
    table[4 * SLOTS : 5 * SLOTS] = jnp.zeros((SLOTS, 8, 128), F32)
    for ref, k, place in places:
        v = ref[k].astype(F32).reshape(8, 8, 128)
        turned = pltpu.roll(v, 4, 1)
        for j in range(8):
            table[place * SLOTS + 2 * j] = v[j]
            table[place * SLOTS + 2 * j + 1] = turned[j]
    half = near.shape[1]
    size = BATCH * 128
    copies = [pltpu.make_async_copy(near, out.at[:, pl.ds(0, half)], sems.at[128 // BATCH])]
    copies[0].start()
    for k in range(128 // BATCH):
        rows = [
            two_blocks(table[slots[k * BATCH + 2 * j]], table[slots[k * BATCH + 2 * j + 1]])
            for j in range(BATCH // 2)
        ]
        read_batch(jnp.concatenate(rows, 0), w, k * BATCH, made.at[k], 0, counts[0])
        copies.append(
            pltpu.make_async_copy(
                made.at[k], out.at[:, pl.ds(half + k * size, size)], sems.at[k]
            )
        )
        copies[-1].start()
    for copy in copies:
        copy.wait()


def far_read(slots, counts, xa, xb, ya, yb, w, near):
    vm = pl.BlockSpec(memory_space=VMEM)
    smem = pl.BlockSpec(memory_space=SMEM)
    return pl.pallas_call(
        far_read_kernel,
        in_specs=[smem, smem] + [vm] * 6,
        out_specs=pl.BlockSpec(memory_space=pl.ANY),
        out_shape=jax.ShapeDtypeStruct((3, 2 * near.shape[1]), F32),
        scratch_shapes=[
            VMEM((9 * SLOTS, 8, 128), F32),
            VMEM((128 // BATCH, 3, BATCH * 128), F32),
            pltpu.SemaphoreType.DMA((128 // BATCH + 1,)),
        ],
        compiler_params=params(24),
        cost_estimate=cost(2 * 128 * 32 * 128 * 128, 5 * MIB),
        name="far_read",
    )(slots, counts, xa, xb, ya, yb, w, near)


def band(pin, pout, out_last):
    out = np.zeros((4, C, len(pin), len(pout), C), np.float32)
    for i, p in enumerate(pin):
        for j, q in enumerate(pout):
            if p is not None and q is not None and abs(p - q) <= 1:
                out[p - q + 1, np.arange(C), i, j, np.arange(C)] = 1
    if out_last:
        out = out.swapaxes(3, 4)
    return jnp.asarray(out.reshape(4 * C, -1), BF16)


def prepare_kernel(
    c1, c2, bias1, bias2, head, e1a, e1o, e1r, e2a, e2b, t1a, t1o, t1r, t2a, t2b, hx, b1, b2
):
    one = (
        lax.broadcasted_iota(jnp.int32, (C, C), 0) == lax.broadcasted_iota(jnp.int32, (C, C), 1)
    ).astype(BF16)
    nothing = jnp.zeros((C, C), BF16)
    for t in (t1o, t1r):
        third = t.shape[0] // 4
        t[0:third, 128:256] = jnp.zeros((third, 128), BF16)
        t[3 * third : 4 * third, 0:128] = jnp.zeros((third, 128), BF16)
    plans = (
        (c1, ((e1a, t1a, 256), (e1o, t1o, 128), (e1r, t1r, 128))),
        (c2, ((e2a, t2a, 256), (e2b, t2b, 256))),
    )
    for conv, made in plans:
        pieces = []
        for k in range(9):
            pieces += [conv[k // 3 * 9 + d * 3 + k % 3] for d in range(3)] + [nothing]
        turned = lax.dot_general(
            one, jnp.concatenate(pieces, 0), (((1,), (1,)), ((), ())), preferred_element_type=F32
        ).astype(BF16)
        lhs = jnp.concatenate([turned[:, 128 * k : 128 * k + 128] for k in range(9)], 0)
        for e, t, width in made:
            planes = e.shape[1] // width
            for p in range(planes):
                r = jnp.dot(lhs, e[:, p * width : (p + 1) * width], preferred_element_type=F32)
                r = r.astype(BF16)
                for k in range(9):
                    block = r[C * k : C * k + C]
                    at = (k * planes + p) * C
                    if width == 256:
                        t[at : at + C, :] = block
                        continue
                    for zo in range(2):
                        down = at + zo * 3 * planes * C
                        t[down : down + C, zo * 128 : zo * 128 + 128] = block
    row = lax.broadcasted_iota(jnp.int32, (256, 256), 0)
    col = lanes_of((256, 256))
    t2a[2304:2560, :] = ((row & 31) == (col >> 3)).astype(F32).astype(BF16) * (
        (row >> 5) == (col & 7)
    ).astype(F32).astype(BF16)
    spread = (
        lax.broadcasted_iota(jnp.int32, (C, 256), 0) == (lanes_of((C, 256)) >> 3)
    ).astype(F32)
    wide = jnp.dot(head[...], spread.astype(BF16), preferred_element_type=F32)
    keep = (lanes_of((8, 256)) & 7) == lax.broadcasted_iota(jnp.int32, (8, 256), 0)
    parts = [jnp.where(keep, jnp.broadcast_to(wide[a : a + 1], (8, 256)), 0.0) for a in range(3)]
    one_z = jnp.concatenate(parts + [jnp.zeros((8, 256), F32)], 0)
    turned = jnp.concatenate([one_z] * 4, 0).T
    group = lanes_of((256, 128)) >> 5
    for p in range(4):
        hx[p * 256 : p * 256 + 256, :] = jnp.where(group == p, turned, 0.0).astype(BF16)
    b1[...] = jnp.concatenate([bias1[...]] * 8, 1)
    b2[...] = jnp.dot(
        bias2[...], spread, preferred_element_type=F32, precision=lax.Precision.HIGHEST
    )


def prepare(conv_first, conv_second, bias_first, bias_second, head):
    none = None
    inner = [none, 1, 2, 3, 4, 5, 6, none]
    every = list(range(8))
    e1a = band(every, inner, False)
    e1o = band([0, 1, 6, 7], [-1, 0, 7, 8], False)
    e1r = band([-2, -1, 8, 9], [-1, 0, 7, 8], False)
    e2a = band(inner, every, True)
    e2b = band([-1, 0, 7, 8], every, True)
    vm = pl.BlockSpec(memory_space=VMEM)
    return pl.pallas_call(
        prepare_kernel,
        in_specs=[vm] * 10,
        out_specs=[vm] * 8,
        out_shape=[
            jax.ShapeDtypeStruct((2304, 256), BF16),
            jax.ShapeDtypeStruct((1536, 256), BF16),
            jax.ShapeDtypeStruct((1536, 256), BF16),
            jax.ShapeDtypeStruct((2560, 256), BF16),
            jax.ShapeDtypeStruct((1152, 256), BF16),
            jax.ShapeDtypeStruct((1024, 128), BF16),
            jax.ShapeDtypeStruct((1, 256), F32),
            jax.ShapeDtypeStruct((1, 256), F32),
        ],
        compiler_params=params(16),
        cost_estimate=cost(2 * 300 * 128 * 6144, 5 * MIB),
        name="prepare",
    )(conv_first, conv_second, bias_first[None], bias_second[None], head, e1a, e1o, e1r, e2a, e2b)


def on_device(
    features,
    weights,
    owners,
    tile_ids,
    counts,
    conv_first,
    bias_first,
    conv_second,
    bias_second,
    head,
):
    particles = features.shape[1]

    def swap(x, axis, partner, reach=1):
        size = lax.axis_size(axis)
        route = []
        for i in range(size):
            up = (i // reach) % 2 == (0 if partner == "a" else 1)
            route.append((i, (i + (reach if up else -reach)) % size))
        return lax.ppermute(x, axis, route)

    to_a, mid, to_b, slots = far_splat(features, weights, owners, tile_ids, counts)
    xb = swap(to_b, "gx", "b")
    xa = swap(to_a, "gx", "a")
    made = prepare(conv_first, conv_second, bias_first, bias_second, head)
    own = own_splat(features, weights, tile_ids)
    own, made, xa, xb = lax.optimization_barrier((own, made, xa, xb))
    t1a, t1o, t1r, t2a, t2b, headx, b1, b2 = made
    to_a, to_b = bundle(xa, xb, mid)
    from_ya = swap(to_a, "gy", "a")
    from_yb = swap(to_b, "gy", "b")
    own, to_a, to_b = lax.optimization_barrier((own, to_a, to_b))

    g, idx, near_a, near_b, fwd_a, fwd_b, keep_lo, keep_hi = column(own, xa, xb, mid)
    near_a = swap(near_a, "gy", "a")
    near_b = swap(near_b, "gy", "b")
    far_a = swap(fwd_a, "gy", "a", 2)
    far_b = swap(fwd_b, "gy", "b", 2)
    g, x, to_a, to_b, ids = sum_tiles(
        g, from_ya, from_yb, near_a, near_b, far_a, far_b, keep_lo, keep_hi
    )

    xb = swap(to_b, "gx", "b")
    xa = swap(to_a, "gx", "a")
    part, pre = inner_convs(x, g, t1a, t1o, b1, t2a, b2)
    total, table, ans_ya, ans_yb, ans_x = edge_convs(xa, xb, part, pre, t1r, t2b, headx, ids, idx)

    back_ya = swap(ans_ya, "gy", "a")
    back_yb = swap(ans_yb, "gy", "b")
    grid_out = turn(total)
    grid_out, back_ya, back_yb = lax.optimization_barrier((grid_out, back_ya, back_yb))
    near, far_w = own_read(tile_ids, table, weights, particles)
    to_a = jnp.stack([back_ya[0], ans_x[0], back_yb[0]])
    to_b = jnp.stack([back_ya[2], ans_x[1], back_yb[2]])
    back_xb = swap(to_b, "gx", "b")
    back_xa = swap(to_a, "gx", "a")
    velocity = far_read(slots, counts, back_xa, back_xb, back_ya, back_yb, far_w, near)
    return grid_out, velocity


def solution(mesh):
    in_specs = (
        P(None, ("gx", "gy")),
        P(("gx", "gy"), None),
        P(("gx", "gy")),
        P(("gx", "gy")),
        P(("gx", "gy")),
        P(),
        P(),
        P(),
        P(),
        P(),
    )
    out_specs = (P(None, None, "gx", "gy"), P(None, ("gx", "gy")))
    return jax.shard_map(
        on_device, mesh=mesh, in_specs=in_specs, out_specs=out_specs, check_vma=False
    )
```
